128 devices in a mesh: fsdp: 2 (over y_lo), ctx: 16 (over y_hi, x, core), tp: 4 (over z).
Axes of the slice: x: 4, y: 4 (y_hi: 2, y_lo: 2; y = y_hi * 2 + y_lo), z: 4, core: 2. Of those that a mesh axis runs over, the one named last changes fastest.
Arguments:
- tokens: bfloat16 [4096, 2048], P(('fsdp', 'ctx')), may hold values from -6 to 6
- lengths: int32 [2, 3], P('fsdp'), may hold values from 1 to 1920, as said below
- routes: int32 [4096, 6], P(('fsdp', 'ctx')), may hold values from 0 to 7, all different within a row
- cotangent: bfloat16 [4096, 2048], P(('fsdp', 'ctx')), may hold values from -6 to 6
- attn_gain: bfloat16 [2048], P(('fsdp', 'ctx')), may hold values from 0.5 to 1.5
- w_query: bfloat16 [2048, 3072], P(('fsdp', 'ctx'), 'tp'), may hold values from -0.125 to 0.125
- w_latent: bfloat16 [2048, 576], P(('fsdp', 'ctx')), may hold values from -0.125 to 0.125
- latent_gain: bfloat16 [512], P(('fsdp', 'ctx')), may hold values from 0.5 to 1.5
- w_expand: bfloat16 [512, 4096], P(('fsdp', 'ctx'), 'tp'), may hold values from -0.25 to 0.25
- w_out: bfloat16 [2048, 2048], P('tp', ('fsdp', 'ctx')), may hold values from -3 to 3
- moe_gain: bfloat16 [2048], P(('fsdp', 'ctx')), may hold values from 0.5 to 1.5
- w_router: bfloat16 [2048, 8], P(('fsdp', 'ctx')), may hold values from -0.0625 to 0.0625
- w_gate: bfloat16 [8, 2048, 1408], P(None, ('fsdp', 'ctx'), 'tp'), may hold values from -0.125 to 0.125
- w_up: bfloat16 [8, 2048, 1408], P(None, ('fsdp', 'ctx'), 'tp'), may hold values from -0.125 to 0.125
- w_down: bfloat16 [8, 1408, 2048], P(None, 'tp', ('fsdp', 'ctx')), may hold values from -0.15625 to 0.15625
- shared_gate: bfloat16 [2048, 2816], P(('fsdp', 'ctx'), 'tp'), may hold values from -0.125 to 0.125
- shared_up: bfloat16 [2048, 2816], P(('fsdp', 'ctx'), 'tp'), may hold values from -0.125 to 0.125
- shared_down: bfloat16 [2816, 2048], P('tp', ('fsdp', 'ctx')), may hold values from -0.109375 to 0.109375
Outputs:
- output: bfloat16 [4096, 2048], P(('fsdp', 'ctx'))
- d_tokens: float32 [4096, 2048], P(('fsdp', 'ctx'))
- d_attn_gain: float32 [2048], P(('fsdp', 'ctx'))
- d_w_query: float32 [2048, 3072], P(('fsdp', 'ctx'), 'tp')
- d_w_latent: float32 [2048, 576], P(('fsdp', 'ctx'))
- d_latent_gain: float32 [512], P(('fsdp', 'ctx'))
- d_w_expand: float32 [512, 4096], P(('fsdp', 'ctx'), 'tp')
- d_w_out: float32 [2048, 2048], P('tp', ('fsdp', 'ctx'))
- d_moe_gain: float32 [2048], P(('fsdp', 'ctx'))
- d_w_router: float32 [2048, 8], P(('fsdp', 'ctx'))
- d_w_gate: float32 [8, 2048, 1408], P(None, ('fsdp', 'ctx'), 'tp')
- d_w_up: float32 [8, 2048, 1408], P(None, ('fsdp', 'ctx'), 'tp')
- d_w_down: float32 [8, 1408, 2048], P(None, 'tp', ('fsdp', 'ctx'))
- d_shared_gate: float32 [2048, 2816], P(('fsdp', 'ctx'), 'tp')
- d_shared_up: float32 [2048, 2816], P(('fsdp', 'ctx'), 'tp')
- d_shared_down: float32 [2816, 2048], P('tp', ('fsdp', 'ctx'))
The draws below stay inside these ranges and needn't reach their ends.
Inputs may be any that keep to these rules, and one draw needn't show every extreme that they name: `lengths`: in each row the first and the last document are shorter than 128 and the middle one has 1920 positions; a row sums to 2048. `routes`: each row names 6 different experts.
All inputs are finite; a program needn't handle non-finite values.
Results may differ from the reference program's by a relative error of at most 0.035.
Values may be sent and summed in bfloat16 or wider, within the bound.
No kernel may reach another device: no remote copies, remote signals or barrier semaphores. Data moves between devices by JAX's collectives and lax.ppermute only.
A program may use at most 192 MiB of HBM per device.

```python
import jax
import jax.numpy as jnp
from jax import lax

D = 2048
H = 16
NOPE = 128
ROPE = 64
VD = 128
R = 512
FF = 1408
SFF = 2816
TOP = 6
E = 8
PACK_MIN = 2048
TOK_DEV = 128
PACK = 2048
TOKENS = 4096
N_FSDP = 2
N_CTX = 16


def draw_lengths(key, part):
    key = jax.random.fold_in(key, 7)
    leading = jax.random.randint(key, (N_FSDP, 1), 1, TOK_DEV).astype(jnp.int32)
    trailing = (TOK_DEV - leading).astype(jnp.int32)
    middle_len = jnp.full((N_FSDP, 1), TOK_DEV * N_CTX - TOK_DEV, jnp.int32)
    return jnp.concatenate([leading, middle_len, trailing], axis=1).astype(jnp.int32)


def block_levels(rng, dims, cuts, smallest, largest):
    level, own = 1.0, jax.random.fold_in(rng, 6)
    for axis_at, blocks in cuts:
        draws = jnp.exp(jax.random.uniform(jax.random.fold_in(own, axis_at), (blocks,), jnp.float32, smallest / len(cuts), largest / len(cuts)))
        level = level * jnp.repeat(draws, dims[axis_at] // blocks).reshape([-1 if axis == axis_at else 1 for axis in range(len(dims))])
    return level


def distinct(rng, rows, amount, top, lift):
    order = jax.random.permutation(jax.random.fold_in(rng, 1), amount)
    boost = order
    for power in range(3):
        boost = boost * boost // amount
    boost = boost * lift // amount
    lots = jax.random.randint(jax.random.fold_in(rng, 2), (rows, amount), 0, 4096) + boost
    sure = jax.random.permutation(jax.random.fold_in(rng, 3), rows)[jnp.arange(amount) % rows]
    lots = jnp.where(jnp.arange(rows)[:, None] == sure[None, :], 1 << 14, lots)
    score = lots * amount + jnp.arange(amount)
    return lax.top_k(score.astype(jnp.int32), top)[1].astype(jnp.int32)


def noise(key, extent, spread, most, shards=(), held_as=jnp.bfloat16):
    drawn = jax.random.normal(key, extent, jnp.float32) * spread
    if len(shards) > 0:
        drawn = block_levels(key, extent, shards, -0.22, 0.18) * drawn
    return jnp.clip(drawn, min=-most, max=most).astype(held_as)


def setup_inputs(seed: int = 0) -> dict:
    splits = jax.random.split(jax.random.key(seed), 19)
    tokens = noise(splits[0], (TOKENS, D), 1.0, 6.0, ((0, 32),))
    lengths = draw_lengths(jax.random.fold_in(splits[18], 71), 0)
    routes = distinct(splits[2], TOKENS, E, TOP, 6144)
    cotangent = noise(splits[3], (TOKENS, D), 1.0, 6.0, ((0, 32),))
    attn_gain = jnp.clip(1.0 + 0.1 * jax.random.normal(splits[4], (D,), jnp.float32), 0.5, 1.5).astype(jnp.bfloat16)
    w_query = noise(splits[5], (D, H * (NOPE + ROPE)), D ** -0.5, 0.125, ((0, 32), (1, 4)))
    w_latent = noise(splits[6], (D, R + ROPE), D ** -0.5, 0.125, ((0, 32),))
    latent_gain = jnp.clip(1.0 + 0.1 * jax.random.normal(splits[7], (R,), jnp.float32), 0.5, 1.5).astype(jnp.bfloat16)
    w_expand = noise(splits[8], (R, H * (NOPE + VD)), R ** -0.5, 0.25, ((0, 32), (1, 4)))
    w_out = noise(splits[9], (H * VD, D), (max(1, 4 * H * VD // PACK_MIN)) ** -0.5, 3.0, ((0, 4), (1, 32)))
    moe_gain = jnp.clip(1.0 + 0.1 * jax.random.normal(splits[10], (D,), jnp.float32), 0.5, 1.5).astype(jnp.bfloat16)
    w_router = noise(splits[11], (D, E), (4 * D) ** -0.5, 0.0625, ((0, 32),))
    w_gate = noise(splits[12], (E, D, FF), D ** -0.5, 0.125, ((1, 32), (2, 4)))
    w_up = noise(splits[13], (E, D, FF), D ** -0.5, 0.125, ((1, 32), (2, 4)))
    w_down = noise(splits[14], (E, FF, D), FF ** -0.5, 0.15625, ((1, 4), (2, 32)))
    shared_gate = noise(splits[15], (D, SFF), D ** -0.5, 0.125, ((0, 32), (1, 4)))
    shared_up = noise(splits[16], (D, SFF), D ** -0.5, 0.125, ((0, 32), (1, 4)))
    shared_down = noise(splits[17], (SFF, D), SFF ** -0.5, 0.109375, ((0, 4), (1, 32)))
    return dict(tokens=tokens, lengths=lengths, routes=routes, cotangent=cotangent, attn_gain=attn_gain, w_query=w_query, w_latent=w_latent, latent_gain=latent_gain, w_expand=w_expand, w_out=w_out, moe_gain=moe_gain, w_router=w_router, w_gate=w_gate, w_up=w_up, w_down=w_down, shared_gate=shared_gate, shared_up=shared_up, shared_down=shared_down)


@jax.custom_vjp
def low(v):
    return lax.optimization_barrier(v.astype(jnp.bfloat16)).astype(jnp.float32)

@jax.custom_vjp
def low_back(v):
    return v

def low_keep(v):
    return (low(v), None)

def low_pass(kept, grad):
    return (grad,)

def back_keep(v):
    return (v, None)

def back_low(kept, grad):
    return (low(grad),)
low.defvjp(low_keep, low_pass)
low_back.defvjp(back_keep, back_low)
epsilon = 1e-06
rope_base = 50000.0
route_scale = 2.446
highest = lax.Precision.HIGHEST

def product(left, right):
    return jnp.dot(left, right, precision=highest, preferred_element_type=jnp.float32)

def rms_unit(values):
    return values * lax.rsqrt(lax.optimization_barrier(jnp.mean(values * values, axis=-1, keepdims=True)) + epsilon)

def rotary(values, cosine, sine_part):
    half_width = values.shape[-1] // 2
    front_half = values[..., :half_width]
    back_half = values[..., half_width:]
    return jnp.concatenate([front_half * cosine - back_half * sine_part, back_half * cosine + front_half * sine_part], axis=-1)

def angle_tables(within, half_width):
    frequency = rope_base ** (-jnp.arange(half_width, dtype=jnp.float32) / half_width)
    angles = within.astype(jnp.float32)[:, None] * frequency[None, :]
    return (jnp.cos(angles), jnp.sin(angles))

def doc_layout(doc_lengths, pack_len):
    doc_ends = jnp.cumsum(doc_lengths).astype(jnp.int32)
    positions = jnp.arange(pack_len, dtype=jnp.int32)
    doc_ids = lax.optimization_barrier(jnp.sum((positions[:, None] >= doc_ends[None, :-1]).astype(jnp.int32), axis=1))
    doc_starts = doc_ends - doc_lengths
    belongs = doc_ids[:, None] == jnp.arange(doc_lengths.shape[0], dtype=jnp.int32)[None, :]
    doc_first = lax.optimization_barrier(jnp.sum(jnp.where(belongs, doc_starts[None, :], 0), axis=1)).astype(jnp.int32)
    return (doc_ids, positions, positions - doc_first)

def attend_block(query_rows, row_docs, row_places, key_rows, doc_ids, positions):
    score_scale = (NOPE + ROPE) ** (-0.5)
    scores = low_back(score_scale * jnp.einsum('thc,kc->htk', query_rows, key_rows, precision=highest))
    allowed = (row_docs[:, None] == doc_ids[None, :]) & (positions[None, :] <= row_places[:, None])
    scores = jnp.where(allowed[None], scores, -1e+30)
    weights_soft = low(jax.nn.softmax(scores, axis=-1))
    return jnp.einsum('htk,kr->thr', weights_soft, key_rows[:, :R], precision=highest)

def attend(query_cat, key_rows, doc_ids, positions):
    row_count = query_cat.shape[0]
    block_rows = min(512, row_count)
    blocks = row_count // block_rows
    shaped = (query_cat.reshape(blocks, block_rows, query_cat.shape[1], query_cat.shape[2]), doc_ids.reshape(blocks, block_rows), positions.reshape(blocks, block_rows))
    step_fn = jax.checkpoint(lambda pieces: attend_block(pieces[0], pieces[1], pieces[2], key_rows, doc_ids, positions))
    mixture = lax.map(step_fn, shaped)
    return mixture.reshape(row_count, query_cat.shape[1], R)

def expert_branch(normed, gate_weight, up_weight, down_weight):
    gate_pre = low_back(product(normed, gate_weight))
    up_pre = low_back(product(normed, up_weight))
    hidden_act = low(jax.nn.silu(gate_pre) * up_pre)
    return low_back(product(hidden_act, down_weight))

def layer(residual_in, weights_f32, doc_ids, positions, within, chosen):
    attn_gain, w_query, w_latent, latent_gain, w_expand, w_out, moe_gain, w_router, w_gate, w_up, w_down, shared_gate, shared_up, shared_down = weights_f32
    row_count = residual_in.shape[0]
    head_count = w_query.shape[1] // (NOPE + ROPE)
    cosine, sine_part = angle_tables(within, ROPE // 2)
    hidden = low(rms_unit(residual_in) * attn_gain)
    queries = low_back(product(hidden, w_query)).reshape(row_count, head_count, NOPE + ROPE)
    queries = low(jnp.concatenate([queries[..., :NOPE], rotary(queries[..., NOPE:], cosine[:, None], sine_part[:, None])], axis=-1))
    latent = low_back(product(hidden, w_latent))
    compact = low(rms_unit(latent[:, :R]) * latent_gain)
    key_rot = low(rotary(latent[:, R:], cosine, sine_part))
    key_rows = jnp.concatenate([compact, key_rot], axis=-1)
    expand = w_expand.reshape(R, head_count, NOPE + VD)
    absorbed = low(low_back(jnp.einsum('thn,rhn->thr', queries[..., :NOPE], expand[..., :NOPE], precision=highest)))
    query_cat = jnp.concatenate([absorbed, queries[..., NOPE:]], axis=-1)
    mixture = low(low_back(attend(query_cat, key_rows, doc_ids, positions)))
    head_out = low(low_back(jnp.einsum('thr,rhv->thv', mixture, expand[..., NOPE:], precision=highest)))
    attention = low_back(product(head_out.reshape(row_count, head_count * VD), w_out))
    middle = residual_in + attention
    normed = low(rms_unit(middle) * moe_gain)
    router_sig = jax.nn.sigmoid(product(normed, w_router))
    picked = lax.optimization_barrier(jnp.sum((chosen[:, :, None] == jnp.arange(E, dtype=jnp.int32)[None, None, :]).astype(jnp.float32), axis=1))
    weighted = router_sig * picked
    gate_values = route_scale * weighted / lax.optimization_barrier(jnp.sum(weighted, axis=1, keepdims=True))
    expert_rows = jax.vmap(expert_branch, in_axes=(None, 0, 0, 0))(normed, w_gate, w_up, w_down)
    expert_sum = lax.optimization_barrier(jnp.sum(gate_values.T[:, :, None] * expert_rows, axis=0)) + expert_branch(normed, shared_gate, shared_up, shared_down)
    return middle + expert_sum

def reference(tokens, lengths, routes, cotangent, attn_gain, w_query, w_latent, latent_gain, w_expand, w_out, moe_gain, w_router, w_gate, w_up, w_down, shared_gate, shared_up, shared_down):
    weights_f32 = tuple((weight.astype(jnp.float32) for weight in (attn_gain, w_query, w_latent, latent_gain, w_expand, w_out, moe_gain, w_router, w_gate, w_up, w_down, shared_gate, shared_up, shared_down)))
    stream = tokens.astype(jnp.float32).reshape(N_FSDP, PACK, D)
    upstream = cotangent.astype(jnp.float32).reshape(N_FSDP, PACK, D)
    chosen_all = routes.reshape(N_FSDP, PACK, TOP)

    def pack_step(grad_sums, pack_item):
        residual_in, grad_out, doc_lengths, chosen = pack_item
        doc_ids, positions, within = doc_layout(doc_lengths, PACK)

        def forward(stream_in, weight_set):
            return layer(stream_in, weight_set, doc_ids, positions, within, chosen)
        output, pullback = jax.vjp(forward, residual_in, weights_f32)
        grad_in, grad_weights = pullback(grad_out)
        grad_sums = jax.tree.map(lambda left, right: left + right, grad_sums, grad_weights)
        return (grad_sums, (output.astype(jnp.bfloat16), grad_in))
    zero_grads = jax.tree.map(jnp.zeros_like, weights_f32)
    grad_sums, (outputs, grad_tokens) = lax.scan(pack_step, zero_grads, (stream, upstream, lengths, chosen_all))
    return (outputs.reshape(TOKENS, D), grad_tokens.reshape(TOKENS, D), grad_sums[0], grad_sums[1], grad_sums[2], grad_sums[3], grad_sums[4], grad_sums[5], grad_sums[6], grad_sums[7], grad_sums[8], grad_sums[9], grad_sums[10], grad_sums[11], grad_sums[12], grad_sums[13])
```

```python
import jax
import jax.numpy as jnp
from jax import lax
from jax.experimental import pallas as pl
from jax.experimental.pallas import tpu as pltpu
from jax.sharding import PartitionSpec as P

NOPE = 128
ROPE = 64
VD = 128
R = 512
E = 8
FF_PAD = 384
SH_PAD = 128

epsilon = 1e-06
rope_base = 50000.0
route_scale = 2.446
highest = lax.Precision.HIGHEST
bf16 = jnp.bfloat16
f32 = jnp.float32

PLANE = ("fsdp", "ctx")


def mask(ky=0, kx=0, kc=0):
    return (ky & 1) * 16 + (ky >> 1) * 8 + kx * 2 + kc


def swap(values, ky=0, kx=0, kc=0):
    bits = mask(ky, kx, kc)
    return lax.ppermute(values, PLANE, [(i, i ^ bits) for i in range(32)])


def swap_z(values, k):
    return lax.ppermute(values, "tp", [(i, i ^ k) for i in range(4)])


def arrange(parts, places, count, rows, me):
    width = parts[0].shape[-1]

    def kernel(me_ref, *refs):
        ins, out, sem = refs[: len(parts)], refs[len(parts)], refs[len(parts) + 1]
        copies = []
        for n, (part, index, row, bits) in enumerate(places):
            height = parts[part].shape[1]
            copies.append(
                pltpu.make_async_copy(
                    ins[part].at[index],
                    out.at[me_ref[0] ^ bits, pl.ds(row, height)],
                    sem.at[n],
                )
            )
        for copy in copies:
            copy.start()
        for copy in copies:
            copy.wait()

    return pl.pallas_call(
        kernel,
        out_shape=jax.ShapeDtypeStruct((count, rows, width), parts[0].dtype),
        in_specs=[pl.BlockSpec(memory_space=pltpu.SMEM)]
        + [pl.BlockSpec(memory_space=pl.ANY)] * len(parts),
        out_specs=pl.BlockSpec(memory_space=pl.ANY),
        scratch_shapes=[pltpu.SemaphoreType.DMA((len(places),))],
    )(me.reshape(1), *parts)


def pick(source, order, me):
    def kernel(me_ref, src, out, sem):
        copies = [
            pltpu.make_async_copy(src.at[me_ref[0] ^ bits], out.at[n], sem.at[n])
            for n, bits in enumerate(order)
        ]
        for copy in copies:
            copy.start()
        for copy in copies:
            copy.wait()

    return pl.pallas_call(
        kernel,
        out_shape=jax.ShapeDtypeStruct((len(order),) + source.shape[1:], source.dtype),
        in_specs=[
            pl.BlockSpec(memory_space=pltpu.SMEM),
            pl.BlockSpec(memory_space=pl.ANY),
        ],
        out_specs=pl.BlockSpec(memory_space=pl.ANY),
        scratch_shapes=[pltpu.SemaphoreType.DMA((len(order),))],
    )(me.reshape(1), source)


def total(parts, dtype=bf16):
    out = parts[0].astype(f32)
    for part in parts[1:]:
        out = out + part.astype(f32)
    return out.astype(dtype)


def gather_plane(block, me):
    half = block.shape[0] // 2
    along_x = jnp.stack([block[:half]] + [swap(block[:half], kx=k) for k in (1, 2, 3)])
    along_y = jnp.stack([block[half:]] + [swap(block[half:], ky=k) for k in (1, 2, 3)])
    first = [along_x] + [swap(along_x, ky=k) for k in (1, 2, 3)]
    second = [along_y] + [swap(along_y, kx=k) for k in (1, 2, 3)]
    parts, places = [], []
    for kc in (0, 1):
        for major in range(4):
            for row, halves in ((0, first), (half, second)):
                part = halves[major] if kc == 0 else swap(halves[major], kc=1)
                for minor in range(4):
                    ky, kx = (major, minor) if row == 0 else (minor, major)
                    places.append((len(parts), minor, row, mask(ky, kx, kc)))
                parts.append(part)
    return arrange(parts, places, 32, block.shape[0], me)


def scatter_plane(blocks, me):
    order = [mask(ky, kx, 0) for ky in range(4) for kx in range(4)]
    keep = pick(blocks, order, me)
    send = pick(blocks, [bits + 1 for bits in order], me)
    both = total([keep, swap(send, kc=1)])
    both = both.reshape((4, 4) + both.shape[1:])
    half = blocks.shape[1] // 2
    first, second = both[:, :, :half], both[:, :, half:]
    first = total([first[:, 0]] + [swap(first[:, k], kx=k) for k in (1, 2, 3)])
    second = total([second[0]] + [swap(second[k], ky=k) for k in (1, 2, 3)])
    first = total([first[0]] + [swap(first[k], ky=k) for k in (1, 2, 3)], f32)
    second = total([second[0]] + [swap(second[k], kx=k) for k in (1, 2, 3)], f32)
    return jnp.concatenate([first, second], axis=0)


def part_z(values, k, z):
    rows = values.shape[0] // 4
    return lax.dynamic_slice_in_dim(values, (z ^ k) * rows, rows, 0)


def scatter_z(values, z, dtype=bf16):
    return total([part_z(values, 0, z)] + [swap_z(part_z(values, k, z), k) for k in (1, 2, 3)], dtype)


def gather_z(values, z):
    rows = values.shape[0]
    out = jnp.zeros((4 * rows,) + values.shape[1:], values.dtype)
    for k in range(4):
        piece = values if k == 0 else swap_z(values, k)
        out = lax.dynamic_update_slice_in_dim(out, piece, (z ^ k) * rows, 0)
    return out


def gather_rows(values):
    own = [values] + [swap(values, kx=k) for k in (1, 2, 3)]
    other = [swap(part, kc=1) for part in own]
    return jnp.concatenate(own + other, axis=0)


def rms_parts(values):
    inverse = lax.rsqrt(jnp.mean(values * values, axis=-1, keepdims=True) + epsilon)
    return (values * inverse, inverse)


def norm_back(grad_normed, unit_rows, inverse, gain_vec):
    scaled = grad_normed * gain_vec
    grad_gain = jnp.sum(grad_normed * unit_rows, axis=0)
    grad_in = inverse * (scaled - unit_rows * jnp.mean(scaled * unit_rows, axis=-1, keepdims=True))
    return (grad_in, grad_gain)


def rotary(values, cosine, sine_part):
    half_width = values.shape[-1] // 2
    front_half = values[..., :half_width]
    back_half = values[..., half_width:]
    return jnp.concatenate(
        [front_half * cosine - back_half * sine_part, back_half * cosine + front_half * sine_part],
        axis=-1,
    )


def angle_tables(within, half_width):
    frequency = rope_base ** (-jnp.arange(half_width, dtype=jnp.float32) / half_width)
    angles = within.astype(jnp.float32)[:, None] * frequency[None, :]
    return (jnp.cos(angles), jnp.sin(angles))


def doc_layout(doc_lengths, pack_len):
    doc_ends = jnp.cumsum(doc_lengths)
    positions = jnp.arange(pack_len, dtype=jnp.int32)
    doc_ids = jnp.sum((positions[:, None] >= doc_ends[None, :-1]).astype(jnp.int32), axis=1)
    doc_starts = doc_ends - doc_lengths
    belongs = doc_ids[:, None] == jnp.arange(doc_lengths.shape[0], dtype=jnp.int32)[None, :]
    doc_first = jnp.sum(jnp.where(belongs, doc_starts[None, :], 0), axis=1)
    return (doc_ids, positions, positions - doc_first)


def pad_to(values, width):
    return jnp.pad(values, [(0, 0)] * (values.ndim - 1) + [(0, width - values.shape[-1])])


def dot(left, right):
    return jnp.dot(left, right, preferred_element_type=f32)


def shards(
    tokens,
    lengths,
    routes,
    cotangent,
    attn_gain,
    w_query,
    w_latent,
    latent_gain,
    w_expand,
    w_out,
    moe_gain,
    w_router,
    w_gate,
    w_up,
    w_down,
    shared_gate,
    shared_up,
    shared_down,
):
    me = lax.axis_index("fsdp") * 16 + lax.axis_index("ctx")
    place = lax.axis_index("ctx")
    member = place % 8
    z = lax.axis_index("tp")
    row_count, width = tokens.shape
    db = width // 32
    pack_len = row_count * 16
    rb = R // 32
    local_heads = w_query.shape[1] // (NOPE + ROPE)
    ff, sh = w_gate.shape[2], shared_gate.shape[1] // 8

    aux = jnp.concatenate(
        [attn_gain[None], moe_gain[None], pad_to(latent_gain[None], db), jnp.zeros((5, db), bf16), w_router.T],
        axis=0,
    )
    aux = jnp.pad(aux, ((0, db - 16), (0, 0)))
    expand_rows = jnp.concatenate(jnp.split(w_expand, local_heads, axis=1), axis=0)
    packed = jnp.concatenate([w_query, w_latent, aux, w_out.T, expand_rows], axis=1)
    gathered = gather_plane(packed, me)
    cuts, edge = [], 0
    for piece in (w_query, w_latent, aux, w_out.T, expand_rows):
        cuts.append(gathered[:, :, edge : edge + piece.shape[1]])
        edge += piece.shape[1]
    query_weight = cuts[0].reshape(width, -1)
    latent_weight = cuts[1].reshape(width, -1)
    gain_attn = cuts[2][:, 0].reshape(width).astype(f32)
    gain_moe = cuts[2][:, 1].reshape(width).astype(f32)
    gain_latent = cuts[2][:, 2, :rb].reshape(R).astype(f32)
    router_weight = jnp.swapaxes(cuts[2][:, 8:16], 0, 1).reshape(E, width).T
    out_weight_t = cuts[3].reshape(width, -1)
    expand = jnp.swapaxes(cuts[4].reshape(32, local_heads, rb, NOPE + VD), 0, 1).reshape(
        local_heads, R, NOPE + VD
    )
    key_weight = expand[..., :NOPE]
    value_weight = expand[..., NOPE:]

    def with_shared(routed, shared):
        shared = jnp.stack(jnp.split(shared, 8, axis=1))
        return jnp.concatenate([pad_to(routed, FF_PAD), pad_to(shared, SH_PAD)], axis=-1)

    experts = jnp.stack(
        [
            with_shared(w_gate, shared_gate),
            with_shared(w_up, shared_up),
            with_shared(jnp.swapaxes(w_down, 1, 2), shared_down.T),
        ],
        axis=1,
    )
    wide = experts.shape[-1]
    experts = pick(experts.reshape(8, 3 * db, wide), [mask(0, kx, kc) for kc in (0, 1) for kx in range(4)], member)
    other = swap(experts[4:], kc=1)
    by_x = jnp.stack([experts[:4], other], axis=1)
    mine = [by_x[0]] + [swap(by_x[k], kx=k) for k in (1, 2, 3)]
    mine = jnp.stack(mine)
    from_y = [mine] + [swap(mine, ky=k) for k in (1, 2, 3)]
    parts = [part.reshape(8, 3 * db, wide) for part in from_y]
    places = [
        (ky, kx * 2 + kc, 0, mask(ky, kx, kc)) for ky in range(4) for kx in range(4) for kc in (0, 1)
    ]
    mine = arrange(parts, places, 32, 3 * db, me).reshape(32, 3, db, wide)
    gate_weight = mine[:, 0].reshape(width, wide)
    up_weight = mine[:, 1].reshape(width, wide)
    down_weight_t = mine[:, 2].reshape(width, wide)

    picked = jnp.sum(
        (routes[:, :, None] == jnp.arange(E, dtype=jnp.int32)[None, None, :]).astype(f32), axis=1
    )
    group_in = gather_rows(jnp.concatenate([cotangent, pad_to(picked.astype(bf16), 128)], axis=1))
    group_cot = group_in[:, :width]
    group_picked = group_in[:, width : width + E].astype(f32)

    doc_ids, positions, within_all = doc_layout(lengths[0], pack_len)
    offset = place * row_count
    own_docs = lax.dynamic_slice_in_dim(doc_ids, offset, row_count, 0)
    own_places = lax.dynamic_slice_in_dim(positions, offset, row_count, 0)
    own_within = lax.dynamic_slice_in_dim(within_all, offset, row_count, 0)
    cosine, sine_part = angle_tables(own_within, ROPE // 2)
    residual_in = tokens.astype(f32)
    unit_attn, scale_attn = rms_parts(residual_in)
    hidden = (unit_attn * gain_attn).astype(bf16)
    query_raw = dot(hidden, query_weight).reshape(row_count, local_heads, NOPE + ROPE)
    queries = jnp.concatenate(
        [query_raw[..., :NOPE], rotary(query_raw[..., NOPE:], cosine[:, None], sine_part[:, None])],
        axis=-1,
    ).astype(bf16)
    latent = dot(hidden, latent_weight)
    unit_latent, scale_latent = rms_parts(latent[:, :R])
    compact = unit_latent * gain_latent
    key_rot = rotary(latent[:, R:], cosine, sine_part)
    own_keys = jnp.concatenate([compact, key_rot], axis=-1).astype(bf16)

    along_x = jnp.stack([own_keys] + [swap(own_keys, kx=k) for k in (1, 2, 3)])
    along_y = [along_x, swap(along_x, ky=2)]
    key_parts = along_y + [swap(part, kc=1) for part in along_y]
    key_places = [
        (kc * 2 + yh, kx, 0, yh * 8 + kx * 2 + kc) for kc in (0, 1) for yh in (0, 1) for kx in range(4)
    ]
    key_rows = arrange(key_parts, key_places, 16, row_count, place).reshape(pack_len, R + ROPE)

    absorbed = jnp.einsum(
        "thn,hrn->thr", queries[..., :NOPE], key_weight, preferred_element_type=f32
    ).astype(bf16)
    query_cat = jnp.concatenate([absorbed, queries[..., NOPE:]], axis=-1)
    score_scale = (NOPE + ROPE) ** (-0.5)
    allowed = (own_docs[:, None] == doc_ids[None, :]) & (positions[None, :] <= own_places[:, None])
    scores = score_scale * jnp.einsum("thc,kc->htk", query_cat, key_rows, preferred_element_type=f32)
    scores = jnp.where(allowed[None], scores, -1e30)
    row_max = jnp.max(scores, axis=-1, keepdims=True)
    weights = jnp.exp(scores - row_max)
    probs_low = (weights / jnp.sum(weights, axis=-1, keepdims=True)).astype(bf16)
    mixture = jnp.einsum("htk,kr->thr", probs_low, key_rows[:, :R], preferred_element_type=f32).astype(bf16)
    head_out = (
        jnp.einsum("thr,hrv->thv", mixture, value_weight, preferred_element_type=f32)
        .astype(bf16)
        .reshape(row_count, local_heads * VD)
    )
    attention = jnp.einsum("tv,dv->td", head_out, out_weight_t, preferred_element_type=f32)
    attention = gather_z(scatter_z(attention.astype(bf16), z), z)
    middle = residual_in + attention.astype(f32)
    unit_moe, scale_moe = rms_parts(middle)
    normed = (unit_moe * gain_moe).astype(bf16)
    router_sig = jax.nn.sigmoid(dot(normed, router_weight))
    weighted = router_sig * picked
    gate_total = jnp.sum(weighted, axis=1, keepdims=True)
    gate_values = route_scale * weighted / gate_total
    grad_out = cotangent.astype(f32)

    group = gather_rows(normed)
    group_weighted = jax.nn.sigmoid(dot(group, router_weight)) * group_picked
    group_gates = route_scale * group_weighted / jnp.sum(group_weighted, axis=1, keepdims=True)
    gate_own = jnp.sum(
        jnp.where(jnp.arange(E)[None, :] == member, group_gates, 0.0), axis=1, keepdims=True
    )
    gate_row = jnp.concatenate(
        [jnp.broadcast_to(gate_own, (gate_own.shape[0], FF_PAD)), jnp.ones((gate_own.shape[0], SH_PAD), f32)],
        axis=1,
    )
    gate_pre = dot(group, gate_weight)
    up_pre = dot(group, up_weight)
    sig = jax.nn.sigmoid(gate_pre)
    silu = gate_pre * sig
    act = silu * up_pre
    act_low = (gate_row * act).astype(bf16)
    grad_act_bare = dot(group_cot, down_weight_t)
    grad_gate_own = jnp.sum((act * grad_act_bare)[:, :FF_PAD], axis=1, keepdims=True)
    grad_act = grad_act_bare * gate_row
    grad_gate_pre = (grad_act * up_pre * (sig * (1.0 + gate_pre * (1.0 - sig)))).astype(bf16)
    grad_up_pre = (grad_act * silu).astype(bf16)
    expert_part = jnp.einsum("tf,df->td", act_low, down_weight_t, preferred_element_type=f32).astype(bf16)
    grad_part = (
        jnp.einsum("tf,df->td", grad_gate_pre, gate_weight, preferred_element_type=f32)
        + jnp.einsum("tf,df->td", grad_up_pre, up_weight, preferred_element_type=f32)
    ).astype(bf16)
    d_down_t = jnp.einsum("td,tf->df", group_cot, act_low, preferred_element_type=f32).astype(bf16)
    d_gate = jnp.einsum("td,tf->df", group, grad_gate_pre, preferred_element_type=f32).astype(bf16)
    d_up = jnp.einsum("td,tf->df", group, grad_up_pre, preferred_element_type=f32).astype(bf16)
    lane = jnp.arange(128)[None, :]
    high = grad_gate_own.astype(bf16).astype(f32)
    gates_part = (
        jnp.where(lane == member, high, 0.0) + jnp.where(lane == member + E, grad_gate_own - high, 0.0)
    ).astype(bf16)
    first = expert_part.reshape(2, 4, row_count, -1)
    second = jnp.concatenate([grad_part, gates_part], axis=1).reshape(2, 4, row_count, -1)
    first = total([first[0], swap(first[1], kc=1)])
    second = total([second[0], swap(second[1], kc=1)])
    first = total([first[0]] + [swap(first[k], kx=k) for k in (1, 2, 3)])
    quarter = row_count // 4

    def z_rows(values, k):
        return lax.dynamic_slice_in_dim(values, (z ^ k) * quarter, quarter, 1)

    second = total([z_rows(second, 0)] + [swap_z(z_rows(second, k), k) for k in (1, 2, 3)])
    first = scatter_z(first, z)
    second = total([second[0]] + [swap(second[k], kx=k) for k in (1, 2, 3)])
    expert_sum = gather_z(first, z)
    second = gather_z(second, z)
    output = (middle + expert_sum.astype(f32)).astype(bf16)
    grad_normed = second[:, :width].astype(f32)
    grad_gates = second[:, width : width + E].astype(f32) + second[:, width + E : width + 2 * E].astype(f32)

    d_experts = jnp.stack(
        [d_gate.reshape(32, db, wide), d_up.reshape(32, db, wide), d_down_t.reshape(32, db, wide)], axis=1
    ).reshape(32, 3 * db, wide)
    d_experts = pick(
        d_experts, [mask(ky, kx, kc) for ky in range(4) for kx in range(4) for kc in (0, 1)], me
    ).reshape(4, 4, 2, 3 * db, wide)
    d_experts = total([d_experts[0]] + [swap(d_experts[k], ky=k) for k in (1, 2, 3)])
    d_experts = jnp.stack([d_experts[0]] + [swap(d_experts[k], kx=k) for k in (1, 2, 3)])
    d_parts = [d_experts[:, 0], swap(d_experts[:, 1], kc=1)]
    d_experts = arrange(
        d_parts, [(kc, kx, 0, kx * 2 + kc) for kc in (0, 1) for kx in range(4)], 8, 3 * db, member
    )
    d_experts = d_experts.reshape(8, 3, db, wide).astype(f32)
    d_routed = [d_experts[:, i, :, :ff] for i in range(3)]
    d_shared = [
        jnp.concatenate([d_experts[e, i, :, FF_PAD : FF_PAD + sh] for e in range(8)], axis=1) for i in range(3)
    ]

    grad_weighted = (
        route_scale * grad_gates - jnp.sum(grad_gates * gate_values, axis=1, keepdims=True)
    ) / gate_total
    grad_logits = grad_weighted * picked * router_sig * (1.0 - router_sig)
    d_router = jnp.dot(normed.astype(f32).T, grad_logits, precision=highest)
    grad_normed = grad_normed + jnp.dot(grad_logits, router_weight.astype(f32).T, precision=highest)
    grad_middle_norm, d_gain_moe = norm_back(grad_normed, unit_moe, scale_moe, gain_moe)
    grad_middle = grad_out + grad_middle_norm
    grad_attention = grad_middle.astype(bf16)
    d_out_t = jnp.einsum("td,tv->dv", grad_attention, head_out, preferred_element_type=f32)
    grad_heads = dot(grad_attention, out_weight_t).astype(bf16).reshape(row_count, local_heads, VD)
    d_value = jnp.einsum("thr,thv->hrv", mixture, grad_heads, preferred_element_type=f32)
    grad_mixture = jnp.einsum("thv,hrv->thr", grad_heads, value_weight, preferred_element_type=f32).astype(bf16)
    probs = probs_low.astype(f32)
    grad_probs = jnp.einsum("thr,kr->htk", grad_mixture, key_rows[:, :R], preferred_element_type=f32)
    grad_scores = (probs * (grad_probs - jnp.sum(probs * grad_probs, axis=-1, keepdims=True))).astype(bf16)
    grad_keys_latent = jnp.einsum("htk,thr->kr", probs_low, grad_mixture, preferred_element_type=f32)
    grad_query_cat = score_scale * jnp.einsum("htk,kc->thc", grad_scores, key_rows, preferred_element_type=f32)
    grad_keys = score_scale * jnp.einsum("htk,thc->kc", grad_scores, query_cat, preferred_element_type=f32)
    grad_keys = (grad_keys + pad_to(grad_keys_latent, R + ROPE)).astype(bf16)
    grad_absorbed = grad_query_cat[..., :R].astype(bf16)
    d_key = jnp.einsum("thn,thr->hrn", queries[..., :NOPE], grad_absorbed, preferred_element_type=f32)
    grad_nope = jnp.einsum("thr,hrn->thn", grad_absorbed, key_weight, preferred_element_type=f32)
    grad_rope = rotary(grad_query_cat[..., R:], cosine[:, None], -sine_part[:, None])
    grad_queries = (
        jnp.concatenate([grad_nope, grad_rope], axis=-1)
        .astype(bf16)
        .reshape(row_count, local_heads * (NOPE + ROPE))
    )
    d_query = jnp.einsum("td,tq->dq", hidden, grad_queries, preferred_element_type=f32)
    grad_hidden_part = jnp.einsum("tq,dq->td", grad_queries, query_weight, preferred_element_type=f32)

    grad_keys = pick(
        grad_keys.reshape(16, row_count, R + ROPE),
        [yh * 8 + kx * 2 + kc for kc in (0, 1) for kx in range(4) for yh in (0, 1)],
        place,
    ).reshape(2, 4, 2, row_count, R + ROPE)
    grad_keys = total([grad_keys[0], swap(grad_keys[1], kc=1)])
    grad_keys = total([grad_keys[0]] + [swap(grad_keys[k], kx=k) for k in (1, 2, 3)])
    grad_keys = total([grad_keys[0], swap(grad_keys[1], ky=2)])
    own_key_grads = total([grad_keys] + [swap_z(grad_keys, k) for k in (1, 2, 3)], f32)
    grad_hidden = gather_z(scatter_z(grad_hidden_part.astype(bf16), z), z).astype(f32)

    grad_compact_in, d_gain_latent = norm_back(own_key_grads[:, :R], unit_latent, scale_latent, gain_latent)
    grad_key_rot = rotary(own_key_grads[:, R:], cosine, -sine_part)
    grad_latent = jnp.concatenate([grad_compact_in, grad_key_rot], axis=-1).astype(bf16)
    d_latent = jnp.einsum("td,tq->dq", hidden, grad_latent, preferred_element_type=f32)
    grad_hidden = grad_hidden + jnp.einsum("tq,dq->td", grad_latent, latent_weight, preferred_element_type=f32)
    grad_input_norm, d_gain_attn = norm_back(grad_hidden, unit_attn, scale_attn, gain_attn)
    grad_tokens = grad_middle + grad_input_norm

    d_aux = jnp.concatenate(
        [
            d_gain_attn.reshape(32, 1, db),
            d_gain_moe.reshape(32, 1, db),
            pad_to(d_gain_latent.reshape(32, 1, rb), db),
            jnp.zeros((32, 5, db), f32),
            jnp.swapaxes(d_router.reshape(32, db, E), 1, 2),
        ],
        axis=1,
    )
    d_aux = jnp.pad(d_aux, ((0, 0), (0, db - 16), (0, 0)))
    d_expand = jnp.concatenate([d_key, d_value], axis=-1).reshape(local_heads, 32, rb, NOPE + VD)
    d_expand = jnp.swapaxes(d_expand, 0, 1).reshape(32, db, NOPE + VD)
    grads = jnp.concatenate(
        [
            piece.astype(bf16)
            for piece in (
                d_query.reshape(32, db, -1),
                d_latent.reshape(32, db, -1),
                d_aux,
                d_out_t.reshape(32, db, -1),
                d_expand,
            )
        ],
        axis=2,
    )
    owned = scatter_plane(grads, me)
    cuts, edge = [], 0
    for piece in (w_query, w_latent, aux, w_out.T, expand_rows):
        cuts.append(owned[:, edge : edge + piece.shape[1]])
        edge += piece.shape[1]
    return (
        output,
        grad_tokens,
        cuts[2][0],
        cuts[0],
        cuts[1],
        cuts[2][2, :rb],
        jnp.concatenate(jnp.split(cuts[4], local_heads, axis=0), axis=1),
        cuts[3].T,
        cuts[2][1],
        cuts[2][8:16].T,
        d_routed[0],
        d_routed[1],
        jnp.swapaxes(d_routed[2], 1, 2),
        d_shared[0],
        d_shared[1],
        d_shared[2].T,
    )


def solution(mesh):
    rows = P(PLANE, None)
    split = P(PLANE, "tp")
    vector = P(PLANE)
    turned = P("tp", PLANE)
    expert_rows = P(None, PLANE, "tp")
    expert_columns = P(None, "tp", PLANE)
    return jax.shard_map(
        shards,
        mesh=mesh,
        in_specs=(
            rows,
            P("fsdp", None),
            rows,
            rows,
            vector,
            split,
            rows,
            vector,
            split,
            turned,
            vector,
            rows,
            expert_rows,
            expert_rows,
            expert_columns,
            split,
            split,
            turned,
        ),
        out_specs=(
            rows,
            rows,
            vector,
            split,
            rows,
            vector,
            split,
            turned,
            vector,
            rows,
            expert_rows,
            expert_rows,
            expert_columns,
            split,
            split,
            turned,
        ),
        check_vma=False,
    )
```

```python
import math

import jax
import jax.numpy as jnp
from jax import lax
from jax.experimental import pallas as pl
from jax.experimental.pallas import tpu as pltpu
from jax.sharding import Mesh
from jax.sharding import PartitionSpec as P

NOPE = 128
ROPE = 64
VD = 128
R = 512
E = 8
FF_PAD = 384
SH_PAD = 128
HEADS = 4

epsilon = 1e-06
rope_base = 50000.0
route_scale = 2.446
bf16 = jnp.bfloat16
f32 = jnp.float32

PLANE = ("yl", "yh", "x", "c")
YS = ("yl", "yh")


def mask(ky=0, kx=0, kc=0):
    return (ky & 1) * 16 + (ky >> 1) * 8 + kx * 2 + kc


def swap(values, ky=0, kx=0, kc=0):
    bits = mask(ky, kx, kc)
    return lax.ppermute(values, PLANE, [(i, i ^ bits) for i in range(32)])


def swap_z(values, k):
    return lax.ppermute(values, "z", [(i, i ^ k) for i in range(4)])


def total(parts, dtype=bf16):
    out = parts[0].astype(f32)
    for part in parts[1:]:
        out = out + part.astype(f32)
    return out.astype(dtype)


def nn(left, right):
    return jnp.dot(left, right, preferred_element_type=f32)


def nt(left, right):
    return lax.dot_general(left, right, (((1,), (1,)), ((), ())), preferred_element_type=f32)


def tn(left, right):
    return lax.dot_general(left, right, (((0,), (0,)), ((), ())), preferred_element_type=f32)


def lanes(shape):
    return lax.broadcasted_iota(jnp.int32, shape, 1)


def high_low(values):
    high = values.astype(bf16)
    return high, (values - high.astype(f32)).astype(bf16)


def start_all(copies, sem):
    for source, destination in copies:
        pltpu.make_async_copy(source, destination, sem).start()


def wait_for(ref, sem):
    pltpu.make_async_copy(ref, ref, sem).wait()


def call(kernel, outs, ins, scratch, macs=0, vmem=60, after=()):
    count, late = len(ins), len(after)
    body = kernel
    if late:

        def body(*refs):
            kernel(*refs[:count], *refs[count + late :])

    moved = sum(array.size * array.dtype.itemsize for array, _ in ins)
    moved += sum(math.prod(shape) * jnp.dtype(dtype).itemsize for shape, dtype, _ in outs)
    spaces = {"s": pltpu.SMEM, "v": pltpu.VMEM, "a": pl.ANY}
    return pl.pallas_call(
        body,
        out_shape=[jax.ShapeDtypeStruct(shape, dtype) for shape, dtype, _ in outs],
        in_specs=[pl.BlockSpec(memory_space=spaces[space]) for _, space in ins]
        + [pl.BlockSpec(memory_space=pl.ANY)] * late,
        out_specs=[pl.BlockSpec(memory_space=spaces[space]) for _, _, space in outs],
        scratch_shapes=scratch,
        compiler_params=pltpu.CompilerParams(vmem_limit_bytes=vmem << 20),
        cost_estimate=pl.CostEstimate(flops=4 * macs, bytes_accessed=moved, transcendentals=0),
    )(*[array for array, _ in ins], *after)


def exchange(blocks, axes):
    return lax.all_to_all(blocks, axes, 0, 0, tiled=True)


def gather(copies, axes, after):
    own = hold(exchange(copies, axes), *after)
    return [own, swap(own, kc=1)]


def pair_copies(parts, core, target, columns=None):
    if columns is not None:
        parts = [part.at[:, :, columns] for part in parts]
    return [(parts[0], target.at[:, core]), (parts[1], target.at[:, 1 - core])]


def hold(values, *after):
    def kernel(*refs):
        pass

    return pl.pallas_call(
        kernel,
        out_shape=jax.ShapeDtypeStruct(values.shape, values.dtype),
        in_specs=[pl.BlockSpec(memory_space=pl.ANY)] * (1 + len(after)),
        out_specs=pl.BlockSpec(memory_space=pl.ANY),
        input_output_aliases={0: 0},
    )(values, *after)


def tie(values, *after):
    late = sum(jnp.abs(lax.slice(one, (0,) * one.ndim, (1,) * one.ndim).reshape(()).astype(f32)) for one in after)
    return values + jnp.where(late > 3e38, 1.0, 0.0).astype(values.dtype)


def pack_attention(w_query, w_latent, attn_gain, moe_gain, latent_gain, router_t, out_t, w_expand):
    db = w_query.shape[0]
    query = w_query.shape[1]
    late = w_latent.shape[1]
    out = out_t.shape[1]
    per_head = NOPE + ROPE

    def kernel(q, lat, ag, mg, lg, rt, ot, ex, a, b):
        plain = [q[:, h * per_head : h * per_head + NOPE] for h in range(HEADS)]
        front = [q[:, h * per_head + NOPE : h * per_head + NOPE + ROPE // 2] for h in range(HEADS)]
        back = [q[:, h * per_head + NOPE + ROPE // 2 : (h + 1) * per_head] for h in range(HEADS)]
        rb = lg.shape[1]
        small = jnp.concatenate(
            [
                ag[...].astype(f32),
                mg[...].astype(f32),
                jnp.concatenate([lg[...].astype(f32), jnp.zeros((1, db - rb), f32)], axis=1),
                jnp.zeros((5, db), f32),
                rt[...].astype(f32),
            ]
            + ([jnp.zeros((db - 16, db), f32)] if db > 16 else []),
            axis=0,
        ).astype(bf16)
        one = jnp.concatenate(plain + front + back + [lat[...], small], axis=1)
        for n in range(16):
            a[n] = one
        width = ex.shape[1] // HEADS
        expand = jnp.concatenate([ex[:, h * width : (h + 1) * width] for h in range(HEADS)], axis=0)
        b[...] = jnp.concatenate([ot[...], expand], axis=1)

    one, two = query + late + db, out + w_expand.shape[1] // HEADS
    ins = [w_query, w_latent, attn_gain[None], moe_gain[None], latent_gain[None], router_t, out_t, w_expand]
    return call(
        kernel,
        [((16, db, one), bf16, "v"), ((db, two), bf16, "v")],
        [(array, "v") for array in ins],
        [],
    )


def pack_experts(info, gate, up, down_t, shared_gate, shared_up, shared_down_t, router):
    count, db, ff = gate.shape
    sh = shared_gate.shape[1] // count
    wide = FF_PAD + SH_PAD

    def kernel(info, g, u, d, sg, su, sd, rt, keep, send, packed, sem):
        fill = FF_PAD - ff - count
        for n, (routed, shared) in enumerate(((g, sg), (u, su), (d, sd))):
            extra = rt[...] if n == 0 else jnp.zeros((db, count), bf16)
            for e in range(count):
                packed[e, n] = jnp.concatenate(
                    [
                        routed[e],
                        extra,
                        jnp.zeros((db, fill), bf16),
                        shared[:, e * sh : (e + 1) * sh],
                        jnp.zeros((db, SH_PAD - sh), bf16),
                    ],
                    axis=1,
                )
        copies = []
        for kx in range(4):
            copies.append((packed.at[info[2] ^ (kx * 2)], keep.at[kx], sem.at[0]))
            copies.append((packed.at[info[2] ^ (kx * 2 + 1)], send.at[kx], sem.at[1]))
        for source, destination, which in copies:
            pltpu.make_async_copy(source, destination, which).start()
        wait_for(keep, sem.at[0])
        wait_for(send, sem.at[1])

    ins = [gate, up, down_t, shared_gate, shared_up, shared_down_t, router]
    return call(
        kernel,
        [((4, 3, db, wide), bf16, "a")] * 2,
        [(info, "s")] + [(array, "v") for array in ins],
        [pltpu.VMEM((count, 3, db, wide), bf16), pltpu.SemaphoreType.DMA((2,))],
    )


def project(info, tokens, cos4, sin4, parts, after):
    rows, width = tokens.shape
    db = width // 32
    rb = R // 32
    query = HEADS * (NOPE + ROPE)
    tile = ROPE + db
    half = ROPE // 2
    columns = query + R + tile

    def kernel(info, tok, cos, sin, *refs):
        ins, refs = refs[: len(parts)], refs[len(parts) :]
        hidden, q_nope, q_rope, keys, latent_out, small, gain_row, pairs, sem = refs
        start_all(pair_copies(ins, info[1] % 2, pairs), sem)
        x = tok[...].astype(f32)
        inverse = lax.rsqrt(jnp.mean(x * x, axis=-1, keepdims=True) + epsilon)
        unit = x * inverse
        wait_for(pairs, sem)
        weights = pairs.reshape(32, db, columns)
        lane = lanes((16, tile))
        tiles = []
        for t in range(16):
            even = weights[2 * t, 0:16, columns - tile :].astype(f32)
            odd = weights[2 * t + 1, 0:16, columns - tile :].astype(f32)
            tiles.append(jnp.where(lane < db, pltpu.roll(even, tile - db, 1), odd))
        table = jnp.concatenate(tiles, axis=1)
        small[...] = table.astype(bf16)
        lane = lanes((1, tile))
        per = tile // rb
        pieces = []
        for t in range(32 // per):
            piece = jnp.zeros((1, tile), f32)
            for i in range(per):
                row = weights[t * per + i, 0:16, columns - tile :].astype(f32)[2:3]
                piece = jnp.where(lane // rb == i, pltpu.roll(row, (i * rb + tile - db) % tile, 1), piece)
            pieces.append(piece)
        gain_latent = jnp.concatenate(pieces, axis=1)
        gain_row[...] = gain_latent
        low = (unit * table[0:1]).astype(bf16)
        hidden[...] = low
        raw = nn(low, weights[:, :, :query].reshape(width, query))
        q_nope[...] = raw[:, : HEADS * NOPE].astype(bf16)
        front = raw[:, HEADS * NOPE : HEADS * NOPE + tile]
        back = raw[:, HEADS * NOPE + tile :]
        turned_front = front * cos[...] - back * sin[...]
        turned_back = back * cos[...] + front * sin[...]
        lane = lanes((rows, tile))
        for h in range(HEADS):
            head = jnp.where(
                lane < half,
                pltpu.roll(turned_front, (tile - h * half) % tile, 1),
                jnp.where(lane < ROPE, pltpu.roll(turned_back, (tile - h * half + half) % tile, 1), 0.0),
            )
            q_rope[h * rows : (h + 1) * rows] = head.astype(bf16)
        late = nn(low, weights[:, :, query:].reshape(width, R + tile))
        latent_out[...] = late
        plain = late[:, :R]
        inverse = lax.rsqrt(jnp.mean(plain * plain, axis=-1, keepdims=True) + epsilon)
        key = jnp.concatenate(
            [plain * inverse * gain_latent, turn(late[:, R:], cos[...], sin[...])], axis=1
        ).astype(bf16)
        for n in range(8):
            keys[n] = key

    return call(
        kernel,
        [
            ((rows, width), bf16, "v"),
            ((rows, HEADS * NOPE), bf16, "v"),
            ((HEADS * rows, tile), bf16, "v"),
            ((8, rows, R + tile), bf16, "v"),
            ((rows, R + tile), f32, "v"),
            ((16, width), bf16, "v"),
            ((1, R), f32, "v"),
        ],
        [(info, "s"), (tokens, "v"), (cos4, "v"), (sin4, "v")] + [(part, "a") for part in parts],
        [pltpu.VMEM((16, 2, db, columns), bf16), pltpu.SemaphoreType.DMA(())],
        macs=rows * width * columns,
        after=after,
    )


def turn(values, cosine, sine_part):
    width = values.shape[1]
    half = ROPE // 2
    lane = lanes(values.shape)
    swapped = jnp.where(lane < half, -pltpu.roll(values, width - half, 1), pltpu.roll(values, half, 1))
    return jnp.where(lane < ROPE, values * cosine + swapped * sine_part, 0.0)


def put_quarters(values, targets, z):
    quarter = values.shape[0] // 4
    for n in range(4):
        for k in range(4):

            @pl.when(z ^ k == n)
            def _(n=n, k=k):
                targets[k][0] = values[n * quarter : (n + 1) * quarter]


def visible(info, shape, row_count):
    place = lax.broadcasted_iota(jnp.int32, shape, 0) + info[1] * row_count
    key = lax.broadcasted_iota(jnp.int32, shape, 1)
    end0 = info[4]
    end1 = info[4] + info[5]
    row_doc = (place >= end0).astype(jnp.int32) + (place >= end1).astype(jnp.int32)
    key_doc = (key >= end0).astype(jnp.int32) + (key >= end1).astype(jnp.int32)
    return (row_doc == key_doc) & (key <= place)


def attend(info, q_nope, q_rope, key_parts, pack, after):
    rows = q_nope.shape[0]
    db = pack.shape[1]
    width = 32 * db
    tile = q_rope.shape[1]
    out = HEADS * VD
    keys = 16 * rows
    quarter = rows // 4
    rb = R // 32

    def kernel(info, qn, qr, *refs):
        key_ins, refs = refs[:2], refs[2:]
        pack_in, refs = refs[0], refs[1:]
        probs, cat, mixture, head_out, result, key_rows, weights, expand, sem = refs
        start_all(pair_copies(key_ins, info[1] % 2, key_rows), sem.at[0])
        start_all([(pack_in, weights)], sem.at[1])
        wait_for(weights, sem.at[1])
        for h in range(HEADS):
            expand[h] = weights[:, h * rb : (h + 1) * rb, out:].reshape(R, NOPE + VD)
        for h in range(HEADS):
            own = slice(h * rows, (h + 1) * rows)
            cat[own, :R] = nt(qn[:, h * NOPE : (h + 1) * NOPE], expand[h, :, :NOPE]).astype(bf16)
            cat[own, R:] = qr[own]
        wait_for(key_rows, sem.at[0])
        flat = key_rows[...].reshape(keys, R + tile)
        seen = visible(info, (rows, keys), rows)
        scale = (NOPE + ROPE) ** (-0.5)
        for h in range(HEADS):
            own = slice(h * rows, (h + 1) * rows)
            scores = jnp.where(seen, scale * nt(cat[own], flat), -1e30)
            weight = jnp.exp(scores - jnp.max(scores, axis=-1, keepdims=True))
            prob = (weight / jnp.sum(weight, axis=-1, keepdims=True)).astype(bf16)
            probs[own] = prob
            mixed = nn(prob, flat[:, :R]).astype(bf16)
            mixture[own] = mixed
            head_out[:, h * VD : (h + 1) * VD] = nn(mixed, expand[h, :, NOPE:]).astype(bf16)
        summed = nt(head_out[...], weights[:, :, :out].reshape(width, out)).astype(bf16)
        result[...] = summed.reshape(4, quarter, width)

    return call(
        kernel,
        [
            ((HEADS * rows, keys), bf16, "v"),
            ((HEADS * rows, R + tile), bf16, "v"),
            ((HEADS * rows, R), bf16, "v"),
            ((rows, out), bf16, "v"),
        ]
        + [((4, quarter, width), bf16, "v")],
        [(info, "s"), (q_nope, "v"), (q_rope, "v")]
        + [(part, "a") for part in key_parts + [pack]],
        [
            pltpu.VMEM((8, 2, rows, R + tile), bf16),
            pltpu.VMEM((32, db, out + NOPE + VD), bf16),
            pltpu.VMEM((HEADS, R, NOPE + VD), bf16),
            pltpu.SemaphoreType.DMA((2,)),
        ],
        macs=HEADS * rows * keys * (2 * R + tile) * 2,
        after=after,
    )


def quarter_norm(info, parts, tokens, small, after):
    _, quarter, width = parts.shape

    def kernel(info, came, tok, table, attention, normed):
        summed = came[0].astype(f32) + came[1].astype(f32) + came[2].astype(f32) + came[3].astype(f32)
        low = summed.astype(bf16)
        attention[0] = low
        middle = tok[info[3]].astype(f32) + low.astype(f32)
        inverse = lax.rsqrt(jnp.mean(middle * middle, axis=-1, keepdims=True) + epsilon)
        rows = (middle * inverse * table[1:2].astype(f32)).astype(bf16)
        for n in range(16):
            normed[n] = rows

    return call(
        kernel,
        [((1, quarter, width), bf16, "v"), ((16, quarter, width), bf16, "v")],
        [(info, "s"), (parts, "v"), (tokens.reshape(4, quarter, width), "v"), (small, "v")],
        [],
        after=after,
    )


def expert_copies(parts, me, targets):
    copies = []
    for ky, part in enumerate(parts):
        for i in range(8):
            for n, target in enumerate(targets):
                copies.append((part.at[i, n], target.at[me ^ mask(ky, i // 2, i % 2)]))
    return copies


def expert_rows(info, normed_parts, cots, weights, ff):
    _, quarter, width = normed_parts[0].shape
    extra = cots.shape[-1] - width
    db, wide = weights[0].shape[-2:]
    count = 32 * quarter
    step = count // 4
    lane0 = FF_PAD - extra

    def kernel(info, *refs):
        nref, refs = refs[:2], refs[2:]
        cref, wref, refs = refs[0], refs[1:5], refs[5:]
        act_out, gate_out, up_out, keep, send, x, g, wg, wu, wd, result, sem = refs
        start_all(expert_copies(wref, info[0], (wg, wu, wd)), sem.at[0])
        start_all([(cref.at[:, info[1] % 2], g.at[0]), (cref.at[:, 1 - info[1] % 2], g.at[1])], sem.at[1])
        start_all([(nref[0], x.at[0]), (nref[1], x.at[1])], sem.at[2])
        for ref in (wg, wu, wd):
            wait_for(ref, sem.at[0])
        wait_for(g, sem.at[1])
        wait_for(x, sem.at[2])
        tile_lane = lanes((step, extra))
        lane = lanes((step, wide))
        half = step // quarter

        def body(i, carry):
            own = pl.ds(pl.multiple_of(i * step, step), step)
            core, at = i // 2, (i % 2) * half
            rows = x[core, pl.ds(at, half)].reshape(step, width)
            cot = g[core, pl.ds(at // 4, half // 4)].reshape(step, width + extra)
            gate_weight = wg[...].reshape(width, wide)
            up_weight = wu[...].reshape(width, wide)
            down_weight = wd[...].reshape(width, wide)
            gate_pre = nn(rows, gate_weight)
            up_pre = nn(rows, up_weight)
            back = nn(cot[:, :width], down_weight)
            router = jax.nn.sigmoid(gate_pre[:, lane0:FF_PAD])
            weighted = router * cot[:, width:].astype(f32)
            gates = route_scale * weighted / jnp.sum(weighted, axis=1, keepdims=True)
            gate = jnp.sum(jnp.where(tile_lane == ff - lane0 + info[2], gates, 0.0), axis=1, keepdims=True)
            gate_row = jnp.where(lane < FF_PAD, gate, 1.0)
            sig = jax.nn.sigmoid(gate_pre)
            silu = gate_pre * sig
            act = silu * up_pre
            own_grad = jnp.sum(jnp.where(lane < FF_PAD, act * back, 0.0), axis=1, keepdims=True)
            act_low = (gate_row * act).astype(bf16)
            grad_act = gate_row * back
            grad_gate = (grad_act * up_pre * (sig * (1.0 + gate_pre * (1.0 - sig)))).astype(bf16)
            grad_up = (grad_act * silu).astype(bf16)
            act_out[own] = act_low
            gate_out[own] = grad_gate
            up_out[own] = grad_up
            result[own, :width] = nt(act_low, down_weight).astype(bf16)
            result[own, width : 2 * width] = (nt(grad_gate, gate_weight) + nt(grad_up, up_weight)).astype(bf16)
            high = own_grad.astype(bf16).astype(f32)
            result[own, 2 * width :] = (
                jnp.where(tile_lane == 8 + info[2], high, 0.0)
                + jnp.where(tile_lane == 24 + info[2], own_grad - high, 0.0)
            ).astype(bf16)
            return carry

        lax.fori_loop(0, 4, body, 0)
        for core, target in enumerate((keep, send)):
            pltpu.make_async_copy(result.at[pl.ds(core * count // 2, count // 2)], target, sem.at[3 + core]).start()
        for core, target in enumerate((keep, send)):
            wait_for(target, sem.at[3 + core])

    return call(
        kernel,
        [((count, wide), bf16, "v")] * 3
        + [((count // 2, 2 * width + extra), bf16, "a")] * 2,
        [(info, "s")] + [(part, "a") for part in normed_parts + [cots] + weights],
        [
            pltpu.VMEM((2, 16, quarter, width), bf16),
            pltpu.VMEM((2, 4, 4, quarter, width + extra), bf16),
            pltpu.VMEM((32, db, wide), bf16),
            pltpu.VMEM((32, db, wide), bf16),
            pltpu.VMEM((32, db, wide), bf16),
            pltpu.VMEM((count, 2 * width + extra), bf16),
            pltpu.SemaphoreType.DMA((5,)),
        ],
        macs=6 * count * width * wide,
    )


def expert_weights(info, normed_parts, cots, act, grad_gate, grad_up, after):
    _, quarter, width = normed_parts[0].shape
    extra = cots.shape[-1] - width
    count, wide = act.shape
    db = width // 32
    step = width // 8
    blocks = step // db

    def kernel(info, *refs):
        nref, refs = refs[:2], refs[2:]
        cref, refs = refs[0], refs[1:]
        a, gg, gu, *results, x, g, grads, sem = refs
        start_all([(cref.at[:, info[1] % 2], g.at[0]), (cref.at[:, 1 - info[1] % 2], g.at[1])], sem.at[0])
        start_all([(nref[0], x.at[0]), (nref[1], x.at[1])], sem.at[1])
        wait_for(g, sem.at[0])
        wait_for(x, sem.at[1])

        def body(i, carry):
            cols = pl.ds(pl.multiple_of(i * step, step), step)
            rows = x[:, :, :, cols].reshape(count, step)
            cot = g[:, :, :, :, cols].reshape(count, step)
            own = pl.ds(i * blocks, blocks)
            grads[own, 0] = tn(rows, gg[...]).astype(bf16).reshape(blocks, db, wide)
            grads[own, 1] = tn(rows, gu[...]).astype(bf16).reshape(blocks, db, wide)
            grads[own, 2] = tn(cot, a[...]).astype(bf16).reshape(blocks, db, wide)
            return carry

        lax.fori_loop(0, 8, body, 0)
        for ky in range(4):
            for kx in range(4):
                for kc in (0, 1):
                    pltpu.make_async_copy(
                        grads.at[info[0] ^ mask(ky, kx, kc)], results[ky].at[kx, kc], sem.at[2]
                    ).start()
        for result in results:
            wait_for(result, sem.at[2])

    return call(
        kernel,
        [((4, 2, 3, db, wide), bf16, "a")] * 4,
        [(info, "s")]
        + [(part, "a") for part in normed_parts + [cots]]
        + [(act, "v"), (grad_gate, "v"), (grad_up, "v")],
        [
            pltpu.VMEM((2, 16, quarter, width), bf16),
            pltpu.VMEM((2, 4, 4, quarter, width + extra), bf16),
            pltpu.VMEM((32, 3, db, wide), bf16),
            pltpu.SemaphoreType.DMA((3,)),
        ],
        macs=3 * count * width * wide,
        after=after,
    )


def quarter_copies(parts, z, target, columns=None):
    if columns is None:
        return [(part.at[0], target.at[z ^ k]) for k, part in enumerate(parts)]
    return [(part.at[0, :, columns], target.at[z ^ k]) for k, part in enumerate(parts)]


def attend_back(
    info, tokens, cotangent, picked, att_parts, grad_parts, small, head_out, mixture, probs, cat, q_nope, hidden,
    key_parts, pack2, parts1, cos4, sin4, after,
):
    rows, width = tokens.shape
    quarter = rows // 4
    db = width // 32
    rb = R // 32
    tile = cat.shape[1] - R
    out = HEADS * VD
    keys = 16 * rows
    query = HEADS * (NOPE + ROPE)
    half = ROPE // 2
    extra = grad_parts[0].shape[-1] - 2 * width
    scale = (NOPE + ROPE) ** (-0.5)
    late = out + NOPE + VD

    def kernel(info, tok, cotan, pick, table, ho, mix, pr, ca, qn, hid, cos, sin, *refs):
        att_in, refs = refs[:4], refs[4:]
        grad_in, refs = refs[:4], refs[4:]
        key_in, refs = refs[:2], refs[2:]
        in2, refs = refs[0], refs[1:]
        in1, refs = refs[: len(parts1)], refs[len(parts1) :]
        (
            grad_middle, small_grads, key_keep, key_send, hid0, hid1, hid2, hid3, keep, send,
            att, arrived, key_rows, w2, w1, expand, grad_mix, grad_scores, key_grads, weight_grads, grad_q, sem,
        ) = refs
        start_all(quarter_copies(grad_in, info[3], arrived, pl.ds(width, width + extra)), sem.at[0])
        start_all(quarter_copies(att_in, info[3], att), sem.at[1])
        start_all([(in2, w2)], sem.at[2])
        start_all(pair_copies(key_in, info[1] % 2, key_rows), sem.at[3])
        columns = pl.ds(0, query)
        start_all(pair_copies([one.at[:, :, columns] for one in in1], info[1] % 2, w1), sem.at[4])
        wait_for(arrived, sem.at[0])
        wait_for(att, sem.at[1])
        middle = tok[...].astype(f32) + att[...].reshape(rows, width).astype(f32)
        inverse = lax.rsqrt(jnp.mean(middle * middle, axis=-1, keepdims=True) + epsilon)
        unit = middle * inverse
        gain = table[1:2].astype(f32)
        normed = (unit * gain).astype(bf16)
        came = arrived[...].reshape(rows, width + extra)
        sig = jax.nn.sigmoid(nt(normed, table[...]))
        chosen = pick[...]
        weighted = sig * chosen
        gate_total = jnp.sum(weighted, axis=1, keepdims=True)
        gates = route_scale * weighted / gate_total
        grad_gates = came[:, width : width + 16].astype(f32) + came[:, width + 16 : width + 32].astype(f32)
        grad_weighted = (route_scale * grad_gates - jnp.sum(grad_gates * gates, axis=1, keepdims=True)) / gate_total
        grad_logits = grad_weighted * chosen * sig * (1.0 - sig)
        high, low = high_low(grad_logits)
        grads = tn(high, normed) + tn(low, normed)
        grad_normed = came[:, :width].astype(f32) + nn(high, table[...]) + nn(low, table[...])
        scaled = grad_normed * gain
        grad_mid = cotan[...].astype(f32) + inverse * (
            scaled - unit * jnp.mean(scaled * unit, axis=-1, keepdims=True)
        )
        d_gain = jnp.sum(grad_normed * unit, axis=0, keepdims=True)
        row16 = lax.broadcasted_iota(jnp.int32, (16, width), 0)
        small_grads[...] = jnp.where(row16 >= 8, grads, jnp.where(row16 == 1, d_gain, 0.0))
        grad_middle[...] = grad_mid
        grad_att = grad_mid.astype(bf16)
        wait_for(w2, sem.at[2])
        for h in range(HEADS):
            expand[h] = w2[:, h * rb : (h + 1) * rb, out:].reshape(R, NOPE + VD)
        grad_heads = nn(grad_att, w2[:, :, :out].reshape(width, out)).astype(bf16)
        weight_grads[:, :, :, :out] = tn(grad_att, ho[...]).astype(bf16).reshape(16, 2, db, out)
        for h in range(HEADS):
            own = slice(h * rows, (h + 1) * rows)
            mine = grad_heads[:, h * VD : (h + 1) * VD]
            weight_grads[:, :, h * rb : (h + 1) * rb, out + NOPE : late] = (
                tn(mix[own], mine).astype(bf16).reshape(16, 2, rb, VD)
            )
            grad_mix[own] = nt(mine, expand[h, :, NOPE:]).astype(bf16)
        wait_for(key_rows, sem.at[3])
        flat = key_rows[...].reshape(keys, R + tile)
        lane = lanes((rows, tile))
        front = jnp.zeros((rows, tile), f32)
        back = jnp.zeros((rows, tile), f32)
        for h in range(HEADS):
            own = slice(h * rows, (h + 1) * rows)
            grad_prob = nt(grad_mix[own], flat[:, :R])
            prob = pr[own].astype(f32)
            inner = jnp.sum(prob * grad_prob, axis=-1, keepdims=True)
            grad_score = (prob * (grad_prob - inner)).astype(bf16)
            grad_scores[own] = grad_score
            grad_cat = scale * nn(grad_score, flat)
            grad_abs = grad_cat[:, :R].astype(bf16)
            weight_grads[:, :, h * rb : (h + 1) * rb, out : out + NOPE] = (
                tn(grad_abs, qn[:, h * NOPE : (h + 1) * NOPE]).astype(bf16).reshape(16, 2, rb, NOPE)
            )
            grad_q[:, h * NOPE : (h + 1) * NOPE] = nn(grad_abs, expand[h, :, :NOPE]).astype(bf16)
            turned = grad_cat[:, R:]
            inside = (lane >= h * half) & (lane < (h + 1) * half)
            front = jnp.where(inside, pltpu.roll(turned, (h * half) % tile, 1), front)
            back = jnp.where(inside, pltpu.roll(turned, (h * half + tile - half) % tile, 1), back)
        grad_q[:, HEADS * NOPE : HEADS * NOPE + tile] = (front * cos[...] + back * sin[...]).astype(bf16)
        grad_q[:, HEADS * NOPE + tile :] = (back * cos[...] - front * sin[...]).astype(bf16)
        chunk = keys // 4
        for n in range(4):
            cols = slice(n * chunk, (n + 1) * chunk)
            part = scale * tn(grad_scores[:, cols], ca[...])
            latent = part[:, :R] + tn(pr[:, cols], grad_mix[...])
            own = slice(n * 2, (n + 1) * 2)
            key_grads[own, :, :, :R] = latent.astype(bf16).reshape(2, 2, rows, R)
            key_grads[own, :, :, R:] = part[:, R:].astype(bf16).reshape(2, 2, rows, tile)
        core = info[1] % 2
        pltpu.make_async_copy(key_grads.at[:, core], key_keep, sem.at[5]).start()
        pltpu.make_async_copy(key_grads.at[:, 1 - core], key_send, sem.at[6]).start()
        wait_for(w1, sem.at[4])
        wq = w1[...].reshape(width, query)
        summed = nt(grad_q[...], wq).astype(bf16)
        put_quarters(summed, (hid0, hid1, hid2, hid3), info[3])
        weight_grads[:, :, :, late:] = tn(hid[...], grad_q[...]).astype(bf16).reshape(16, 2, db, query)
        pltpu.make_async_copy(weight_grads.at[:, core], keep, sem.at[7]).start()
        pltpu.make_async_copy(weight_grads.at[:, 1 - core], send, sem.at[8]).start()
        for n, ref in enumerate((key_keep, key_send, keep, send)):
            wait_for(ref, sem.at[5 + n])

    vmem_ins = [tokens, cotangent, picked, small, head_out, mixture, probs, cat, q_nope, hidden, cos4, sin4]
    return call(
        kernel,
        [
            ((rows, width), f32, "v"),
            ((16, width), f32, "v"),
            ((8, rows, R + tile), bf16, "a"),
            ((8, rows, R + tile), bf16, "a"),
            ((1, quarter, width), bf16, "v"),
            ((1, quarter, width), bf16, "v"),
            ((1, quarter, width), bf16, "v"),
            ((1, quarter, width), bf16, "v"),
            ((16, db, late + query), bf16, "a"),
            ((16, db, late + query), bf16, "a"),
        ],
        [(info, "s")]
        + [(array, "v") for array in vmem_ins]
        + [(part, "a") for part in att_parts + grad_parts + key_parts + [pack2] + parts1],
        [
            pltpu.VMEM((4, quarter, width), bf16),
            pltpu.VMEM((4, quarter, width + extra), bf16),
            pltpu.VMEM((8, 2, rows, R + tile), bf16),
            pltpu.VMEM((32, db, late), bf16),
            pltpu.VMEM((16, 2, db, query), bf16),
            pltpu.VMEM((HEADS, R, NOPE + VD), bf16),
            pltpu.VMEM((HEADS * rows, R), bf16),
            pltpu.VMEM((HEADS * rows, keys), bf16),
            pltpu.VMEM((8, 2, rows, R + tile), bf16),
            pltpu.VMEM((16, 2, db, late + query), bf16),
            pltpu.VMEM((rows, query), bf16),
            pltpu.SemaphoreType.DMA((9,)),
        ],
        macs=HEADS * rows * keys * (4 * R + 2 * tile) * 2,
        after=after,
    )


def finish(
    info, tokens, grad_middle, hidden, latent, gain_latent, small, small_grads, key_parts, hidden_parts, att_parts,
    sum_parts, parts1, cos4, sin4, after,
):
    rows, width = tokens.shape
    quarter = rows // 4
    db = width // 32
    rb = R // 32
    tile = latent.shape[1] - R
    query = HEADS * (NOPE + ROPE)

    def kernel(info, tok, gm, hid, lat, gl, table, sg, cos, sin, *refs):
        key_in, refs = refs[:4], refs[4:]
        hid_in, refs = refs[:4], refs[4:]
        att_in, refs = refs[:4], refs[4:]
        sum_in, refs = refs[:4], refs[4:]
        in1, refs = refs[: len(parts1)], refs[len(parts1) :]
        output, d_tokens, keep, send, own_keys, part, att, sums, w1, grads, sem = refs
        start_all(quarter_copies(key_in, info[3], own_keys), sem.at[6])
        start_all(pair_copies(in1, info[1] % 2, w1, pl.ds(query, R + tile)), sem.at[0])
        start_all(quarter_copies(hid_in, info[3], part), sem.at[1])
        start_all(quarter_copies(att_in, info[3], att), sem.at[2])
        start_all(quarter_copies(sum_in, info[3], sums, pl.ds(0, width)), sem.at[3])
        wait_for(own_keys, sem.at[6])
        own = own_keys[...].reshape(rows, R + tile)
        plain = lat[:, :R]
        inverse = lax.rsqrt(jnp.mean(plain * plain, axis=-1, keepdims=True) + epsilon)
        unit = plain * inverse
        grad_y = own[:, :R]
        scaled = grad_y * gl[...]
        d_gain_latent = jnp.sum(grad_y * unit, axis=0, keepdims=True)
        grad_in = inverse * (scaled - unit * jnp.mean(scaled * unit, axis=-1, keepdims=True))
        grad_latent = jnp.concatenate([grad_in, turn(own[:, R:], cos[...], -sin[...])], axis=1).astype(bf16)
        d_latent = tn(hid[...], grad_latent).astype(bf16)
        grads[...] = d_latent.reshape(16, 2, db, R + tile)
        wait_for(w1, sem.at[0])
        wait_for(part, sem.at[1])
        x = tok[...].astype(f32)
        inverse = lax.rsqrt(jnp.mean(x * x, axis=-1, keepdims=True) + epsilon)
        unit = x * inverse
        grad_hidden = part[...].reshape(rows, width).astype(f32) + nt(
            grad_latent, w1[...].reshape(width, R + tile)
        )
        scaled = grad_hidden * table[0:1].astype(f32)
        d_tokens[...] = gm[...] + inverse * (scaled - unit * jnp.mean(scaled * unit, axis=-1, keepdims=True))
        d_gain = jnp.sum(grad_hidden * unit, axis=0, keepdims=True)
        row16 = lax.broadcasted_iota(jnp.int32, (16, width), 0)
        every = jnp.where(row16 == 0, d_gain, sg[...])
        lane = lanes((16, tile))
        row = lax.broadcasted_iota(jnp.int32, (16, tile), 0)
        per = tile // rb
        for j in range(32):
            t = j // 2
            values = every[:, t * tile : (t + 1) * tile]
            if j % 2 == 0:
                values = pltpu.roll(values, db, 1)
            gains = d_gain_latent[:, (j // per) * tile : (j // per + 1) * tile]
            gains = pltpu.roll(gains, (db + tile - (j % per) * rb) % tile, 1)
            values = jnp.where(row == 2, jnp.where(lane < db + rb, gains, 0.0), values)
            before = grads[j // 2, j % 2, 0:16, R:].astype(f32)
            grads[j // 2, j % 2, 0:16, R:] = jnp.where(lane < db, before, values).astype(bf16)
        core = info[1] % 2
        pltpu.make_async_copy(grads.at[:, core], keep, sem.at[4]).start()
        pltpu.make_async_copy(grads.at[:, 1 - core], send, sem.at[5]).start()
        wait_for(att, sem.at[2])
        wait_for(sums, sem.at[3])
        middle = x + att[...].reshape(rows, width).astype(f32)
        output[...] = (middle + sums[...].reshape(rows, width).astype(f32)).astype(bf16)
        wait_for(keep, sem.at[4])
        wait_for(send, sem.at[5])

    vmem_ins = [tokens, grad_middle, hidden, latent, gain_latent, small, small_grads, cos4, sin4]
    return call(
        kernel,
        [
            ((rows, width), bf16, "v"),
            ((rows, width), f32, "v"),
            ((16, db, R + tile), bf16, "a"),
            ((16, db, R + tile), bf16, "a"),
        ],
        [(info, "s")]
        + [(array, "v") for array in vmem_ins]
        + [(part, "a") for part in key_parts + hidden_parts + att_parts + sum_parts + parts1],
        [
            pltpu.VMEM((4, quarter, R + tile), f32),
            pltpu.VMEM((4, quarter, width), bf16),
            pltpu.VMEM((4, quarter, width), bf16),
            pltpu.VMEM((4, quarter, width), bf16),
            pltpu.VMEM((16, 2, db, R + tile), bf16),
            pltpu.VMEM((16, 2, db, R + tile), bf16),
            pltpu.SemaphoreType.DMA((7,)),
        ],
        macs=4 * rows * width * (R + tile),
        after=after,
    )


def unpack_experts(info, own, other, ff, sh):
    _, _, db, wide = other.shape

    def kernel(info, a0, a1, a2, a3, b, gate, up, down, sg, su, sd, slots, sem):
        for kx, a in enumerate((a0, a1, a2, a3)):
            pltpu.make_async_copy(a.at[0], slots.at[info[2] ^ (kx * 2)], sem).start()
            pltpu.make_async_copy(b.at[kx], slots.at[info[2] ^ (kx * 2 + 1)], sem).start()
        wait_for(slots, sem)
        for n, (routed, shared) in enumerate(((gate, sg), (up, su), (down, sd))):
            for e in range(8):
                routed[e] = slots[e, n, :, :ff].astype(f32)
            shared[...] = jnp.concatenate(
                [slots[e, n, :, FF_PAD : FF_PAD + sh].astype(f32) for e in range(8)], axis=1
            )

    return call(
        kernel,
        [((8, db, ff), f32, "v")] * 3 + [((db, 8 * sh), f32, "v")] * 3,
        [(info, "s")] + [(part, "a") for part in own] + [(other, "a")],
        [pltpu.VMEM((8, 3, db, wide), bf16), pltpu.SemaphoreType.DMA(())],
    )


def unpack_attention(grads):
    db, _ = grads.shape
    rb = R // 32
    out = HEADS * VD
    late = out + NOPE + VD
    per_head, half = NOPE + ROPE, ROPE // 2

    def kernel(g, d_out, d_expand, d_query):
        d_out[...] = g[:, :out].astype(f32)
        for h in range(HEADS):
            d_expand[:, h * (NOPE + VD) : (h + 1) * (NOPE + VD)] = g[h * rb : (h + 1) * rb, out:late].astype(f32)
            plain = g[:, late + h * NOPE : late + (h + 1) * NOPE].astype(f32)
            front = late + HEADS * NOPE + h * half
            back = front + HEADS * half
            d_query[:, h * per_head : (h + 1) * per_head] = jnp.concatenate(
                [plain, g[:, front : front + half].astype(f32), g[:, back : back + half].astype(f32)], axis=1
            )

    return call(
        kernel,
        [
            ((db, out), f32, "v"),
            ((rb, HEADS * (NOPE + VD)), f32, "v"),
            ((db, HEADS * per_head), f32, "v"),
        ],
        [(grads, "v")],
        [],
    )


def shards(
    tokens,
    lengths,
    routes,
    cotangent,
    attn_gain,
    w_query,
    w_latent,
    latent_gain,
    w_expand,
    w_out,
    moe_gain,
    w_router,
    w_gate,
    w_up,
    w_down,
    shared_gate,
    shared_up,
    shared_down,
):
    me = lax.axis_index(PLANE)
    place = me % 16
    member = me % 8
    z = lax.axis_index("z")
    rows, width = tokens.shape
    quarter = rows // 4
    db = width // 32
    rb = R // 32
    ff, sh = w_gate.shape[2], shared_gate.shape[1] // 8
    tile = ROPE + db
    query = HEADS * (NOPE + ROPE)
    half = ROPE // 2
    extra = min(128, FF_PAD)
    wide = FF_PAD + SH_PAD
    info = jnp.concatenate([jnp.stack([me, place, member, z]).astype(jnp.int32), lengths[0]])

    one, two = pack_attention(
        w_query, w_latent, attn_gain, moe_gain, latent_gain, w_router.T, w_out.T, w_expand
    )
    pack2 = lax.all_gather(two, PLANE, axis=0)
    keep, send = pack_experts(
        info, w_gate, w_up, jnp.swapaxes(w_down, 1, 2), shared_gate, shared_up, shared_down.T, w_router
    )
    came = swap(send, kc=1)
    by_x = [jnp.stack([keep[k], came[k]]) for k in range(4)]
    parts1 = gather(one, ("yl", "yh", "x"), by_x)
    by_x = [by_x[0]] + [swap(hold(by_x[k], parts1[0]), kx=k) for k in (1, 2, 3)]
    mine = jnp.concatenate(by_x)
    weights = [mine] + [swap(mine, ky=k) for k in (1, 2, 3)]

    position = place * rows + jnp.arange(rows, dtype=jnp.int32)
    ends = jnp.stack([lengths[0, 0], lengths[0, 0] + lengths[0, 1]])
    start = jnp.where(position >= ends[1], ends[1], jnp.where(position >= ends[0], ends[0], 0))
    frequency = rope_base ** (-jnp.arange(half, dtype=f32) / half)
    angles = (position - start).astype(f32)[:, None] * jnp.tile(frequency, 2 * HEADS * half // ROPE)[None, :]
    cos4, sin4 = jnp.cos(angles), jnp.sin(angles)
    picked = jnp.sum(
        (routes[:, :, None] == jnp.arange(16, dtype=jnp.int32)[None, None, :] - 8).astype(f32), axis=1
    )
    lane_pick = jnp.sum(
        (routes[:, :, None] == jnp.arange(extra, dtype=jnp.int32)[None, None, :] - (ff - FF_PAD + extra)), axis=1
    ).astype(bf16)

    hidden, q_nope, q_rope, keys, latent, small, gain_latent = project(info, tokens, cos4, sin4, parts1, ())
    key_parts = gather(keys, ("yh", "x"), (mine,))
    cots = tie(jnp.concatenate([cotangent, lane_pick], axis=1), key_parts[0])
    cots = lax.all_gather(cots, ("x", "c"), axis=0).reshape(4, 2, 4, quarter, width + extra)
    probs, cat, mixture, head_out, attention = attend(info, q_nope, q_rope, key_parts, pack2, ())
    attention = hold(exchange(attention, "z"), weights[1], weights[3])
    own_attention, normed = quarter_norm(info, attention, tokens, small, ())
    normed_parts = gather(normed, ("x", "z"), (weights[2],))
    att_parts = [own_attention] + [swap_z(own_attention, k) for k in (1, 2, 3)]

    act, grad_gate, grad_up, keep, send = expert_rows(
        info, normed_parts, cots, weights, ff
    )
    def collect(values):
        return jnp.sum(values.astype(f32), axis=0, keepdims=True).astype(bf16)

    both = total([keep, swap(send, kc=1)])
    d_experts = expert_weights(info, normed_parts, cots, act, grad_gate, grad_up, (both,))
    both = collect(hold(exchange(both.reshape(16, quarter, -1), ("x", "z")), d_experts[0]))
    d_from_y = [swap(d_experts[k], ky=k) for k in (1, 2, 3)]
    sum_parts = [both] + [swap_z(both, k) for k in (1, 2, 3)]

    grad_middle, small_grads, key_keep, key_send, *hidden_part, keep, send = attend_back(
        info, tokens, cotangent, picked, att_parts, sum_parts, small, head_out, mixture, probs, cat, q_nope,
        hidden, key_parts, pack2, parts1, cos4, sin4, (d_from_y[0], d_from_y[2]),
    )
    key_send = hold(key_send, d_from_y[1])
    grad_keys = total([key_keep, swap(key_send, kc=1)]).reshape(32, quarter, R + tile)
    send = hold(send, grad_keys)
    most = total([keep, swap(send, kc=1)])
    most = lax.psum_scatter(most, ("yl", "yh", "x"), scatter_dimension=0)
    grad_keys = exchange(grad_keys, ("yh", "x", "z"))
    grad_hidden = total([hidden_part[0]] + [swap_z(hidden_part[k], k) for k in (1, 2, 3)])
    hidden_parts = [grad_hidden] + [swap_z(grad_hidden, k) for k in (1, 2, 3)]
    grad_keys = jnp.sum(grad_keys.astype(f32), axis=0, keepdims=True)
    grad_key_parts = [grad_keys] + [swap_z(grad_keys, k) for k in (1, 2, 3)]
    d_mine = [total([part[k] for part in [d_experts[0]] + d_from_y]) for k in range(4)]
    d_mine = [d_mine[0]] + [swap(hold(d_mine[k], grad_keys), kx=k) for k in (1, 2, 3)]

    output, d_tokens, keep, send = finish(
        info, tokens, grad_middle, hidden, latent, gain_latent, small, small_grads, grad_key_parts, hidden_parts,
        att_parts, sum_parts, parts1, cos4, sin4, (),
    )
    rest = total([keep, swap(send, kc=1)])
    rest = lax.all_to_all(rest, ("yl", "yh", "x"), 0, 0, tiled=True)
    d_other = swap(jnp.stack([part[1] for part in d_mine]), kc=1)
    d_routed = unpack_experts(info, d_mine, d_other, ff, sh)
    d_out, d_expand, d_query = unpack_attention(most)
    rest = jnp.sum(rest.astype(f32), axis=0)

    aux = rest[:16, R + ROPE :]
    return (
        output,
        d_tokens,
        aux[0],
        d_query,
        rest[:, : R + ROPE],
        aux[2, :rb],
        d_expand,
        d_out.T,
        aux[1],
        aux[8:16].T,
        d_routed[0],
        d_routed[1],
        jnp.swapaxes(d_routed[2], 1, 2),
        d_routed[3],
        d_routed[4],
        d_routed[5].T,
    )


def solution(mesh):
    rows = P(PLANE, None)
    split = P(PLANE, "z")
    vector = P(PLANE)
    turned = P("z", PLANE)
    expert_rows = P(None, PLANE, "z")
    expert_columns = P(None, "z", PLANE)
    fine = Mesh(mesh.devices.reshape(2, 2, 4, 2, 4), ("yl", "yh", "x", "c", "z"))
    return jax.shard_map(
        shards,
        mesh=fine,
        in_specs=(
            rows,
            P("yl", None),
            rows,
            rows,
            vector,
            split,
            rows,
            vector,
            split,
            turned,
            vector,
            rows,
            expert_rows,
            expert_rows,
            expert_columns,
            split,
            split,
            turned,
        ),
        out_specs=(
            rows,
            rows,
            vector,
            split,
            rows,
            vector,
            split,
            turned,
            vector,
            rows,
            expert_rows,
            expert_rows,
            expert_columns,
            split,
            split,
            turned,
        ),
        check_vma=False,
    )
```

```python
import math

import jax
import jax.numpy as jnp
from jax import lax
from jax.experimental import pallas as pl
from jax.experimental.pallas import tpu as pltpu
from jax.sharding import Mesh
from jax.sharding import PartitionSpec as P

NOPE = 128
ROPE = 64
VD = 128
R = 512
E = 8
FF_PAD = 384
SH_PAD = 128
HEADS = 4

epsilon = 1e-06
rope_base = 50000.0
route_scale = 2.446
bf16 = jnp.bfloat16
f32 = jnp.float32

PLANE = ("yl", "yh", "x", "c")
YS = ("yl", "yh")


def mask(ky=0, kx=0, kc=0):
    return (ky & 1) * 16 + (ky >> 1) * 8 + kx * 2 + kc


def swap(values, ky=0, kx=0, kc=0):
    bits = mask(ky, kx, kc)
    return lax.ppermute(values, PLANE, [(i, i ^ bits) for i in range(32)])


def swap_z(values, k):
    return lax.ppermute(values, "z", [(i, i ^ k) for i in range(4)])


def total(parts, dtype=bf16):
    out = parts[0].astype(f32)
    for part in parts[1:]:
        out = out + part.astype(f32)
    return out.astype(dtype)


def nn(left, right):
    return jnp.dot(left, right, preferred_element_type=f32)


def nt(left, right):
    return lax.dot_general(left, right, (((1,), (1,)), ((), ())), preferred_element_type=f32)


def tn(left, right):
    return lax.dot_general(left, right, (((0,), (0,)), ((), ())), preferred_element_type=f32)


def lanes(shape):
    return lax.broadcasted_iota(jnp.int32, shape, 1)


def high_low(values):
    high = values.astype(bf16)
    return high, (values - high.astype(f32)).astype(bf16)


def start_all(copies, sem):
    for source, destination in copies:
        pltpu.make_async_copy(source, destination, sem).start()


def wait_for(ref, sem):
    pltpu.make_async_copy(ref, ref, sem).wait()


def call(kernel, outs, ins, scratch, macs=0, vmem=60, after=()):
    count, late = len(ins), len(after)
    body = kernel
    if late:

        def body(*refs):
            kernel(*refs[:count], *refs[count + late :])

    moved = sum(array.size * array.dtype.itemsize for array, _ in ins)
    moved += sum(math.prod(shape) * jnp.dtype(dtype).itemsize for shape, dtype, _ in outs)
    spaces = {"s": pltpu.SMEM, "v": pltpu.VMEM, "a": pl.ANY}
    return pl.pallas_call(
        body,
        out_shape=[jax.ShapeDtypeStruct(shape, dtype) for shape, dtype, _ in outs],
        in_specs=[pl.BlockSpec(memory_space=spaces[space]) for _, space in ins]
        + [pl.BlockSpec(memory_space=pl.ANY)] * late,
        out_specs=[pl.BlockSpec(memory_space=spaces[space]) for _, _, space in outs],
        scratch_shapes=scratch,
        compiler_params=pltpu.CompilerParams(vmem_limit_bytes=vmem << 20),
        cost_estimate=pl.CostEstimate(flops=4 * macs, bytes_accessed=moved, transcendentals=0),
    )(*[array for array, _ in ins], *after)


def exchange(blocks, axes):
    return lax.all_to_all(blocks, axes, 0, 0, tiled=True)


def gather(copies, axes, after):
    own = hold(exchange(copies, axes), *after)
    return [own, swap(own, kc=1)]


def pair_copies(parts, core, target, columns=None):
    if columns is not None:
        parts = [part.at[:, :, columns] for part in parts]
    return [(parts[0], target.at[:, core]), (parts[1], target.at[:, 1 - core])]


def pack_copies(pack, columns, target):
    return [
        (pack.at[yh, yl, :, :, columns], target.at[pl.ds(yl * 16 + yh * 8, 8)]) for yh in (0, 1) for yl in (0, 1)
    ]


def hold(values, *after):
    def kernel(*refs):
        pass

    return pl.pallas_call(
        kernel,
        out_shape=jax.ShapeDtypeStruct(values.shape, values.dtype),
        in_specs=[pl.BlockSpec(memory_space=pl.ANY)] * (1 + len(after)),
        out_specs=pl.BlockSpec(memory_space=pl.ANY),
        input_output_aliases={0: 0},
    )(values, *after)


def tie(values, *after):
    late = sum(jnp.abs(lax.slice(one, (0,) * one.ndim, (1,) * one.ndim).reshape(()).astype(f32)) for one in after)
    return values + jnp.where(late > 3e38, 1.0, 0.0).astype(values.dtype)


def pack_attention(w_query, w_latent, attn_gain, moe_gain, latent_gain, router_t, out_t, w_expand):
    db = w_query.shape[0]
    query = w_query.shape[1]
    late = w_latent.shape[1]
    out = out_t.shape[1]
    per_head = NOPE + ROPE

    def kernel(q, lat, ag, mg, lg, rt, ot, ex, first, second):
        plain = [q[:, h * per_head : h * per_head + NOPE] for h in range(HEADS)]
        front = [q[:, h * per_head + NOPE : h * per_head + NOPE + ROPE // 2] for h in range(HEADS)]
        back = [q[:, h * per_head + NOPE + ROPE // 2 : (h + 1) * per_head] for h in range(HEADS)]
        rb = lg.shape[1]
        small = jnp.concatenate(
            [
                ag[...].astype(f32),
                mg[...].astype(f32),
                jnp.concatenate([lg[...].astype(f32), jnp.zeros((1, db - rb), f32)], axis=1),
                jnp.zeros((5, db), f32),
                rt[...].astype(f32),
            ]
            + ([jnp.zeros((db - 16, db), f32)] if db > 16 else []),
            axis=0,
        ).astype(bf16)
        one = jnp.concatenate([lat[...], small], axis=1)
        for n in range(16):
            first[n] = one
        width = ex.shape[1] // HEADS
        expand = jnp.concatenate([ex[:, h * width : (h + 1) * width] for h in range(HEADS)], axis=0)
        second[...] = jnp.concatenate(plain + front + back + [ot[...], expand], axis=1)

    two = query + out + w_expand.shape[1] // HEADS
    ins = [w_query, w_latent, attn_gain[None], moe_gain[None], latent_gain[None], router_t, out_t, w_expand]
    return call(
        kernel,
        [((16, db, late + db), bf16, "v"), ((db, two), bf16, "v")],
        [(array, "v") for array in ins],
        [],
    )


def pack_experts(info, gate, up, down_t, shared_gate, shared_up, shared_down_t, router):
    count, db, ff = gate.shape
    sh = shared_gate.shape[1] // count
    wide = FF_PAD + SH_PAD

    def kernel(info, g, u, d, sg, su, sd, rt, keep, send, packed, sem):
        fill = FF_PAD - ff - count
        for n, (routed, shared) in enumerate(((g, sg), (u, su), (d, sd))):
            extra = rt[...] if n == 0 else jnp.zeros((db, count), bf16)
            for e in range(count):
                packed[e, n] = jnp.concatenate(
                    [
                        routed[e],
                        extra,
                        jnp.zeros((db, fill), bf16),
                        shared[:, e * sh : (e + 1) * sh],
                        jnp.zeros((db, SH_PAD - sh), bf16),
                    ],
                    axis=1,
                )
        copies = []
        for kx in range(4):
            copies.append((packed.at[info[2] ^ (kx * 2)], keep.at[kx], sem.at[0]))
            copies.append((packed.at[info[2] ^ (kx * 2 + 1)], send.at[kx], sem.at[1]))
        for source, destination, which in copies:
            pltpu.make_async_copy(source, destination, which).start()
        wait_for(keep, sem.at[0])
        wait_for(send, sem.at[1])

    ins = [gate, up, down_t, shared_gate, shared_up, shared_down_t, router]
    return call(
        kernel,
        [((4, 3, db, wide), bf16, "a")] * 2,
        [(info, "s")] + [(array, "v") for array in ins],
        [pltpu.VMEM((count, 3, db, wide), bf16), pltpu.SemaphoreType.DMA((2,))],
    )


def project_latent(info, tokens, cos4, sin4, parts):
    rows, width = tokens.shape
    db = width // 32
    rb = R // 32
    tile = ROPE + db

    def kernel(info, tok, cos, sin, own, other, hidden, keys, latent_out, small, gain_row, pairs, sem):
        start_all(pair_copies((own, other), info[1] % 2, pairs), sem)
        x = tok[...].astype(f32)
        inverse = lax.rsqrt(jnp.mean(x * x, axis=-1, keepdims=True) + epsilon)
        unit = x * inverse
        wait_for(pairs, sem)
        weights = pairs.reshape(32, db, R + tile)
        lane = lanes((16, tile))
        tiles = []
        for t in range(16):
            even = weights[2 * t, 0:16, R:].astype(f32)
            odd = weights[2 * t + 1, 0:16, R:].astype(f32)
            tiles.append(jnp.where(lane < db, pltpu.roll(even, tile - db, 1), odd))
        table = jnp.concatenate(tiles, axis=1)
        small[...] = table.astype(bf16)
        lane = lanes((1, tile))
        per = tile // rb
        pieces = []
        for t in range(32 // per):
            piece = jnp.zeros((1, tile), f32)
            for i in range(per):
                row = weights[t * per + i, 0:16, R:].astype(f32)[2:3]
                piece = jnp.where(lane // rb == i, pltpu.roll(row, (i * rb + tile - db) % tile, 1), piece)
            pieces.append(piece)
        gain_latent = jnp.concatenate(pieces, axis=1)
        gain_row[...] = gain_latent
        low = (unit * table[0:1]).astype(bf16)
        hidden[...] = low
        late = nn(low, weights[...].reshape(width, R + tile))
        latent_out[...] = late
        plain = late[:, :R]
        inverse = lax.rsqrt(jnp.mean(plain * plain, axis=-1, keepdims=True) + epsilon)
        key = jnp.concatenate(
            [plain * inverse * gain_latent, turn(late[:, R:], cos[...], sin[...])], axis=1
        ).astype(bf16)
        for n in range(8):
            keys[n] = key

    return call(
        kernel,
        [
            ((rows, width), bf16, "v"),
            ((8, rows, R + tile), bf16, "v"),
            ((rows, R + tile), f32, "v"),
            ((16, width), bf16, "v"),
            ((1, R), f32, "v"),
        ],
        [(info, "s"), (tokens, "v"), (cos4, "v"), (sin4, "v")] + [(part, "a") for part in parts],
        [pltpu.VMEM((16, 2, db, R + tile), bf16), pltpu.SemaphoreType.DMA(())],
        macs=rows * width * (R + tile),
    )


def project_query(hidden, cos4, sin4, pack):
    rows, width = hidden.shape
    db = width // 32
    query = HEADS * (NOPE + ROPE)
    tile = ROPE + db
    half = ROPE // 2

    def kernel(hid, cos, sin, packed, q_nope, q_rope, weights, sem):
        start_all(pack_copies(packed, pl.ds(0, query), weights), sem)
        wait_for(weights, sem)
        raw = nn(hid[...], weights[...].reshape(width, query))
        q_nope[...] = raw[:, : HEADS * NOPE].astype(bf16)
        front = raw[:, HEADS * NOPE : HEADS * NOPE + tile]
        back = raw[:, HEADS * NOPE + tile :]
        turned_front = front * cos[...] - back * sin[...]
        turned_back = back * cos[...] + front * sin[...]
        lane = lanes((rows, tile))
        for h in range(HEADS):
            head = jnp.where(
                lane < half,
                pltpu.roll(turned_front, (tile - h * half) % tile, 1),
                jnp.where(lane < ROPE, pltpu.roll(turned_back, (tile - h * half + half) % tile, 1), 0.0),
            )
            q_rope[h * rows : (h + 1) * rows] = head.astype(bf16)

    return call(
        kernel,
        [((rows, HEADS * NOPE), bf16, "v"), ((HEADS * rows, tile), bf16, "v")],
        [(hidden, "v"), (cos4, "v"), (sin4, "v"), (pack, "a")],
        [pltpu.VMEM((32, db, query), bf16), pltpu.SemaphoreType.DMA(())],
        macs=rows * width * query,
    )


def turn(values, cosine, sine_part):
    width = values.shape[1]
    half = ROPE // 2
    lane = lanes(values.shape)
    swapped = jnp.where(lane < half, -pltpu.roll(values, width - half, 1), pltpu.roll(values, half, 1))
    return jnp.where(lane < ROPE, values * cosine + swapped * sine_part, 0.0)


def put_quarters(values, targets, z):
    quarter = values.shape[0] // 4
    for n in range(4):
        for k in range(4):

            @pl.when(z ^ k == n)
            def _(n=n, k=k):
                targets[k][0] = values[n * quarter : (n + 1) * quarter]


def visible(info, shape, row_count):
    place = lax.broadcasted_iota(jnp.int32, shape, 0) + info[1] * row_count
    key = lax.broadcasted_iota(jnp.int32, shape, 1)
    end0 = info[4]
    end1 = info[4] + info[5]
    row_doc = (place >= end0).astype(jnp.int32) + (place >= end1).astype(jnp.int32)
    key_doc = (key >= end0).astype(jnp.int32) + (key >= end1).astype(jnp.int32)
    return (row_doc == key_doc) & (key <= place)


def attend(info, q_nope, q_rope, key_parts, pack, after):
    rows = q_nope.shape[0]
    db = pack.shape[3]
    columns = pl.ds(HEADS * (NOPE + ROPE), HEADS * VD + NOPE + VD)
    width = 32 * db
    tile = q_rope.shape[1]
    out = HEADS * VD
    keys = 16 * rows
    quarter = rows // 4
    rb = R // 32

    def kernel(info, qn, qr, *refs):
        key_ins, refs = refs[:2], refs[2:]
        pack_in, refs = refs[0], refs[1:]
        probs, cat, mixture, head_out, result, key_rows, weights, expand, sem = refs
        start_all(pair_copies(key_ins, info[1] % 2, key_rows), sem.at[0])
        start_all(pack_copies(pack_in, columns, weights), sem.at[1])
        wait_for(weights, sem.at[1])
        for h in range(HEADS):
            expand[h] = weights[:, h * rb : (h + 1) * rb, out:].reshape(R, NOPE + VD)
        for h in range(HEADS):
            own = slice(h * rows, (h + 1) * rows)
            cat[own, :R] = nt(qn[:, h * NOPE : (h + 1) * NOPE], expand[h, :, :NOPE]).astype(bf16)
            cat[own, R:] = qr[own]
        wait_for(key_rows, sem.at[0])
        flat = key_rows[...].reshape(keys, R + tile)
        seen = visible(info, (rows, keys), rows)
        scale = (NOPE + ROPE) ** (-0.5)
        for h in range(HEADS):
            own = slice(h * rows, (h + 1) * rows)
            scores = jnp.where(seen, scale * nt(cat[own], flat), -1e30)
            weight = jnp.exp(scores - jnp.max(scores, axis=-1, keepdims=True))
            prob = (weight / jnp.sum(weight, axis=-1, keepdims=True)).astype(bf16)
            probs[own] = prob
            mixed = nn(prob, flat[:, :R]).astype(bf16)
            mixture[own] = mixed
            head_out[:, h * VD : (h + 1) * VD] = nn(mixed, expand[h, :, NOPE:]).astype(bf16)
        summed = nt(head_out[...], weights[:, :, :out].reshape(width, out)).astype(bf16)
        result[...] = summed.reshape(4, quarter, width)

    return call(
        kernel,
        [
            ((HEADS * rows, keys), bf16, "v"),
            ((HEADS * rows, R + tile), bf16, "v"),
            ((HEADS * rows, R), bf16, "v"),
            ((rows, out), bf16, "v"),
        ]
        + [((4, quarter, width), bf16, "v")],
        [(info, "s"), (q_nope, "v"), (q_rope, "v")]
        + [(part, "a") for part in key_parts + [pack]],
        [
            pltpu.VMEM((8, 2, rows, R + tile), bf16),
            pltpu.VMEM((32, db, out + NOPE + VD), bf16),
            pltpu.VMEM((HEADS, R, NOPE + VD), bf16),
            pltpu.SemaphoreType.DMA((2,)),
        ],
        macs=HEADS * rows * keys * (2 * R + tile) * 2,
        after=after,
    )


def quarter_norm(info, parts, tokens, small, after):
    _, quarter, width = parts.shape

    def kernel(info, came, tok, table, attention, normed):
        summed = came[0].astype(f32) + came[1].astype(f32) + came[2].astype(f32) + came[3].astype(f32)
        low = summed.astype(bf16)
        attention[0] = low
        middle = tok[info[3]].astype(f32) + low.astype(f32)
        inverse = lax.rsqrt(jnp.mean(middle * middle, axis=-1, keepdims=True) + epsilon)
        rows = (middle * inverse * table[1:2].astype(f32)).astype(bf16)
        for n in range(16):
            normed[n] = rows

    return call(
        kernel,
        [((1, quarter, width), bf16, "v"), ((16, quarter, width), bf16, "v")],
        [(info, "s"), (parts, "v"), (tokens.reshape(4, quarter, width), "v"), (small, "v")],
        [],
        after=after,
    )


def pass_on(from_one, from_three):
    half = from_one.shape[0] // 2
    return [swap(from_three[:half], ky=1), swap(from_one[half:], ky=3)]


def expert_copies(parts, me, targets):
    copies = []
    half = parts[3].shape[0]
    for part, ky, first in zip(parts, (0, 1, 3, 2, 2), (0, 0, 0, 0, half), strict=True):
        for i in range(part.shape[0]):
            block = first + i
            for n, target in enumerate(targets):
                copies.append((part.at[i, n], target.at[me ^ mask(ky, block // 2, block % 2)]))
    return copies


def expert_rows(info, normed_parts, cots, weights, ff):
    _, quarter, width = normed_parts[0].shape
    extra = cots.shape[-1] - width
    db, wide = weights[0].shape[-2:]
    count = 32 * quarter
    step = count // 4
    lane0 = FF_PAD - extra

    def kernel(info, *refs):
        nref, refs = refs[:2], refs[2:]
        cref, wref, refs = refs[0], refs[1:6], refs[6:]
        act_out, gate_out, up_out, first, keep2, send2, x, g, wg, wu, wd, out1, out2, sem = refs
        start_all(expert_copies(wref, info[0], (wg, wu, wd)), sem.at[0])
        start_all([(cref.at[:, info[1] % 2], g.at[0]), (cref.at[:, 1 - info[1] % 2], g.at[1])], sem.at[1])
        start_all([(nref[0], x.at[0]), (nref[1], x.at[1])], sem.at[2])
        for ref in (wg, wu, wd):
            wait_for(ref, sem.at[0])
        wait_for(g, sem.at[1])
        wait_for(x, sem.at[2])
        tile_lane = lanes((step, extra))
        lane = lanes((step, wide))
        half = step // quarter

        def body(i, carry):
            own = pl.ds(pl.multiple_of(i * step, step), step)
            core, at = i // 2, (i % 2) * half
            rows = x[core, pl.ds(at, half)].reshape(step, width)
            cot = g[core, pl.ds(at // 4, half // 4)].reshape(step, width + extra)
            gate_weight = wg[...].reshape(width, wide)
            up_weight = wu[...].reshape(width, wide)
            down_weight = wd[...].reshape(width, wide)
            gate_pre = nn(rows, gate_weight)
            up_pre = nn(rows, up_weight)
            back = nn(cot[:, :width], down_weight)
            router = jax.nn.sigmoid(gate_pre[:, lane0:FF_PAD])
            weighted = router * cot[:, width:].astype(f32)
            gates = route_scale * weighted / jnp.sum(weighted, axis=1, keepdims=True)
            gate = jnp.sum(jnp.where(tile_lane == ff - lane0 + info[2], gates, 0.0), axis=1, keepdims=True)
            gate_row = jnp.where(lane < FF_PAD, gate, 1.0)
            sig = jax.nn.sigmoid(gate_pre)
            silu = gate_pre * sig
            act = silu * up_pre
            own_grad = jnp.sum(jnp.where(lane < FF_PAD, act * back, 0.0), axis=1, keepdims=True)
            act_low = (gate_row * act).astype(bf16)
            grad_act = gate_row * back
            grad_gate = (grad_act * up_pre * (sig * (1.0 + gate_pre * (1.0 - sig)))).astype(bf16)
            grad_up = (grad_act * silu).astype(bf16)
            act_out[own] = act_low
            gate_out[own] = grad_gate
            up_out[own] = grad_up
            out1[own] = nt(act_low, down_weight).astype(bf16)
            out2[own, :width] = (nt(grad_gate, gate_weight) + nt(grad_up, up_weight)).astype(bf16)
            high = own_grad.astype(bf16).astype(f32)
            out2[own, width:] = (
                jnp.where(tile_lane == 8 + info[2], high, 0.0)
                + jnp.where(tile_lane == 24 + info[2], own_grad - high, 0.0)
            ).astype(bf16)
            return carry

        lax.fori_loop(0, 4, body, 0)
        core = info[1] % 2
        for n, (of, target) in enumerate(((core, keep2), (1 - core, send2))):
            pltpu.make_async_copy(out2.at[pl.ds(n * count // 2, count // 2)], target, sem.at[3 + n]).start()
            for x_at in range(4):
                rows = pl.ds(n * count // 2 + x_at * 4 * quarter, 4 * quarter)
                pltpu.make_async_copy(out1.at[rows], first.at[x_at * 2 + of], sem.at[5]).start()
        wait_for(keep2, sem.at[3])
        wait_for(send2, sem.at[4])
        wait_for(first, sem.at[5])

    return call(
        kernel,
        [((count, wide), bf16, "v")] * 3
        + [((8, 4 * quarter, width), bf16, "a")]
        + [((count // 2, width + extra), bf16, "a")] * 2,
        [(info, "s")] + [(part, "a") for part in normed_parts + [cots] + weights],
        [
            pltpu.VMEM((2, 16, quarter, width), bf16),
            pltpu.VMEM((2, 4, 4, quarter, width + extra), bf16),
            pltpu.VMEM((32, db, wide), bf16),
            pltpu.VMEM((32, db, wide), bf16),
            pltpu.VMEM((32, db, wide), bf16),
            pltpu.VMEM((count, width), bf16),
            pltpu.VMEM((count, width + extra), bf16),
            pltpu.SemaphoreType.DMA((6,)),
        ],
        macs=6 * count * width * wide,
    )


def expert_weights(info, normed_parts, cots, act, grad_gate, grad_up, after):
    _, quarter, width = normed_parts[0].shape
    extra = cots.shape[-1] - width
    count, wide = act.shape
    db = width // 32
    step = width // 8
    blocks = step // db

    def kernel(info, *refs):
        nref, refs = refs[:2], refs[2:]
        cref, refs = refs[0], refs[1:]
        a, gg, gu, *results, x, g, grads, sem = refs
        start_all([(cref.at[:, info[1] % 2], g.at[0]), (cref.at[:, 1 - info[1] % 2], g.at[1])], sem.at[0])
        start_all([(nref[0], x.at[0]), (nref[1], x.at[1])], sem.at[1])
        wait_for(g, sem.at[0])
        wait_for(x, sem.at[1])

        def body(i, carry):
            cols = pl.ds(pl.multiple_of(i * step, step), step)
            rows = x[:, :, :, cols].reshape(count, step)
            cot = g[:, :, :, :, cols].reshape(count, step)
            own = pl.ds(i * blocks, blocks)
            grads[own, 0] = tn(rows, gg[...]).astype(bf16).reshape(blocks, db, wide)
            grads[own, 1] = tn(rows, gu[...]).astype(bf16).reshape(blocks, db, wide)
            grads[own, 2] = tn(cot, a[...]).astype(bf16).reshape(blocks, db, wide)
            return carry

        lax.fori_loop(0, 8, body, 0)
        for ky in range(4):
            for kx in range(4):
                for kc in (0, 1):
                    pltpu.make_async_copy(
                        grads.at[info[0] ^ mask(ky, kx, kc)], results[2 * ky + kx // 2].at[kx % 2, kc], sem.at[2]
                    ).start()
        for result in results:
            wait_for(result, sem.at[2])

    return call(
        kernel,
        [((2, 2, 3, db, wide), bf16, "a")] * 8,
        [(info, "s")]
        + [(part, "a") for part in normed_parts + [cots]]
        + [(act, "v"), (grad_gate, "v"), (grad_up, "v")],
        [
            pltpu.VMEM((2, 16, quarter, width), bf16),
            pltpu.VMEM((2, 4, 4, quarter, width + extra), bf16),
            pltpu.VMEM((32, 3, db, wide), bf16),
            pltpu.SemaphoreType.DMA((3,)),
        ],
        macs=3 * count * width * wide,
        after=after,
    )


def quarter_copies(parts, z, target, columns=None):
    if columns is None:
        return [(part.at[0], target.at[z ^ k]) for k, part in enumerate(parts)]
    return [(part.at[0, :, columns], target.at[z ^ k]) for k, part in enumerate(parts)]


def attend_back(
    info, tokens, cotangent, picked, att_parts, grad_parts, small, probs, cat, key_parts, pack2, cos4,
    sin4, after,
):
    rows, width = tokens.shape
    quarter = rows // 4
    db = width // 32
    rb = R // 32
    tile = cat.shape[1] - R
    out = HEADS * VD
    keys = 16 * rows
    query = HEADS * (NOPE + ROPE)
    half = ROPE // 2
    extra = grad_parts[0].shape[-1] - width
    scale = (NOPE + ROPE) ** (-0.5)
    late = out + NOPE + VD

    def kernel(info, tok, cotan, pick, table, pr, ca, cos, sin, *refs):
        att_in, refs = refs[:4], refs[4:]
        grad_in, refs = refs[:4], refs[4:]
        key_in, refs = refs[:2], refs[2:]
        in2, refs = refs[0], refs[1:]
        (
            grad_middle, small_grads, key_keep, key_send, grad_att, grad_heads, grad_abs, grad_q,
            att, arrived, key_rows, w2, expand, grad_mix, grad_scores, key_grads, sem,
        ) = refs
        start_all(quarter_copies(grad_in, info[3], arrived), sem.at[0])
        start_all(quarter_copies(att_in, info[3], att), sem.at[1])
        start_all(pack_copies(in2, pl.ds(query, late), w2), sem.at[2])
        start_all(pair_copies(key_in, info[1] % 2, key_rows), sem.at[3])
        wait_for(arrived, sem.at[0])
        wait_for(att, sem.at[1])
        middle = tok[...].astype(f32) + att[...].reshape(rows, width).astype(f32)
        inverse = lax.rsqrt(jnp.mean(middle * middle, axis=-1, keepdims=True) + epsilon)
        unit = middle * inverse
        gain = table[1:2].astype(f32)
        normed = (unit * gain).astype(bf16)
        came = arrived[...].reshape(rows, width + extra)
        sig = jax.nn.sigmoid(nt(normed, table[...]))
        chosen = pick[...]
        weighted = sig * chosen
        gate_total = jnp.sum(weighted, axis=1, keepdims=True)
        gates = route_scale * weighted / gate_total
        grad_gates = came[:, width : width + 16].astype(f32) + came[:, width + 16 : width + 32].astype(f32)
        grad_weighted = (route_scale * grad_gates - jnp.sum(grad_gates * gates, axis=1, keepdims=True)) / gate_total
        grad_logits = grad_weighted * chosen * sig * (1.0 - sig)
        high, low = high_low(grad_logits)
        grads = tn(high, normed) + tn(low, normed)
        grad_normed = came[:, :width].astype(f32) + nn(high, table[...]) + nn(low, table[...])
        scaled = grad_normed * gain
        grad_mid = cotan[...].astype(f32) + inverse * (
            scaled - unit * jnp.mean(scaled * unit, axis=-1, keepdims=True)
        )
        d_gain = jnp.sum(grad_normed * unit, axis=0, keepdims=True)
        row16 = lax.broadcasted_iota(jnp.int32, (16, width), 0)
        small_grads[...] = jnp.where(row16 >= 8, grads, jnp.where(row16 == 1, d_gain, 0.0))
        grad_middle[...] = grad_mid
        grad_att[...] = grad_mid.astype(bf16)
        wait_for(w2, sem.at[2])
        for h in range(HEADS):
            expand[h] = w2[:, h * rb : (h + 1) * rb, out:].reshape(R, NOPE + VD)
        grad_heads[...] = nn(grad_att[...], w2[:, :, :out].reshape(width, out)).astype(bf16)
        for h in range(HEADS):
            own = slice(h * rows, (h + 1) * rows)
            grad_mix[own] = nt(grad_heads[:, h * VD : (h + 1) * VD], expand[h, :, NOPE:]).astype(bf16)
        wait_for(key_rows, sem.at[3])
        flat = key_rows[...].reshape(keys, R + tile)
        lane = lanes((rows, tile))
        front = jnp.zeros((rows, tile), f32)
        back = jnp.zeros((rows, tile), f32)
        for h in range(HEADS):
            own = slice(h * rows, (h + 1) * rows)
            grad_prob = nt(grad_mix[own], flat[:, :R])
            prob = pr[own].astype(f32)
            inner = jnp.sum(prob * grad_prob, axis=-1, keepdims=True)
            grad_score = (prob * (grad_prob - inner)).astype(bf16)
            grad_scores[own] = grad_score
            grad_cat = scale * nn(grad_score, flat)
            low = grad_cat[:, :R].astype(bf16)
            grad_abs[own] = low
            grad_q[:, h * NOPE : (h + 1) * NOPE] = nn(low, expand[h, :, :NOPE]).astype(bf16)
            turned = grad_cat[:, R:]
            inside = (lane >= h * half) & (lane < (h + 1) * half)
            front = jnp.where(inside, pltpu.roll(turned, (h * half) % tile, 1), front)
            back = jnp.where(inside, pltpu.roll(turned, (h * half + tile - half) % tile, 1), back)
        grad_q[:, HEADS * NOPE : HEADS * NOPE + tile] = (front * cos[...] + back * sin[...]).astype(bf16)
        grad_q[:, HEADS * NOPE + tile :] = (back * cos[...] - front * sin[...]).astype(bf16)
        chunk = keys // 4
        for n in range(4):
            cols = slice(n * chunk, (n + 1) * chunk)
            part = scale * tn(grad_scores[:, cols], ca[...])
            latent = part[:, :R] + tn(pr[:, cols], grad_mix[...])
            own = slice(n * 2, (n + 1) * 2)
            key_grads[own, :, :, :R] = latent.astype(bf16).reshape(2, 2, rows, R)
            key_grads[own, :, :, R:] = part[:, R:].astype(bf16).reshape(2, 2, rows, tile)
        core = info[1] % 2
        pltpu.make_async_copy(key_grads.at[:, core], key_keep, sem.at[5]).start()
        pltpu.make_async_copy(key_grads.at[:, 1 - core], key_send, sem.at[6]).start()
        wait_for(key_keep, sem.at[5])
        wait_for(key_send, sem.at[6])

    vmem_ins = [tokens, cotangent, picked, small, probs, cat, cos4, sin4]
    return call(
        kernel,
        [
            ((rows, width), f32, "v"),
            ((16, width), f32, "v"),
            ((8, rows, R + tile), bf16, "a"),
            ((8, rows, R + tile), bf16, "a"),
            ((rows, width), bf16, "v"),
            ((rows, out), bf16, "v"),
            ((HEADS * rows, R), bf16, "v"),
            ((rows, query), bf16, "v"),
        ],
        [(info, "s")]
        + [(array, "v") for array in vmem_ins]
        + [(part, "a") for part in att_parts + grad_parts + key_parts + [pack2]],
        [
            pltpu.VMEM((4, quarter, width), bf16),
            pltpu.VMEM((4, quarter, width + extra), bf16),
            pltpu.VMEM((8, 2, rows, R + tile), bf16),
            pltpu.VMEM((32, db, late), bf16),
            pltpu.VMEM((HEADS, R, NOPE + VD), bf16),
            pltpu.VMEM((HEADS * rows, R), bf16),
            pltpu.VMEM((HEADS * rows, keys), bf16),
            pltpu.VMEM((8, 2, rows, R + tile), bf16),
            pltpu.SemaphoreType.DMA((7,)),
        ],
        macs=HEADS * rows * keys * (4 * R + 2 * tile) * 2,
        after=after,
    )


def attention_weights(info, grad_att, grad_heads, grad_abs, grad_q, hidden, head_out, mixture, q_nope, pack, after):
    rows, width = hidden.shape
    quarter = rows // 4
    db = width // 32
    rb = R // 32
    out = HEADS * VD
    late = out + NOPE + VD
    query = HEADS * (NOPE + ROPE)

    def kernel(info, ga, gh, gb, gq, hid, ho, mix, qn, *refs):
        packed, hid0, hid1, hid2, hid3, result, w1, grads, sem = refs
        start_all(pack_copies(packed, pl.ds(0, query), w1), sem.at[0])
        grads[:, :, :, :out] = tn(ga[...], ho[...]).astype(bf16).reshape(16, 2, db, out)
        for h in range(HEADS):
            part = slice(h * rows, (h + 1) * rows)
            here = slice(h * rb, (h + 1) * rb)
            grads[:, :, here, out : out + NOPE] = (
                tn(gb[part], qn[:, h * NOPE : (h + 1) * NOPE]).astype(bf16).reshape(16, 2, rb, NOPE)
            )
            grads[:, :, here, out + NOPE : late] = (
                tn(mix[part], gh[:, h * VD : (h + 1) * VD]).astype(bf16).reshape(16, 2, rb, VD)
            )
        grads[:, :, :, late:] = tn(hid[...], gq[...]).astype(bf16).reshape(16, 2, db, query)
        for n in range(16):
            for core in (0, 1):
                target = result.at[(n % 4) * 2 + core, ((n // 4) % 2) * 2 + n // 8]
                pltpu.make_async_copy(grads.at[n, core], target, sem.at[1]).start()
        wait_for(w1, sem.at[0])
        put_quarters(nt(gq[...], w1[...].reshape(width, query)).astype(bf16), (hid0, hid1, hid2, hid3), info[3])
        wait_for(result, sem.at[1])

    vmem_ins = [grad_att, grad_heads, grad_abs, grad_q, hidden, head_out, mixture, q_nope]
    return call(
        kernel,
        [((1, quarter, width), bf16, "v")] * 4 + [((8, 4, db, late + query), bf16, "a")],
        [(info, "s")] + [(array, "v") for array in vmem_ins] + [(pack, "a")],
        [
            pltpu.VMEM((32, db, query), bf16),
            pltpu.VMEM((16, 2, db, late + query), bf16),
            pltpu.SemaphoreType.DMA((2,)),
        ],
        macs=rows * width * (out + 2 * query) + 2 * HEADS * R * rows * NOPE,
        after=after,
    )


def finish(
    info, tokens, grad_middle, hidden, latent, gain_latent, small, small_grads, key_parts, hidden_parts, att_parts,
    sum_parts, parts1, cos4, sin4, after,
):
    rows, width = tokens.shape
    quarter = rows // 4
    db = width // 32
    rb = R // 32
    tile = latent.shape[1] - R
    query = HEADS * (NOPE + ROPE)

    def kernel(info, tok, gm, hid, lat, gl, table, sg, cos, sin, *refs):
        key_in, refs = refs[:4], refs[4:]
        hid_in, refs = refs[:4], refs[4:]
        att_in, refs = refs[:4], refs[4:]
        sum_in, refs = refs[:4], refs[4:]
        in1, refs = refs[: len(parts1)], refs[len(parts1) :]
        output, d_tokens, keep, send, own_keys, part, att, sums, w1, grads, sem = refs
        start_all(quarter_copies(key_in, info[3], own_keys), sem.at[6])
        start_all(pair_copies(in1, info[1] % 2, w1), sem.at[0])
        start_all(quarter_copies(hid_in, info[3], part), sem.at[1])
        start_all(quarter_copies(att_in, info[3], att), sem.at[2])
        start_all(quarter_copies(sum_in, info[3], sums), sem.at[3])
        wait_for(own_keys, sem.at[6])
        own = own_keys[...].reshape(rows, R + tile)
        plain = lat[:, :R]
        inverse = lax.rsqrt(jnp.mean(plain * plain, axis=-1, keepdims=True) + epsilon)
        unit = plain * inverse
        grad_y = own[:, :R]
        scaled = grad_y * gl[...]
        d_gain_latent = jnp.sum(grad_y * unit, axis=0, keepdims=True)
        grad_in = inverse * (scaled - unit * jnp.mean(scaled * unit, axis=-1, keepdims=True))
        grad_latent = jnp.concatenate([grad_in, turn(own[:, R:], cos[...], -sin[...])], axis=1).astype(bf16)
        d_latent = tn(hid[...], grad_latent).astype(bf16)
        grads[...] = d_latent.reshape(16, 2, db, R + tile)
        wait_for(w1, sem.at[0])
        wait_for(part, sem.at[1])
        x = tok[...].astype(f32)
        inverse = lax.rsqrt(jnp.mean(x * x, axis=-1, keepdims=True) + epsilon)
        unit = x * inverse
        grad_hidden = part[...].reshape(rows, width).astype(f32) + nt(
            grad_latent, w1[...].reshape(width, R + tile)
        )
        scaled = grad_hidden * table[0:1].astype(f32)
        d_tokens[...] = gm[...] + inverse * (scaled - unit * jnp.mean(scaled * unit, axis=-1, keepdims=True))
        d_gain = jnp.sum(grad_hidden * unit, axis=0, keepdims=True)
        row16 = lax.broadcasted_iota(jnp.int32, (16, width), 0)
        every = jnp.where(row16 == 0, d_gain, sg[...])
        lane = lanes((16, tile))
        row = lax.broadcasted_iota(jnp.int32, (16, tile), 0)
        per = tile // rb
        for j in range(32):
            t = j // 2
            values = every[:, t * tile : (t + 1) * tile]
            if j % 2 == 0:
                values = pltpu.roll(values, db, 1)
            gains = d_gain_latent[:, (j // per) * tile : (j // per + 1) * tile]
            gains = pltpu.roll(gains, (db + tile - (j % per) * rb) % tile, 1)
            values = jnp.where(row == 2, jnp.where(lane < db + rb, gains, 0.0), values)
            before = grads[j // 2, j % 2, 0:16, R:].astype(f32)
            grads[j // 2, j % 2, 0:16, R:] = jnp.where(lane < db, before, values).astype(bf16)
        core = info[1] % 2
        rows_here = pl.ds(pl.multiple_of(info[3] * (db // 4), db // 4), db // 4)
        pltpu.make_async_copy(grads.at[:, core, rows_here], keep, sem.at[4]).start()
        pltpu.make_async_copy(grads.at[:, 1 - core, rows_here], send, sem.at[5]).start()
        wait_for(att, sem.at[2])
        wait_for(sums, sem.at[3])
        middle = x + att[...].reshape(rows, width).astype(f32)
        output[...] = (middle + sums[...].reshape(rows, width).astype(f32)).astype(bf16)
        wait_for(keep, sem.at[4])
        wait_for(send, sem.at[5])

    vmem_ins = [tokens, grad_middle, hidden, latent, gain_latent, small, small_grads, cos4, sin4]
    return call(
        kernel,
        [
            ((rows, width), bf16, "v"),
            ((rows, width), f32, "v"),
            ((16, db // 4, R + tile), bf16, "a"),
            ((16, db // 4, R + tile), bf16, "a"),
        ],
        [(info, "s")]
        + [(array, "v") for array in vmem_ins]
        + [(part, "a") for part in key_parts + hidden_parts + att_parts + sum_parts + parts1],
        [
            pltpu.VMEM((4, quarter, R + tile), f32),
            pltpu.VMEM((4, quarter, width), bf16),
            pltpu.VMEM((4, quarter, width), bf16),
            pltpu.VMEM((4, quarter, width), bf16),
            pltpu.VMEM((16, 2, db, R + tile), bf16),
            pltpu.VMEM((16, 2, db, R + tile), bf16),
            pltpu.SemaphoreType.DMA((7,)),
        ],
        macs=4 * rows * width * (R + tile),
        after=after,
    )


def unpack_experts(info, own, other, ff, sh):
    _, _, db, wide = other.shape

    def kernel(info, a0, a1, a2, a3, b, gate, up, down, sg, su, sd, slots, sem):
        for kx, a in enumerate((a0, a1, a2, a3)):
            pltpu.make_async_copy(a.at[0], slots.at[info[2] ^ (kx * 2)], sem).start()
            pltpu.make_async_copy(b.at[kx], slots.at[info[2] ^ (kx * 2 + 1)], sem).start()
        wait_for(slots, sem)
        for n, (routed, shared) in enumerate(((gate, sg), (up, su), (down, sd))):
            for e in range(8):
                routed[e] = slots[e, n, :, :ff].astype(f32)
            shared[...] = jnp.concatenate(
                [slots[e, n, :, FF_PAD : FF_PAD + sh].astype(f32) for e in range(8)], axis=1
            )

    return call(
        kernel,
        [((8, db, ff), f32, "v")] * 3 + [((db, 8 * sh), f32, "v")] * 3,
        [(info, "s")] + [(part, "a") for part in own] + [(other, "a")],
        [pltpu.VMEM((8, 3, db, wide), bf16), pltpu.SemaphoreType.DMA(())],
    )


def unpack_rest(info, parts):
    _, quarter, columns = parts[0].shape

    def kernel(info, a, b, c, d, result):
        for k, part in enumerate((a, b, c, d)):
            result[info[3] ^ k] = part[0].astype(f32)

    return call(
        kernel,
        [((4, quarter, columns), f32, "v")],
        [(info, "s")] + [(part, "v") for part in parts],
        [],
    )[0].reshape(4 * quarter, columns)


def unpack_attention(grads):
    db, _ = grads.shape
    rb = R // 32
    out = HEADS * VD
    late = out + NOPE + VD
    per_head, half = NOPE + ROPE, ROPE // 2

    def kernel(g, d_out, d_expand, d_query):
        d_out[...] = g[:, :out].astype(f32)
        for h in range(HEADS):
            d_expand[:, h * (NOPE + VD) : (h + 1) * (NOPE + VD)] = g[h * rb : (h + 1) * rb, out:late].astype(f32)
            plain = g[:, late + h * NOPE : late + (h + 1) * NOPE].astype(f32)
            front = late + HEADS * NOPE + h * half
            back = front + HEADS * half
            d_query[:, h * per_head : (h + 1) * per_head] = jnp.concatenate(
                [plain, g[:, front : front + half].astype(f32), g[:, back : back + half].astype(f32)], axis=1
            )

    return call(
        kernel,
        [
            ((db, out), f32, "v"),
            ((rb, HEADS * (NOPE + VD)), f32, "v"),
            ((db, HEADS * per_head), f32, "v"),
        ],
        [(grads, "v")],
        [],
    )


def shards(
    tokens,
    lengths,
    routes,
    cotangent,
    attn_gain,
    w_query,
    w_latent,
    latent_gain,
    w_expand,
    w_out,
    moe_gain,
    w_router,
    w_gate,
    w_up,
    w_down,
    shared_gate,
    shared_up,
    shared_down,
):
    me = lax.axis_index(PLANE)
    place = me % 16
    member = me % 8
    z = lax.axis_index("z")
    rows, width = tokens.shape
    quarter = rows // 4
    db = width // 32
    rb = R // 32
    ff, sh = w_gate.shape[2], shared_gate.shape[1] // 8
    tile = ROPE + db
    query = HEADS * (NOPE + ROPE)
    half = ROPE // 2
    extra = min(128, FF_PAD)
    wide = FF_PAD + SH_PAD
    info = jnp.concatenate([jnp.stack([me, place, member, z]).astype(jnp.int32), lengths[0]])

    one, two = pack_attention(
        w_query, w_latent, attn_gain, moe_gain, latent_gain, w_router.T, w_out.T, w_expand
    )
    pack = lax.all_gather(two, ("yh", "yl", "x", "c"), axis=0).reshape(2, 2, 8, db, -1)
    keep, send = pack_experts(
        info, w_gate, w_up, jnp.swapaxes(w_down, 1, 2), shared_gate, shared_up, shared_down.T, w_router
    )
    came = swap(send, kc=1)
    by_x = [jnp.stack([keep[k], came[k]]) for k in range(4)]
    latent_parts = gather(one, ("yl", "yh", "x"), ())

    position = place * rows + jnp.arange(rows, dtype=jnp.int32)
    ends = jnp.stack([lengths[0, 0], lengths[0, 0] + lengths[0, 1]])
    start = jnp.where(position >= ends[1], ends[1], jnp.where(position >= ends[0], ends[0], 0))
    frequency = rope_base ** (-jnp.arange(half, dtype=f32) / half)
    angles = (position - start).astype(f32)[:, None] * jnp.tile(frequency, 2 * HEADS * half // ROPE)[None, :]
    cos4, sin4 = jnp.cos(angles), jnp.sin(angles)
    picked = jnp.sum(
        (routes[:, :, None] == jnp.arange(16, dtype=jnp.int32)[None, None, :] - 8).astype(f32), axis=1
    )
    lane_pick = jnp.sum(
        (routes[:, :, None] == jnp.arange(extra, dtype=jnp.int32)[None, None, :] - (ff - FF_PAD + extra)), axis=1
    ).astype(bf16)

    hidden, keys, latent, small, gain_latent = project_latent(info, tokens, cos4, sin4, latent_parts)
    mine = jnp.concatenate([by_x[0]] + [swap(by_x[k], kx=k) for k in (1, 2, 3)])
    weights = [mine] + [swap(mine, ky=k) for k in (1, 3)]
    keys = exchange(hold(keys, mine), ("yh", "x"))
    key_parts = [keys, swap(keys, kc=1)]
    cots = tie(jnp.concatenate([cotangent, lane_pick], axis=1), key_parts[0])
    cots = lax.all_gather(cots, ("x", "c"), axis=0).reshape(4, 2, 4, quarter, width + extra)
    q_nope, q_rope = project_query(hidden, cos4, sin4, pack)
    probs, cat, mixture, head_out, attention = attend(info, q_nope, q_rope, key_parts, pack, ())
    attention = hold(exchange(attention, "z"), weights[1], weights[2])
    own_attention, normed = quarter_norm(info, attention, tokens, small, ())
    weights += pass_on(*weights[1:])
    normed_parts = gather(normed, ("x", "z"), weights[3:])
    att_parts = [own_attention] + [swap_z(own_attention, k) for k in (1, 2, 3)]

    act, grad_gate, grad_up, first, keep2, send2 = expert_rows(
        info, normed_parts, cots, weights, ff
    )

    def scattered(values):
        return exchange(values.reshape(16, quarter, -1), ("x", "z"))

    def collect(values):
        return jnp.sum(values.astype(f32), axis=0, keepdims=True).astype(bf16)

    second = total([keep2, swap(send2, kc=1)])
    d_experts = expert_weights(info, normed_parts, cots, act, grad_gate, grad_up, (second,))
    opposite3, opposite1 = swap(d_experts[4], ky=1), swap(d_experts[5], ky=3)
    straight3, straight1 = swap(d_experts[7], ky=3), swap(d_experts[2], ky=1)
    onward3, onward1 = total([d_experts[6], opposite3]), total([d_experts[3], opposite1])
    second = collect(hold(scattered(second), d_experts[0]))
    first = lax.psum_scatter(first, ("x", "c"), scatter_dimension=0).reshape(4, quarter, width)
    first = lax.psum_scatter(first, "z", scatter_dimension=0)[None]
    onward3, onward1 = swap(onward3, ky=3), swap(onward1, ky=1)
    grad_parts = [second] + [swap_z(second, k) for k in (1, 2, 3)]

    grad_middle, small_grads, key_keep, key_send, grad_att, grad_heads, grad_abs, grad_q = attend_back(
        info, tokens, cotangent, picked, att_parts, grad_parts, small, probs, cat, key_parts, pack, cos4, sin4,
        (straight3, straight1),
    )
    *hidden_part, most = attention_weights(
        info, grad_att, grad_heads, grad_abs, grad_q, hidden, head_out, mixture, q_nope, pack, (onward3, onward1)
    )
    grad_keys = total([key_keep, swap(hold(key_send, onward3, onward1), kc=1)]).reshape(32, quarter, R + tile)
    grad_keys = exchange(grad_keys, ("yh", "x", "z"))
    grad_hidden = total([hidden_part[0]] + [swap_z(hidden_part[k], k) for k in (1, 2, 3)])
    hidden_parts = [grad_hidden] + [swap_z(grad_hidden, k) for k in (1, 2, 3)]
    sum_parts = [first] + [swap_z(first, k) for k in (1, 2, 3)]
    most = lax.psum_scatter(most, ("x", "c"), scatter_dimension=0)
    most = lax.psum_scatter(most, ("yh", "yl"), scatter_dimension=0)
    grad_keys = jnp.sum(grad_keys.astype(f32), axis=0, keepdims=True)
    grad_key_parts = [grad_keys] + [swap_z(grad_keys, k) for k in (1, 2, 3)]
    d_mine = [
        total([part[k % 2] for part in (d_experts[k // 2], (onward3, straight3)[k // 2], (straight1, onward1)[k // 2])])
        for k in range(4)
    ]

    d_mine = [d_mine[0]] + [swap(hold(d_mine[k], grad_keys), kx=k) for k in (1, 2, 3)]
    output, d_tokens, keep, send = finish(
        info, tokens, grad_middle, hidden, latent, gain_latent, small, small_grads, grad_key_parts, hidden_parts,
        att_parts, sum_parts, latent_parts, cos4, sin4, (),
    )
    rest = total([keep, swap(send, kc=1)])
    rest = collect(exchange(hold(rest, *d_mine), ("yl", "yh", "x")))
    d_other = swap(jnp.stack([part[1] for part in d_mine]), kc=1)
    d_routed = unpack_experts(info, d_mine, d_other, ff, sh)
    d_out, d_expand, d_query = unpack_attention(most)
    rest = unpack_rest(info, [rest] + [swap_z(rest, k) for k in (1, 2, 3)])
    aux = rest[:16, R + ROPE :]
    return (
        output,
        d_tokens,
        aux[0],
        d_query,
        rest[:, : R + ROPE],
        aux[2, :rb],
        d_expand,
        d_out.T,
        aux[1],
        aux[8:16].T,
        d_routed[0],
        d_routed[1],
        jnp.swapaxes(d_routed[2], 1, 2),
        d_routed[3],
        d_routed[4],
        d_routed[5].T,
    )


def solution(mesh):
    rows = P(PLANE, None)
    split = P(PLANE, "z")
    vector = P(PLANE)
    turned = P("z", PLANE)
    expert_rows = P(None, PLANE, "z")
    expert_columns = P(None, "z", PLANE)
    fine = Mesh(mesh.devices.reshape(2, 2, 4, 2, 4), ("yl", "yh", "x", "c", "z"))
    return jax.shard_map(
        shards,
        mesh=fine,
        in_specs=(
            rows,
            P("yl", None),
            rows,
            rows,
            vector,
            split,
            rows,
            vector,
            split,
            turned,
            vector,
            rows,
            expert_rows,
            expert_rows,
            expert_columns,
            split,
            split,
            turned,
        ),
        out_specs=(
            rows,
            rows,
            vector,
            split,
            rows,
            vector,
            split,
            turned,
            vector,
            rows,
            expert_rows,
            expert_rows,
            expert_columns,
            split,
            split,
            turned,
        ),
        check_vma=False,
    )
```

```python
import math

import jax
import jax.numpy as jnp
from jax import lax
from jax.experimental import pallas as pl
from jax.experimental.pallas import tpu as pltpu
from jax.sharding import Mesh
from jax.sharding import PartitionSpec as P

NOPE = 128
ROPE = 64
VD = 128
R = 512
E = 8
FF_PAD = 384
SH_PAD = 128
HEADS = 4

epsilon = 1e-06
rope_base = 50000.0
route_scale = 2.446
bf16 = jnp.bfloat16
f32 = jnp.float32

PLANE = ("yl", "yh", "x", "c")
YS = ("yl", "yh")


def mask(ky=0, kx=0, kc=0):
    return (ky & 1) * 16 + (ky >> 1) * 8 + kx * 2 + kc


def swap(values, ky=0, kx=0, kc=0):
    bits = mask(ky, kx, kc)
    return lax.ppermute(values, PLANE, [(i, i ^ bits) for i in range(32)])


def swap_z(values, k):
    return lax.ppermute(values, "z", [(i, i ^ k) for i in range(4)])


def total(parts, dtype=bf16):
    out = parts[0].astype(f32)
    for part in parts[1:]:
        out = out + part.astype(f32)
    return out.astype(dtype)


def nn(left, right):
    return jnp.dot(left, right, preferred_element_type=f32)


def nt(left, right):
    return lax.dot_general(left, right, (((1,), (1,)), ((), ())), preferred_element_type=f32)


def tn(left, right):
    return lax.dot_general(left, right, (((0,), (0,)), ((), ())), preferred_element_type=f32)


def lanes(shape):
    return lax.broadcasted_iota(jnp.int32, shape, 1)


def high_low(values):
    high = values.astype(bf16)
    return high, (values - high.astype(f32)).astype(bf16)


def start_all(copies, sem):
    for source, destination in copies:
        pltpu.make_async_copy(source, destination, sem).start()


def wait_for(ref, sem):
    pltpu.make_async_copy(ref, ref, sem).wait()


def call(kernel, outs, ins, scratch, macs=0, vmem=63, after=()):
    count, late = len(ins), len(after)
    body = kernel
    if late:

        def body(*refs):
            kernel(*refs[:count], *refs[count + late :])

    moved = sum(array.size * array.dtype.itemsize for array, _ in ins)
    moved += sum(math.prod(shape) * jnp.dtype(dtype).itemsize for shape, dtype, _ in outs)
    spaces = {"s": pltpu.SMEM, "v": pltpu.VMEM, "a": pl.ANY}
    return pl.pallas_call(
        body,
        out_shape=[jax.ShapeDtypeStruct(shape, dtype) for shape, dtype, _ in outs],
        in_specs=[pl.BlockSpec(memory_space=spaces[space]) for _, space in ins]
        + [pl.BlockSpec(memory_space=pl.ANY)] * late,
        out_specs=[pl.BlockSpec(memory_space=spaces[space]) for _, _, space in outs],
        scratch_shapes=scratch,
        compiler_params=pltpu.CompilerParams(vmem_limit_bytes=vmem << 20),
        cost_estimate=pl.CostEstimate(flops=4 * macs, bytes_accessed=moved, transcendentals=0),
    )(*[array for array, _ in ins], *after)


def exchange(blocks, axes):
    return lax.all_to_all(blocks, axes, 0, 0, tiled=True)


def gather(copies, axes, after):
    own = hold(exchange(copies, axes), *after)
    return [own, swap(own, kc=1)]


def pair_copies(parts, core, target, columns=None):
    if columns is not None:
        parts = [part.at[:, :, columns] for part in parts]
    return [(parts[0], target.at[:, core]), (parts[1], target.at[:, 1 - core])]


def pack_copies(pack, columns, target):
    return [
        (pack.at[yh, yl, :, :, columns], target.at[pl.ds(yl * 16 + yh * 8, 8)]) for yh in (0, 1) for yl in (0, 1)
    ]


def hold(values, *after):
    def kernel(*refs):
        pass

    return pl.pallas_call(
        kernel,
        out_shape=jax.ShapeDtypeStruct(values.shape, values.dtype),
        in_specs=[pl.BlockSpec(memory_space=pl.ANY)] * (1 + len(after)),
        out_specs=pl.BlockSpec(memory_space=pl.ANY),
        input_output_aliases={0: 0},
    )(values, *after)


def pack_attention(w_query, w_latent, attn_gain, moe_gain, latent_gain, router_t, out_t, w_expand):
    db = w_query.shape[0]
    query = w_query.shape[1]
    late = w_latent.shape[1]
    out = out_t.shape[1]
    per_head = NOPE + ROPE

    def kernel(q, lat, ag, mg, lg, rt, ot, ex, first, second):
        plain = [q[:, h * per_head : h * per_head + NOPE] for h in range(HEADS)]
        front = [q[:, h * per_head + NOPE : h * per_head + NOPE + ROPE // 2] for h in range(HEADS)]
        back = [q[:, h * per_head + NOPE + ROPE // 2 : (h + 1) * per_head] for h in range(HEADS)]
        rb = lg.shape[1]
        small = jnp.concatenate(
            [
                ag[...].astype(f32),
                mg[...].astype(f32),
                jnp.concatenate([lg[...].astype(f32), jnp.zeros((1, db - rb), f32)], axis=1),
                jnp.zeros((5, db), f32),
                rt[...].astype(f32),
            ]
            + ([jnp.zeros((db - 16, db), f32)] if db > 16 else []),
            axis=0,
        ).astype(bf16)
        one = jnp.concatenate([lat[...], small], axis=1)
        for n in range(16):
            first[n] = one
        width = ex.shape[1] // HEADS
        expand = jnp.concatenate([ex[:, h * width : (h + 1) * width] for h in range(HEADS)], axis=0)
        second[...] = jnp.concatenate(plain + front + back + [ot[...], expand], axis=1)

    two = query + out + w_expand.shape[1] // HEADS
    ins = [w_query, w_latent, attn_gain[None], moe_gain[None], latent_gain[None], router_t, out_t, w_expand]
    return call(
        kernel,
        [((16, db, late + db), bf16, "v"), ((db, two), bf16, "v")],
        [(array, "v") for array in ins],
        [],
    )


def pack_experts(info, gate, up, down_t, shared_gate, shared_up, shared_down_t, router):
    count, db, ff = gate.shape
    sh = shared_gate.shape[1] // count
    wide = FF_PAD + SH_PAD

    def kernel(info, g, u, d, sg, su, sd, rt, keep, send, packed, sem):
        fill = FF_PAD - ff - count
        for n, (routed, shared) in enumerate(((g, sg), (u, su), (d, sd))):
            extra = rt[...] if n == 0 else jnp.zeros((db, count), bf16)
            for e in range(count):
                packed[e, n] = jnp.concatenate(
                    [
                        routed[e],
                        extra,
                        jnp.zeros((db, fill), bf16),
                        shared[:, e * sh : (e + 1) * sh],
                        jnp.zeros((db, SH_PAD - sh), bf16),
                    ],
                    axis=1,
                )
        copies = []
        for kx in range(4):
            copies.append((packed.at[info[2] ^ (kx * 2)], keep.at[kx], sem.at[0]))
            copies.append((packed.at[info[2] ^ (kx * 2 + 1)], send.at[kx], sem.at[1]))
        for source, destination, which in copies:
            pltpu.make_async_copy(source, destination, which).start()
        wait_for(keep, sem.at[0])
        wait_for(send, sem.at[1])

    ins = [gate, up, down_t, shared_gate, shared_up, shared_down_t, router]
    return call(
        kernel,
        [((4, 3, db, wide), bf16, "a")] * 2,
        [(info, "s")] + [(array, "v") for array in ins],
        [pltpu.VMEM((count, 3, db, wide), bf16), pltpu.SemaphoreType.DMA((2,))],
    )


def project_latent(info, tokens, cos4, sin4, parts):
    rows, width = tokens.shape
    db = width // 32
    rb = R // 32
    tile = ROPE + db

    def kernel(info, tok, cos, sin, own, other, hidden, keys, latent_out, small, gain_row, pairs, sem):
        start_all(pair_copies((own, other), info[1] % 2, pairs), sem)
        x = tok[...].astype(f32)
        inverse = lax.rsqrt(jnp.mean(x * x, axis=-1, keepdims=True) + epsilon)
        unit = x * inverse
        wait_for(pairs, sem)
        weights = pairs.reshape(32, db, R + tile)
        lane = lanes((16, tile))
        tiles = []
        for t in range(16):
            even = weights[2 * t, 0:16, R:].astype(f32)
            odd = weights[2 * t + 1, 0:16, R:].astype(f32)
            tiles.append(jnp.where(lane < db, pltpu.roll(even, tile - db, 1), odd))
        table = jnp.concatenate(tiles, axis=1)
        small[...] = table.astype(bf16)
        lane = lanes((1, tile))
        per = tile // rb
        pieces = []
        for t in range(32 // per):
            piece = jnp.zeros((1, tile), f32)
            for i in range(per):
                row = weights[t * per + i, 0:16, R:].astype(f32)[2:3]
                piece = jnp.where(lane // rb == i, pltpu.roll(row, (i * rb + tile - db) % tile, 1), piece)
            pieces.append(piece)
        gain_latent = jnp.concatenate(pieces, axis=1)
        gain_row[...] = gain_latent
        low = (unit * table[0:1]).astype(bf16)
        hidden[...] = low
        late = nn(low, weights[...].reshape(width, R + tile))
        latent_out[...] = late
        plain = late[:, :R]
        inverse = lax.rsqrt(jnp.mean(plain * plain, axis=-1, keepdims=True) + epsilon)
        key = jnp.concatenate(
            [plain * inverse * gain_latent, turn(late[:, R:], cos[...], sin[...])], axis=1
        ).astype(bf16)
        for n in range(8):
            keys[n] = key

    return call(
        kernel,
        [
            ((rows, width), bf16, "v"),
            ((8, rows, R + tile), bf16, "v"),
            ((rows, R + tile), f32, "v"),
            ((16, width), bf16, "v"),
            ((1, R), f32, "v"),
        ],
        [(info, "s"), (tokens, "v"), (cos4, "v"), (sin4, "v")] + [(part, "a") for part in parts],
        [pltpu.VMEM((16, 2, db, R + tile), bf16), pltpu.SemaphoreType.DMA(())],
        macs=rows * width * (R + tile),
    )


def project_query(hidden, cos4, sin4, pack):
    rows, width = hidden.shape
    db = width // 32
    query = HEADS * (NOPE + ROPE)
    tile = ROPE + db
    half = ROPE // 2

    def kernel(hid, cos, sin, packed, q_nope, q_rope, weights, sem):
        start_all(pack_copies(packed, pl.ds(0, query), weights), sem)
        wait_for(weights, sem)
        raw = nn(hid[...], weights[...].reshape(width, query))
        q_nope[...] = raw[:, : HEADS * NOPE].astype(bf16)
        front = raw[:, HEADS * NOPE : HEADS * NOPE + tile]
        back = raw[:, HEADS * NOPE + tile :]
        turned_front = front * cos[...] - back * sin[...]
        turned_back = back * cos[...] + front * sin[...]
        lane = lanes((rows, tile))
        for h in range(HEADS):
            head = jnp.where(
                lane < half,
                pltpu.roll(turned_front, (tile - h * half) % tile, 1),
                jnp.where(lane < ROPE, pltpu.roll(turned_back, (tile - h * half + half) % tile, 1), 0.0),
            )
            q_rope[h * rows : (h + 1) * rows] = head.astype(bf16)

    return call(
        kernel,
        [((rows, HEADS * NOPE), bf16, "v"), ((HEADS * rows, tile), bf16, "v")],
        [(hidden, "v"), (cos4, "v"), (sin4, "v"), (pack, "a")],
        [pltpu.VMEM((32, db, query), bf16), pltpu.SemaphoreType.DMA(())],
        macs=rows * width * query,
    )


def turn(values, cosine, sine_part):
    width = values.shape[1]
    half = ROPE // 2
    lane = lanes(values.shape)
    swapped = jnp.where(lane < half, -pltpu.roll(values, width - half, 1), pltpu.roll(values, half, 1))
    return jnp.where(lane < ROPE, values * cosine + swapped * sine_part, 0.0)


def put_quarters(values, targets, z):
    quarter = values.shape[0] // 4
    for n in range(4):
        for k in range(4):

            @pl.when(z ^ k == n)
            def _(n=n, k=k):
                targets[k][0] = values[n * quarter : (n + 1) * quarter]


def visible(info, shape, row_count):
    place = lax.broadcasted_iota(jnp.int32, shape, 0) + info[1] * row_count
    key = lax.broadcasted_iota(jnp.int32, shape, 1)
    end0 = info[4]
    end1 = info[4] + info[5]
    row_doc = (place >= end0).astype(jnp.int32) + (place >= end1).astype(jnp.int32)
    key_doc = (key >= end0).astype(jnp.int32) + (key >= end1).astype(jnp.int32)
    return (row_doc == key_doc) & (key <= place)


def attend(info, q_nope, q_rope, key_parts, pack, after):
    rows = q_nope.shape[0]
    db = pack.shape[3]
    columns = pl.ds(HEADS * (NOPE + ROPE), HEADS * VD + NOPE + VD)
    width = 32 * db
    tile = q_rope.shape[1]
    out = HEADS * VD
    keys = 16 * rows
    quarter = rows // 4
    rb = R // 32

    def kernel(info, qn, qr, *refs):
        key_ins, refs = refs[:2], refs[2:]
        pack_in, refs = refs[0], refs[1:]
        probs, cat, mixture, head_out, result, key_rows, weights, expand, scores, sem = refs
        start_all(pair_copies(key_ins, info[1] % 2, key_rows), sem.at[0])
        start_all(pack_copies(pack_in, columns, weights), sem.at[1])
        wait_for(weights, sem.at[1])
        for h in range(HEADS):
            expand[h] = weights[:, h * rb : (h + 1) * rb, out:].reshape(R, NOPE + VD)
        for h in range(HEADS):
            own = slice(h * rows, (h + 1) * rows)
            cat[own, :R] = nt(qn[:, h * NOPE : (h + 1) * NOPE], expand[h, :, :NOPE]).astype(bf16)
            cat[own, R:] = qr[own]
        wait_for(key_rows, sem.at[0])
        flat = key_rows[...].reshape(keys, R + tile)
        seen = visible(info, (rows, keys), rows)
        scale = (NOPE + ROPE) ** (-0.5)
        chunk = keys // 4
        for n in range(4):
            part = slice(n * chunk, (n + 1) * chunk)
            scores[:, part] = nt(cat[...], flat[part])
        for h in range(HEADS):
            own = slice(h * rows, (h + 1) * rows)
            score = jnp.where(seen, scale * scores[own], -1e30)
            weight = jnp.exp(score - jnp.max(score, axis=-1, keepdims=True))
            probs[own] = (weight / jnp.sum(weight, axis=-1, keepdims=True)).astype(bf16)
        mixture[...] = nn(probs[...], flat[:, :R]).astype(bf16)
        for h in range(HEADS):
            own = slice(h * rows, (h + 1) * rows)
            head_out[:, h * VD : (h + 1) * VD] = nn(mixture[own], expand[h, :, NOPE:]).astype(bf16)
        summed = nt(head_out[...], weights[:, :, :out].reshape(width, out)).astype(bf16)
        result[...] = summed.reshape(4, quarter, width)

    return call(
        kernel,
        [
            ((HEADS * rows, keys), bf16, "v"),
            ((HEADS * rows, R + tile), bf16, "v"),
            ((HEADS * rows, R), bf16, "v"),
            ((rows, out), bf16, "v"),
        ]
        + [((4, quarter, width), bf16, "v")],
        [(info, "s"), (q_nope, "v"), (q_rope, "v")]
        + [(part, "a") for part in key_parts + [pack]],
        [
            pltpu.VMEM((8, 2, rows, R + tile), bf16),
            pltpu.VMEM((32, db, out + NOPE + VD), bf16),
            pltpu.VMEM((HEADS, R, NOPE + VD), bf16),
            pltpu.VMEM((HEADS * rows, keys), f32),
            pltpu.SemaphoreType.DMA((2,)),
        ],
        macs=HEADS * rows * keys * (2 * R + tile) * 2,
        after=after,
    )


def quarter_norm(info, parts, tokens, small, after):
    _, quarter, width = parts.shape

    def kernel(info, came, tok, table, attention, normed):
        summed = came[0].astype(f32) + came[1].astype(f32) + came[2].astype(f32) + came[3].astype(f32)
        low = summed.astype(bf16)
        attention[0] = low
        middle = tok[info[3]].astype(f32) + low.astype(f32)
        inverse = lax.rsqrt(jnp.mean(middle * middle, axis=-1, keepdims=True) + epsilon)
        rows = (middle * inverse * table[1:2].astype(f32)).astype(bf16)
        for n in range(16):
            normed[n] = rows

    return call(
        kernel,
        [((1, quarter, width), bf16, "v"), ((16, quarter, width), bf16, "v")],
        [(info, "s"), (parts, "v"), (tokens.reshape(4, quarter, width), "v"), (small, "v")],
        [],
        after=after,
    )


def pass_on(from_one, from_three):
    half = from_one.shape[0] // 2
    return [swap(from_three[:half], ky=1), swap(from_one[half:], ky=3)]


def expert_copies(parts, me, targets, which):
    copies = []
    half = parts[3].shape[0]
    for part, ky, first in zip(parts, (0, 1, 3, 2, 2), (0, 0, 0, 0, half), strict=True):
        for i in range(part.shape[0]):
            block = first + i
            for target in targets:
                copies.append((part.at[i, which], target.at[me ^ mask(ky, block // 2, block % 2)]))
    return copies


def expert_rows(info, normed_parts, cots, weights, ff):
    _, quarter, width = normed_parts[0].shape
    extra = cots.shape[-1] - width
    db, wide = weights[0].shape[-2:]
    count = 32 * quarter
    step = count // 4
    lane0 = FF_PAD - extra

    def kernel(info, *refs):
        nref, refs = refs[:2], refs[2:]
        cref, wref, refs = refs[0], refs[1:6], refs[6:]
        act_out, grad_out, first, keep2, send2, x, g, wg, wu, wd, out1, out2, sem = refs
        half = step // quarter
        core_here = info[1] % 2

        def row_copies(i):
            core, at = i // 2, (i % 2) * half
            source = (core_here, 1 - core_here)[core]
            return (
                (nref[core].at[pl.ds(at, half)], x.at[core, pl.ds(at, half)]),
                (cref.at[pl.ds(at // 4, half // 4), source], g.at[core, pl.ds(at // 4, half // 4)]),
            )

        for n, (target, source) in enumerate(zip((wg, wu, wd), range(3), strict=True)):
            start_all(expert_copies(wref, info[0], (target,), source), sem.at[n])
            if n == 0:
                start_all(row_copies(0)[:1], sem.at[8])
            if n == 1:
                start_all(row_copies(0)[1:], sem.at[12])
        for i in range(1, 4):
            start_all(row_copies(i)[:1], sem.at[8 + i])
            start_all(row_copies(i)[1:], sem.at[12 + i])
        tile_lane = lanes((step, extra))
        lane = lanes((step, wide))

        def body(i, carry):
            own = pl.ds(pl.multiple_of(i * step, step), step)
            core, at = i // 2, (i % 2) * half
            here, there = x.at[core, pl.ds(at, half)], g.at[core, pl.ds(at // 4, half // 4)]
            wait_for(here, sem.at[8 + i])

            @pl.when(i == 0)
            def _():
                wait_for(wg, sem.at[0])

            rows = here[...].reshape(step, width)
            gate_pre = nn(rows, wg[...].reshape(width, wide))

            @pl.when(i == 0)
            def _():
                wait_for(wu, sem.at[1])

            up_pre = nn(rows, wu[...].reshape(width, wide))
            wait_for(there, sem.at[12 + i])

            @pl.when(i == 0)
            def _():
                wait_for(wd, sem.at[2])

            cot = there[...].reshape(step, width + extra)
            gate_weight = wg[...].reshape(width, wide)
            up_weight = wu[...].reshape(width, wide)
            down_weight = wd[...].reshape(width, wide)
            back = nn(cot[:, :width], down_weight)
            router = jax.nn.sigmoid(gate_pre[:, lane0:FF_PAD])
            weighted = router * cot[:, width:].astype(f32)
            gates = route_scale * weighted / jnp.sum(weighted, axis=1, keepdims=True)
            gate = jnp.sum(jnp.where(tile_lane == ff - lane0 + info[2], gates, 0.0), axis=1, keepdims=True)
            gate_row = jnp.where(lane < FF_PAD, gate, 1.0)
            sig = jax.nn.sigmoid(gate_pre)
            silu = gate_pre * sig
            act = silu * up_pre
            own_grad = jnp.sum(jnp.where(lane < FF_PAD, act * back, 0.0), axis=1, keepdims=True)
            act_low = (gate_row * act).astype(bf16)
            grad_act = gate_row * back
            grad_gate = (grad_act * up_pre * (sig * (1.0 + gate_pre * (1.0 - sig)))).astype(bf16)
            grad_up = (grad_act * silu).astype(bf16)
            act_out[own] = act_low
            grad_out[own, :wide] = grad_gate
            grad_out[own, wide:] = grad_up
            out1[own] = nt(act_low, down_weight).astype(bf16)
            out2[own, :width] = (nt(grad_gate, gate_weight) + nt(grad_up, up_weight)).astype(bf16)
            high = own_grad.astype(bf16).astype(f32)
            out2[own, width:] = (
                jnp.where(tile_lane == 8 + info[2], high, 0.0)
                + jnp.where(tile_lane == 24 + info[2], own_grad - high, 0.0)
            ).astype(bf16)
            of = jnp.where(core == 0, core_here, 1 - core_here)
            block = step // 2
            for n in range(2):
                part = pl.ds(pl.multiple_of(i * step + n * block, block), block)
                target = first.at[((i % 2) * 2 + n) * 2 + of]
                pltpu.make_async_copy(out1.at[part], target, sem.at[5]).start()

            @pl.when(core == 0)
            def _():
                pltpu.make_async_copy(out2.at[own], keep2.at[own], sem.at[3]).start()

            @pl.when(core == 1)
            def _():
                there = pl.ds(pl.multiple_of((i - 2) * step, step), step)
                pltpu.make_async_copy(out2.at[own], send2.at[there], sem.at[4]).start()

            return carry

        lax.fori_loop(0, 4, body, 0)
        wait_for(keep2, sem.at[3])
        wait_for(send2, sem.at[4])
        wait_for(first, sem.at[5])

    return call(
        kernel,
        [((count, wide), bf16, "v"), ((count, 2 * wide), bf16, "v")]
        + [((8, 4 * quarter, width), bf16, "a")]
        + [((count // 2, width + extra), bf16, "a")] * 2,
        [(info, "s")] + [(part, "a") for part in normed_parts + [cots] + weights],
        [
            pltpu.VMEM((2, 16, quarter, width), bf16),
            pltpu.VMEM((2, 4, 4, quarter, width + extra), bf16),
            pltpu.VMEM((32, db, wide), bf16),
            pltpu.VMEM((32, db, wide), bf16),
            pltpu.VMEM((32, db, wide), bf16),
            pltpu.VMEM((count, width), bf16),
            pltpu.VMEM((count, width + extra), bf16),
            pltpu.SemaphoreType.DMA((16,)),
        ],
        macs=6 * count * width * wide,
    )


def expert_weights(info, normed_parts, cots, act, grad_both, after):
    _, quarter, width = normed_parts[0].shape
    extra = cots.shape[-1] - width
    count, wide = act.shape
    db = width // 32
    step = width // 8
    blocks = step // db

    def kernel(info, *refs):
        nref, refs = refs[:2], refs[2:]
        cref, refs = refs[0], refs[1:]
        a, gb, *results, x, g, grads, sem = refs
        start_all([(cref.at[:, info[1] % 2], g.at[0]), (cref.at[:, 1 - info[1] % 2], g.at[1])], sem.at[0])
        start_all([(nref[0], x.at[0]), (nref[1], x.at[1])], sem.at[1])
        wait_for(g, sem.at[0])
        wait_for(x, sem.at[1])

        def body(i, carry):
            cols = pl.ds(pl.multiple_of(i * step, step), step)
            rows = x[:, :, :, cols].reshape(count, step)
            cot = g[:, :, :, :, cols].reshape(count, step)
            own = pl.ds(i * blocks, blocks)
            both = tn(rows, gb[...]).astype(bf16).reshape(blocks, db, 2 * wide)
            grads[own, 0] = both[:, :, :wide]
            grads[own, 1] = both[:, :, wide:]
            grads[own, 2] = tn(cot, a[...]).astype(bf16).reshape(blocks, db, wide)
            return carry

        lax.fori_loop(0, 8, body, 0)
        for ky in range(4):
            for kx in range(4):
                for kc in (0, 1):
                    pltpu.make_async_copy(
                        grads.at[info[0] ^ mask(ky, kx, kc)], results[2 * ky + kx // 2].at[kx % 2, kc], sem.at[2]
                    ).start()
        for result in results:
            wait_for(result, sem.at[2])

    return call(
        kernel,
        [((2, 2, 3, db, wide), bf16, "a")] * 8,
        [(info, "s")]
        + [(part, "a") for part in normed_parts + [cots]]
        + [(act, "v"), (grad_both, "v")],
        [
            pltpu.VMEM((2, 16, quarter, width), bf16),
            pltpu.VMEM((2, 4, 4, quarter, width + extra), bf16),
            pltpu.VMEM((32, 3, db, wide), bf16),
            pltpu.SemaphoreType.DMA((3,)),
        ],
        macs=3 * count * width * wide,
        after=after,
    )


def quarter_copies(parts, z, target, columns=None):
    if columns is None:
        return [(part.at[0], target.at[z ^ k]) for k, part in enumerate(parts)]
    return [(part.at[0, :, columns], target.at[z ^ k]) for k, part in enumerate(parts)]


def attend_back(
    info, tokens, cotangent, picked, att_parts, grad_parts, small, probs, cat, key_parts, pack2, cos4,
    sin4, after,
):
    rows, width = tokens.shape
    quarter = rows // 4
    db = width // 32
    rb = R // 32
    tile = cat.shape[1] - R
    out = HEADS * VD
    keys = 16 * rows
    query = HEADS * (NOPE + ROPE)
    half = ROPE // 2
    extra = grad_parts[0].shape[-1] - width
    scale = (NOPE + ROPE) ** (-0.5)
    late = out + NOPE + VD

    def kernel(info, tok, cotan, pick, table, pr, ca, cos, sin, *refs):
        att_in, refs = refs[:4], refs[4:]
        grad_in, refs = refs[:4], refs[4:]
        key_in, refs = refs[:2], refs[2:]
        in2, refs = refs[0], refs[1:]
        (
            grad_middle, small_grads, key_keep, key_send, grad_att, grad_heads, grad_abs, grad_q,
            att, arrived, key_rows, w2, expand, grad_mix, grad_scores, key_grads, wide, sem,
        ) = refs
        start_all(quarter_copies(grad_in, info[3], arrived), sem.at[0])
        start_all(quarter_copies(att_in, info[3], att), sem.at[1])
        start_all(pack_copies(in2, pl.ds(query, late), w2), sem.at[2])
        start_all(pair_copies(key_in, info[1] % 2, key_rows), sem.at[3])
        wait_for(arrived, sem.at[0])
        wait_for(att, sem.at[1])
        middle = tok[...].astype(f32) + att[...].reshape(rows, width).astype(f32)
        inverse = lax.rsqrt(jnp.mean(middle * middle, axis=-1, keepdims=True) + epsilon)
        unit = middle * inverse
        gain = table[1:2].astype(f32)
        normed = (unit * gain).astype(bf16)
        came = arrived[...].reshape(rows, width + extra)
        sig = jax.nn.sigmoid(nt(normed, table[...]))
        chosen = pick[...]
        weighted = sig * chosen
        gate_total = jnp.sum(weighted, axis=1, keepdims=True)
        gates = route_scale * weighted / gate_total
        grad_gates = came[:, width : width + 16].astype(f32) + came[:, width + 16 : width + 32].astype(f32)
        grad_weighted = (route_scale * grad_gates - jnp.sum(grad_gates * gates, axis=1, keepdims=True)) / gate_total
        grad_logits = grad_weighted * chosen * sig * (1.0 - sig)
        high, low = high_low(grad_logits)
        grads = tn(high, normed) + tn(low, normed)
        grad_normed = came[:, :width].astype(f32) + nn(high, table[...]) + nn(low, table[...])
        scaled = grad_normed * gain
        grad_mid = cotan[...].astype(f32) + inverse * (
            scaled - unit * jnp.mean(scaled * unit, axis=-1, keepdims=True)
        )
        d_gain = jnp.sum(grad_normed * unit, axis=0, keepdims=True)
        row16 = lax.broadcasted_iota(jnp.int32, (16, width), 0)
        small_grads[...] = jnp.where(row16 >= 8, grads, jnp.where(row16 == 1, d_gain, 0.0))
        grad_middle[...] = grad_mid
        grad_att[...] = grad_mid.astype(bf16)
        wait_for(w2, sem.at[2])
        for h in range(HEADS):
            expand[h] = w2[:, h * rb : (h + 1) * rb, out:].reshape(R, NOPE + VD)
        grad_heads[...] = nn(grad_att[...], w2[:, :, :out].reshape(width, out)).astype(bf16)
        for h in range(HEADS):
            own = slice(h * rows, (h + 1) * rows)
            grad_mix[own] = nt(grad_heads[:, h * VD : (h + 1) * VD], expand[h, :, NOPE:]).astype(bf16)
        wait_for(key_rows, sem.at[3])
        flat = key_rows[...].reshape(keys, R + tile)
        lane = lanes((rows, tile))
        front = jnp.zeros((rows, tile), f32)
        back = jnp.zeros((rows, tile), f32)
        chunk = keys // 4
        for n in range(4):
            part = slice(n * chunk, (n + 1) * chunk)
            wide[:, part] = nt(grad_mix[...], flat[part, :R])
        for h in range(HEADS):
            own = slice(h * rows, (h + 1) * rows)
            grad_prob = wide[own]
            prob = pr[own].astype(f32)
            inner = jnp.sum(prob * grad_prob, axis=-1, keepdims=True)
            grad_scores[own] = (prob * (grad_prob - inner)).astype(bf16)
        grad_cat = scale * nn(grad_scores[...], flat)
        grad_abs[...] = grad_cat[:, :R].astype(bf16)
        for h in range(HEADS):
            own = slice(h * rows, (h + 1) * rows)
            grad_q[:, h * NOPE : (h + 1) * NOPE] = nn(grad_abs[own], expand[h, :, :NOPE]).astype(bf16)
            turned = grad_cat[own, R:]
            inside = (lane >= h * half) & (lane < (h + 1) * half)
            front = jnp.where(inside, pltpu.roll(turned, (h * half) % tile, 1), front)
            back = jnp.where(inside, pltpu.roll(turned, (h * half + tile - half) % tile, 1), back)
        grad_q[:, HEADS * NOPE : HEADS * NOPE + tile] = (front * cos[...] + back * sin[...]).astype(bf16)
        grad_q[:, HEADS * NOPE + tile :] = (back * cos[...] - front * sin[...]).astype(bf16)
        chunk = keys // 4
        for n in range(4):
            cols = slice(n * chunk, (n + 1) * chunk)
            part = scale * tn(grad_scores[:, cols], ca[...])
            latent = part[:, :R] + tn(pr[:, cols], grad_mix[...])
            own = slice(n * 2, (n + 1) * 2)
            key_grads[own, :, :, :R] = latent.astype(bf16).reshape(2, 2, rows, R)
            key_grads[own, :, :, R:] = part[:, R:].astype(bf16).reshape(2, 2, rows, tile)
        core = info[1] % 2
        pltpu.make_async_copy(key_grads.at[:, core], key_keep, sem.at[5]).start()
        pltpu.make_async_copy(key_grads.at[:, 1 - core], key_send, sem.at[6]).start()
        wait_for(key_keep, sem.at[5])
        wait_for(key_send, sem.at[6])

    vmem_ins = [tokens, cotangent, picked, small, probs, cat, cos4, sin4]
    return call(
        kernel,
        [
            ((rows, width), f32, "v"),
            ((16, width), f32, "v"),
            ((8, rows, R + tile), bf16, "a"),
            ((8, rows, R + tile), bf16, "a"),
            ((rows, width), bf16, "v"),
            ((rows, out), bf16, "v"),
            ((HEADS * rows, R), bf16, "v"),
            ((rows, query), bf16, "v"),
        ],
        [(info, "s")]
        + [(array, "v") for array in vmem_ins]
        + [(part, "a") for part in att_parts + grad_parts + key_parts + [pack2]],
        [
            pltpu.VMEM((4, quarter, width), bf16),
            pltpu.VMEM((4, quarter, width + extra), bf16),
            pltpu.VMEM((8, 2, rows, R + tile), bf16),
            pltpu.VMEM((32, db, late), bf16),
            pltpu.VMEM((HEADS, R, NOPE + VD), bf16),
            pltpu.VMEM((HEADS * rows, R), bf16),
            pltpu.VMEM((HEADS * rows, keys), bf16),
            pltpu.VMEM((8, 2, rows, R + tile), bf16),
            pltpu.VMEM((HEADS * rows, keys), f32),
            pltpu.SemaphoreType.DMA((7,)),
        ],
        macs=HEADS * rows * keys * (4 * R + 2 * tile) * 2,
        after=after,
    )


def attention_weights(info, grad_att, grad_heads, grad_abs, grad_q, hidden, head_out, mixture, q_nope, pack, after):
    rows, width = hidden.shape
    quarter = rows // 4
    db = width // 32
    rb = R // 32
    out = HEADS * VD
    late = out + NOPE + VD
    query = HEADS * (NOPE + ROPE)

    def kernel(info, ga, gh, gb, gq, hid, ho, mix, qn, *refs):
        packed, hid0, hid1, hid2, hid3, result, w1, grads, sem = refs
        start_all(pack_copies(packed, pl.ds(0, query), w1), sem.at[0])
        grads[:, :, :, :out] = tn(ga[...], ho[...]).astype(bf16).reshape(16, 2, db, out)
        for h in range(HEADS):
            part = slice(h * rows, (h + 1) * rows)
            here = slice(h * rb, (h + 1) * rb)
            grads[:, :, here, out : out + NOPE] = (
                tn(gb[part], qn[:, h * NOPE : (h + 1) * NOPE]).astype(bf16).reshape(16, 2, rb, NOPE)
            )
            grads[:, :, here, out + NOPE : late] = (
                tn(mix[part], gh[:, h * VD : (h + 1) * VD]).astype(bf16).reshape(16, 2, rb, VD)
            )
        grads[:, :, :, late:] = tn(hid[...], gq[...]).astype(bf16).reshape(16, 2, db, query)
        for n in range(16):
            for core in (0, 1):
                target = result.at[(n % 4) * 2 + core, ((n // 4) % 2) * 2 + n // 8]
                pltpu.make_async_copy(grads.at[n, core], target, sem.at[1]).start()
        wait_for(w1, sem.at[0])
        put_quarters(nt(gq[...], w1[...].reshape(width, query)).astype(bf16), (hid0, hid1, hid2, hid3), info[3])
        wait_for(result, sem.at[1])

    vmem_ins = [grad_att, grad_heads, grad_abs, grad_q, hidden, head_out, mixture, q_nope]
    return call(
        kernel,
        [((1, quarter, width), bf16, "v")] * 4 + [((8, 4, db, late + query), bf16, "a")],
        [(info, "s")] + [(array, "v") for array in vmem_ins] + [(pack, "a")],
        [
            pltpu.VMEM((32, db, query), bf16),
            pltpu.VMEM((16, 2, db, late + query), bf16),
            pltpu.SemaphoreType.DMA((2,)),
        ],
        macs=rows * width * (out + 2 * query) + 2 * HEADS * R * rows * NOPE,
        after=after,
    )


def finish(
    info, tokens, grad_middle, hidden, latent, gain_latent, small, small_grads, key_parts, att_parts, sum_parts,
    parts1, cos4, sin4, after,
):
    rows, width = tokens.shape
    quarter = rows // 4
    db = width // 32
    rb = R // 32
    tile = latent.shape[1] - R
    query = HEADS * (NOPE + ROPE)

    def kernel(info, tok, gm, hid, lat, gl, table, sg, cos, sin, *refs):
        key_in, refs = refs[:4], refs[4:]
        att_in, refs = refs[:4], refs[4:]
        sum_in, refs = refs[:4], refs[4:]
        in1, refs = refs[: len(parts1)], refs[len(parts1) :]
        output, d_tokens, keep, send, own_keys, part, att, sums, w1, grads, sem = refs
        start_all(quarter_copies(key_in, info[3], own_keys), sem.at[6])
        start_all(pair_copies(in1, info[1] % 2, w1), sem.at[0])
        start_all(quarter_copies(sum_in, info[3], part, pl.ds(0, width)), sem.at[1])
        start_all(quarter_copies(att_in, info[3], att), sem.at[2])
        start_all(quarter_copies(sum_in, info[3], sums, pl.ds(width, width)), sem.at[3])
        wait_for(own_keys, sem.at[6])
        own = own_keys[...].reshape(rows, R + tile)
        plain = lat[:, :R]
        inverse = lax.rsqrt(jnp.mean(plain * plain, axis=-1, keepdims=True) + epsilon)
        unit = plain * inverse
        grad_y = own[:, :R]
        scaled = grad_y * gl[...]
        d_gain_latent = jnp.sum(grad_y * unit, axis=0, keepdims=True)
        grad_in = inverse * (scaled - unit * jnp.mean(scaled * unit, axis=-1, keepdims=True))
        grad_latent = jnp.concatenate([grad_in, turn(own[:, R:], cos[...], -sin[...])], axis=1).astype(bf16)
        d_latent = tn(hid[...], grad_latent).astype(bf16)
        grads[...] = d_latent.reshape(16, 2, db, R + tile)
        wait_for(w1, sem.at[0])
        wait_for(part, sem.at[1])
        x = tok[...].astype(f32)
        inverse = lax.rsqrt(jnp.mean(x * x, axis=-1, keepdims=True) + epsilon)
        unit = x * inverse
        grad_hidden = part[...].reshape(rows, width).astype(f32) + nt(
            grad_latent, w1[...].reshape(width, R + tile)
        )
        scaled = grad_hidden * table[0:1].astype(f32)
        d_tokens[...] = gm[...] + inverse * (scaled - unit * jnp.mean(scaled * unit, axis=-1, keepdims=True))
        d_gain = jnp.sum(grad_hidden * unit, axis=0, keepdims=True)
        row16 = lax.broadcasted_iota(jnp.int32, (16, width), 0)
        every = jnp.where(row16 == 0, d_gain, sg[...])
        lane = lanes((16, tile))
        row = lax.broadcasted_iota(jnp.int32, (16, tile), 0)
        per = tile // rb
        for j in range(32):
            t = j // 2
            values = every[:, t * tile : (t + 1) * tile]
            if j % 2 == 0:
                values = pltpu.roll(values, db, 1)
            gains = d_gain_latent[:, (j // per) * tile : (j // per + 1) * tile]
            gains = pltpu.roll(gains, (db + tile - (j % per) * rb) % tile, 1)
            values = jnp.where(row == 2, jnp.where(lane < db + rb, gains, 0.0), values)
            before = grads[j // 2, j % 2, 0:16, R:].astype(f32)
            grads[j // 2, j % 2, 0:16, R:] = jnp.where(lane < db, before, values).astype(bf16)
        core = info[1] % 2
        rows_here = pl.ds(pl.multiple_of(info[3] * (db // 4), db // 4), db // 4)
        pltpu.make_async_copy(grads.at[:, core, rows_here], keep, sem.at[4]).start()
        pltpu.make_async_copy(grads.at[:, 1 - core, rows_here], send, sem.at[5]).start()
        wait_for(att, sem.at[2])
        wait_for(sums, sem.at[3])
        middle = x + att[...].reshape(rows, width).astype(f32)
        output[...] = (middle + sums[...].reshape(rows, width).astype(f32)).astype(bf16)
        wait_for(keep, sem.at[4])
        wait_for(send, sem.at[5])

    vmem_ins = [tokens, grad_middle, hidden, latent, gain_latent, small, small_grads, cos4, sin4]
    return call(
        kernel,
        [
            ((rows, width), bf16, "v"),
            ((rows, width), f32, "v"),
            ((16, db // 4, R + tile), bf16, "a"),
            ((16, db // 4, R + tile), bf16, "a"),
        ],
        [(info, "s")]
        + [(array, "v") for array in vmem_ins]
        + [(part, "a") for part in key_parts + att_parts + sum_parts + parts1],
        [
            pltpu.VMEM((4, quarter, R + tile), f32),
            pltpu.VMEM((4, quarter, width), bf16),
            pltpu.VMEM((4, quarter, width), bf16),
            pltpu.VMEM((4, quarter, width), bf16),
            pltpu.VMEM((16, 2, db, R + tile), bf16),
            pltpu.VMEM((16, 2, db, R + tile), bf16),
            pltpu.SemaphoreType.DMA((7,)),
        ],
        macs=4 * rows * width * (R + tile),
        after=after,
    )


def unpack_experts(info, own, other, ff, sh):
    _, _, db, wide = other.shape

    def kernel(info, a0, a1, a2, a3, b, gate, up, down, sg, su, sd, slots, sem):
        for kx, a in enumerate((a0, a1, a2, a3)):
            pltpu.make_async_copy(a.at[0], slots.at[info[2] ^ (kx * 2)], sem).start()
            pltpu.make_async_copy(b.at[kx], slots.at[info[2] ^ (kx * 2 + 1)], sem).start()
        wait_for(slots, sem)
        for n, (routed, shared) in enumerate(((gate, sg), (up, su), (down, sd))):
            for e in range(8):
                routed[e] = slots[e, n, :, :ff].astype(f32)
            shared[...] = jnp.concatenate(
                [slots[e, n, :, FF_PAD : FF_PAD + sh].astype(f32) for e in range(8)], axis=1
            )

    return call(
        kernel,
        [((8, db, ff), f32, "v")] * 3 + [((db, 8 * sh), f32, "v")] * 3,
        [(info, "s")] + [(part, "a") for part in own] + [(other, "a")],
        [pltpu.VMEM((8, 3, db, wide), bf16), pltpu.SemaphoreType.DMA(())],
    )


def unpack_rest(info, parts):
    _, quarter, columns = parts[0].shape
    db = 4 * quarter
    rb = R // 32

    def kernel(info, a, b, c, d, latent, gain_attn, gain_moe, gain_latent, router_t, block):
        for k, part in enumerate((a, b, c, d)):
            block[info[3] ^ k] = part[0].astype(f32)
        whole = block[...].reshape(db, columns)
        latent[...] = whole[:, : R + ROPE]
        small = whole[0:16, R + ROPE :]
        gain_attn[...] = small[0:1]
        gain_moe[...] = small[1:2]
        gain_latent[...] = small[2:3, :rb]
        router_t[...] = small[8:16]

    return call(
        kernel,
        [
            ((db, R + ROPE), f32, "v"),
            ((1, db), f32, "v"),
            ((1, db), f32, "v"),
            ((1, rb), f32, "v"),
            ((8, db), f32, "v"),
        ],
        [(info, "s")] + [(part, "v") for part in parts],
        [pltpu.VMEM((4, quarter, columns), f32)],
    )


def unpack_attention(grads):
    db, _ = grads.shape
    rb = R // 32
    out = HEADS * VD
    late = out + NOPE + VD
    per_head, half = NOPE + ROPE, ROPE // 2

    def kernel(g, d_out, d_expand, d_query):
        d_out[...] = g[:, :out].astype(f32)
        for h in range(HEADS):
            d_expand[:, h * (NOPE + VD) : (h + 1) * (NOPE + VD)] = g[h * rb : (h + 1) * rb, out:late].astype(f32)
            plain = g[:, late + h * NOPE : late + (h + 1) * NOPE].astype(f32)
            front = late + HEADS * NOPE + h * half
            back = front + HEADS * half
            d_query[:, h * per_head : (h + 1) * per_head] = jnp.concatenate(
                [plain, g[:, front : front + half].astype(f32), g[:, back : back + half].astype(f32)], axis=1
            )

    return call(
        kernel,
        [
            ((db, out), f32, "v"),
            ((rb, HEADS * (NOPE + VD)), f32, "v"),
            ((db, HEADS * per_head), f32, "v"),
        ],
        [(grads, "v")],
        [],
    )


def shards(
    tokens,
    lengths,
    routes,
    cotangent,
    attn_gain,
    w_query,
    w_latent,
    latent_gain,
    w_expand,
    w_out,
    moe_gain,
    w_router,
    w_gate,
    w_up,
    w_down,
    shared_gate,
    shared_up,
    shared_down,
):
    me = lax.axis_index(PLANE)
    place = me % 16
    member = me % 8
    z = lax.axis_index("z")
    rows, width = tokens.shape
    quarter = rows // 4
    db = width // 32
    rb = R // 32
    ff, sh = w_gate.shape[2], shared_gate.shape[1] // 8
    tile = ROPE + db
    query = HEADS * (NOPE + ROPE)
    half = ROPE // 2
    extra = min(128, FF_PAD)
    wide = FF_PAD + SH_PAD
    info = jnp.concatenate([jnp.stack([me, place, member, z]).astype(jnp.int32), lengths[0]])

    one, two = pack_attention(
        w_query, w_latent, attn_gain, moe_gain, latent_gain, w_router.T, w_out.T, w_expand
    )
    pack = lax.all_gather(two, ("yh", "yl", "x", "c"), axis=0).reshape(2, 2, 8, db, -1)
    keep, send = pack_experts(
        info, w_gate, w_up, jnp.swapaxes(w_down, 1, 2), shared_gate, shared_up, shared_down.T, w_router
    )
    came = swap(send, kc=1)
    by_x = [jnp.stack([keep[k], came[k]]) for k in range(4)]
    latent_parts = gather(one, ("yl", "yh", "x"), ())

    position = place * rows + jnp.arange(rows, dtype=jnp.int32)
    ends = jnp.stack([lengths[0, 0], lengths[0, 0] + lengths[0, 1]])
    start = jnp.where(position >= ends[1], ends[1], jnp.where(position >= ends[0], ends[0], 0))
    frequency = rope_base ** (-jnp.arange(half, dtype=f32) / half)
    angles = (position - start).astype(f32)[:, None] * jnp.tile(frequency, 2 * HEADS * half // ROPE)[None, :]
    cos4, sin4 = jnp.cos(angles), jnp.sin(angles)
    picked = jnp.sum(
        (routes[:, :, None] == jnp.arange(16, dtype=jnp.int32)[None, None, :] - 8).astype(f32), axis=1
    )
    lane_pick = jnp.sum(
        (routes[:, :, None] == jnp.arange(extra, dtype=jnp.int32)[None, None, :] - (ff - FF_PAD + extra)), axis=1
    ).astype(bf16)

    hidden, keys, latent, small, gain_latent = project_latent(info, tokens, cos4, sin4, latent_parts)
    mine = jnp.concatenate([by_x[0]] + [swap(by_x[k], kx=k) for k in (1, 2, 3)])
    weights = [mine] + [swap(mine, ky=k) for k in (1, 3)]
    q_nope, q_rope = project_query(hidden, cos4, sin4, pack)
    keys = hold(exchange(hold(keys, mine), ("yh", "x")), q_nope)
    key_parts = [keys, swap(keys, kc=1)]
    cots = hold(jnp.concatenate([cotangent, lane_pick], axis=1), key_parts[0])
    cots = lax.all_gather(cots, ("x", "c"), axis=0).reshape(4, 2, 4, quarter, width + extra)
    probs, cat, mixture, head_out, attention = attend(info, q_nope, q_rope, key_parts, pack, ())
    attention = hold(exchange(attention, "z"), weights[1], weights[2])
    own_attention, normed = quarter_norm(info, attention, tokens, small, ())
    weights += pass_on(*weights[1:])
    normed_parts = gather(normed, ("x", "z"), weights[3:])
    att_parts = [own_attention] + [swap_z(own_attention, k) for k in (1, 2, 3)]

    act, grad_both, first, keep2, send2 = expert_rows(
        info, normed_parts, cots, weights, ff
    )

    def scattered(values):
        return exchange(values.reshape(16, quarter, -1), ("x", "z"))

    def collect(values):
        return jnp.sum(values.astype(f32), axis=0, keepdims=True).astype(bf16)

    second = total([keep2, swap(send2, kc=1)])
    d_experts = expert_weights(info, normed_parts, cots, act, grad_both, (second,))
    opposite3, opposite1 = swap(d_experts[4], ky=1), swap(d_experts[5], ky=3)
    straight3, straight1 = swap(d_experts[7], ky=3), swap(d_experts[2], ky=1)
    second = collect(hold(scattered(second), d_experts[0]))
    onward3 = total([hold(d_experts[6], second), opposite3])
    onward1 = total([hold(d_experts[3], second), opposite1])
    first = lax.psum_scatter(first, ("x", "c"), scatter_dimension=0).reshape(4, quarter, width)
    first = lax.psum_scatter(first, "z", scatter_dimension=0)[None]
    onward3, onward1 = swap(onward3, ky=3), swap(onward1, ky=1)
    grad_parts = [second] + [swap_z(second, k) for k in (1, 2, 3)]

    grad_middle, small_grads, key_keep, key_send, grad_att, grad_heads, grad_abs, grad_q = attend_back(
        info, tokens, cotangent, picked, att_parts, grad_parts, small, probs, cat, key_parts, pack, cos4, sin4,
        (straight3, straight1),
    )
    *hidden_part, most = attention_weights(
        info, grad_att, grad_heads, grad_abs, grad_q, hidden, head_out, mixture, q_nope, pack, (onward3, onward1)
    )
    grad_keys = total([key_keep, swap(hold(key_send, onward3, onward1), kc=1)]).reshape(32, quarter, R + tile)
    grad_keys = exchange(grad_keys, ("yh", "x", "z"))
    grad_hidden = total([hidden_part[0]] + [swap_z(hidden_part[k], k) for k in (1, 2, 3)])
    sums = jnp.concatenate([grad_hidden, first], axis=2)
    sum_parts = [sums] + [swap_z(sums, k) for k in (1, 2, 3)]
    grad_keys = hold(grad_keys, *sum_parts[1:])


    most = lax.psum_scatter(most, ("x", "c"), scatter_dimension=0)
    grad_keys = jnp.sum(grad_keys.astype(f32), axis=0, keepdims=True)
    grad_key_parts = [grad_keys] + [swap_z(grad_keys, k) for k in (1, 2, 3)]
    d_mine = [
        total([part[k % 2] for part in (d_experts[k // 2], (onward3, straight3)[k // 2], (straight1, onward1)[k // 2])])
        for k in range(4)
    ]

    d_mine = [hold(part, grad_keys) for part in d_mine]
    d_mine[1], d_mine[3] = swap(d_mine[1], kx=1), swap(d_mine[3], kx=3)
    output, d_tokens, keep, send = finish(
        info, tokens, grad_middle, hidden, latent, gain_latent, small, small_grads, grad_key_parts, att_parts,
        sum_parts, latent_parts, cos4, sin4, (d_mine[1], d_mine[3]),
    )
    most = lax.psum_scatter(hold(most, keep), ("yh", "yl"), scatter_dimension=0)
    rest = total([keep, swap(send, kc=1)])
    d_mine[2] = swap(hold(d_mine[2], d_tokens), kx=2)
    rest = exchange(rest, ("yl", "yh", "x"))
    d_other = swap(jnp.stack([part[1] for part in d_mine]), kc=1)
    d_routed = unpack_experts(info, d_mine, d_other, ff, sh)
    rest = collect(hold(rest, d_routed[0]))
    d_out, d_expand, d_query = unpack_attention(most)
    d_latent, d_attn_gain, d_moe_gain, d_latent_gain, d_router_t = unpack_rest(
        info, [rest] + [swap_z(rest, k) for k in (1, 2, 3)]
    )
    return (
        output,
        d_tokens,
        d_attn_gain[0],
        d_query,
        d_latent,
        d_latent_gain[0],
        d_expand,
        d_out.T,
        d_moe_gain[0],
        d_router_t.T,
        d_routed[0],
        d_routed[1],
        jnp.swapaxes(d_routed[2], 1, 2),
        d_routed[3],
        d_routed[4],
        d_routed[5].T,
    )


def solution(mesh):
    rows = P(PLANE, None)
    split = P(PLANE, "z")
    vector = P(PLANE)
    turned = P("z", PLANE)
    expert_rows = P(None, PLANE, "z")
    expert_columns = P(None, "z", PLANE)
    fine = Mesh(mesh.devices.reshape(2, 2, 4, 2, 4), ("yl", "yh", "x", "c", "z"))
    return jax.shard_map(
        shards,
        mesh=fine,
        in_specs=(
            rows,
            P("yl", None),
            rows,
            rows,
            vector,
            split,
            rows,
            vector,
            split,
            turned,
            vector,
            rows,
            expert_rows,
            expert_rows,
            expert_columns,
            split,
            split,
            turned,
        ),
        out_specs=(
            rows,
            rows,
            vector,
            split,
            rows,
            vector,
            split,
            turned,
            vector,
            rows,
            expert_rows,
            expert_rows,
            expert_columns,
            split,
            split,
            turned,
        ),
        check_vma=False,
    )
```

```python
import math

import jax
import jax.numpy as jnp
from jax import lax
from jax.experimental import pallas as pl
from jax.experimental.pallas import tpu as pltpu
from jax.sharding import Mesh
from jax.sharding import PartitionSpec as P

NOPE = 128
ROPE = 64
VD = 128
R = 512
E = 8
FF_PAD = 384
SH_PAD = 128
HEADS = 4

epsilon = 1e-06
rope_base = 50000.0
route_scale = 2.446
bf16 = jnp.bfloat16
f32 = jnp.float32

PLANE = ("yl", "yh", "x", "c")
YS = ("yl", "yh")


def mask(ky=0, kx=0, kc=0):
    return (ky & 1) * 16 + (ky >> 1) * 8 + kx * 2 + kc


def swap(values, ky=0, kx=0, kc=0):
    bits = mask(ky, kx, kc)
    return lax.ppermute(values, PLANE, [(i, i ^ bits) for i in range(32)])


def swap_z(values, k):
    return lax.ppermute(values, "z", [(i, i ^ k) for i in range(4)])


def total(parts, dtype=bf16):
    out = parts[0].astype(f32)
    for part in parts[1:]:
        out = out + part.astype(f32)
    return out.astype(dtype)


def nn(left, right):
    return jnp.dot(left, right, preferred_element_type=f32)


def nt(left, right):
    return lax.dot_general(left, right, (((1,), (1,)), ((), ())), preferred_element_type=f32)


def tn(left, right):
    return lax.dot_general(left, right, (((0,), (0,)), ((), ())), preferred_element_type=f32)


def lanes(shape):
    return lax.broadcasted_iota(jnp.int32, shape, 1)


def high_low(values):
    high = values.astype(bf16)
    return high, (values - high.astype(f32)).astype(bf16)


def start_all(copies, sem):
    for source, destination in copies:
        pltpu.make_async_copy(source, destination, sem).start()


def wait_for(ref, sem):
    pltpu.make_async_copy(ref, ref, sem).wait()


def call(kernel, outs, ins, scratch, macs=0, vmem=63, after=()):
    count, late = len(ins), len(after)
    body = kernel
    if late:

        def body(*refs):
            kernel(*refs[:count], *refs[count + late :])

    moved = sum(array.size * array.dtype.itemsize for array, _ in ins)
    moved += sum(math.prod(shape) * jnp.dtype(dtype).itemsize for shape, dtype, _ in outs)
    spaces = {"s": pltpu.SMEM, "v": pltpu.VMEM, "a": pl.ANY}
    return pl.pallas_call(
        body,
        out_shape=[jax.ShapeDtypeStruct(shape, dtype) for shape, dtype, _ in outs],
        in_specs=[pl.BlockSpec(memory_space=spaces[space]) for _, space in ins]
        + [pl.BlockSpec(memory_space=pl.ANY)] * late,
        out_specs=[pl.BlockSpec(memory_space=spaces[space]) for _, _, space in outs],
        scratch_shapes=scratch,
        compiler_params=pltpu.CompilerParams(vmem_limit_bytes=vmem << 20),
        cost_estimate=pl.CostEstimate(flops=4 * macs, bytes_accessed=moved, transcendentals=0),
    )(*[array for array, _ in ins], *after)


def exchange(blocks, axes):
    return lax.all_to_all(blocks, axes, 0, 0, tiled=True)


def gather(copies, axes, after):
    own = hold(exchange(copies, axes), *after)
    return [own, swap(own, kc=1)]


def pair_copies(parts, core, target, columns=None):
    if columns is not None:
        parts = [part.at[:, :, columns] for part in parts]
    return [(parts[0], target.at[:, core]), (parts[1], target.at[:, 1 - core])]


def pack_copies(pack, columns, target):
    return [
        (pack.at[yh, yl, :, :, columns], target.at[pl.ds(yl * 16 + yh * 8, 8)]) for yh in (0, 1) for yl in (0, 1)
    ]


def hold(values, *after):
    def kernel(*refs):
        pass

    return pl.pallas_call(
        kernel,
        out_shape=jax.ShapeDtypeStruct(values.shape, values.dtype),
        in_specs=[pl.BlockSpec(memory_space=pl.ANY)] * (1 + len(after)),
        out_specs=pl.BlockSpec(memory_space=pl.ANY),
        input_output_aliases={0: 0},
    )(values, *after)


def pack_attention(w_query, w_latent, attn_gain, moe_gain, latent_gain, router_t, out_t, w_expand):
    db = w_query.shape[0]
    query = w_query.shape[1]
    late = w_latent.shape[1]
    out = out_t.shape[1]
    per_head = NOPE + ROPE

    def kernel(q, lat, ag, mg, lg, rt, ot, ex, first, second):
        plain = [q[:, h * per_head : h * per_head + NOPE] for h in range(HEADS)]
        front = [q[:, h * per_head + NOPE : h * per_head + NOPE + ROPE // 2] for h in range(HEADS)]
        back = [q[:, h * per_head + NOPE + ROPE // 2 : (h + 1) * per_head] for h in range(HEADS)]
        rb = lg.shape[1]
        small = jnp.concatenate(
            [
                ag[...].astype(f32),
                mg[...].astype(f32),
                jnp.concatenate([lg[...].astype(f32), jnp.zeros((1, db - rb), f32)], axis=1),
                jnp.zeros((5, db), f32),
                rt[...].astype(f32),
            ]
            + ([jnp.zeros((db - 16, db), f32)] if db > 16 else []),
            axis=0,
        ).astype(bf16)
        one = jnp.concatenate([lat[...], small], axis=1)
        for n in range(16):
            first[n] = one
        width = ex.shape[1] // HEADS
        expand = jnp.concatenate([ex[:, h * width : (h + 1) * width] for h in range(HEADS)], axis=0)
        second[...] = jnp.concatenate(plain + front + back + [ot[...], expand], axis=1)

    two = query + out + w_expand.shape[1] // HEADS
    ins = [w_query, w_latent, attn_gain[None], moe_gain[None], latent_gain[None], router_t, out_t, w_expand]
    return call(
        kernel,
        [((16, db, late + db), bf16, "v"), ((db, two), bf16, "v")],
        [(array, "v") for array in ins],
        [],
    )


def pack_experts(info, gate, up, down_t, shared_gate, shared_up, shared_down_t, router):
    count, db, ff = gate.shape
    sh = shared_gate.shape[1] // count
    wide = FF_PAD + SH_PAD

    def kernel(info, g, u, d, sg, su, sd, rt, keep, send, packed, sem):
        fill = FF_PAD - ff - count
        for n, (routed, shared) in enumerate(((g, sg), (u, su), (d, sd))):
            extra = rt[...] if n == 0 else jnp.zeros((db, count), bf16)
            for e in range(count):
                packed[e, n] = jnp.concatenate(
                    [
                        routed[e],
                        extra,
                        jnp.zeros((db, fill), bf16),
                        shared[:, e * sh : (e + 1) * sh],
                        jnp.zeros((db, SH_PAD - sh), bf16),
                    ],
                    axis=1,
                )
        copies = []
        for kx in range(4):
            copies.append((packed.at[info[2] ^ (kx * 2)], keep.at[kx], sem.at[0]))
            copies.append((packed.at[info[2] ^ (kx * 2 + 1)], send.at[kx], sem.at[1]))
        for source, destination, which in copies:
            pltpu.make_async_copy(source, destination, which).start()
        wait_for(keep, sem.at[0])
        wait_for(send, sem.at[1])

    ins = [gate, up, down_t, shared_gate, shared_up, shared_down_t, router]
    return call(
        kernel,
        [((4, 3, db, wide), bf16, "a")] * 2,
        [(info, "s")] + [(array, "v") for array in ins],
        [pltpu.VMEM((count, 3, db, wide), bf16), pltpu.SemaphoreType.DMA((2,))],
    )


def project_latent(info, tokens, cos4, sin4, parts):
    rows, width = tokens.shape
    db = width // 32
    rb = R // 32
    tile = ROPE + db

    def kernel(info, tok, cos, sin, own, other, hidden, keys, latent_out, small, gain_row, pairs, sem):
        start_all(pair_copies((own, other), info[1] % 2, pairs), sem)
        x = tok[...].astype(f32)
        inverse = lax.rsqrt(jnp.mean(x * x, axis=-1, keepdims=True) + epsilon)
        unit = x * inverse
        wait_for(pairs, sem)
        weights = pairs.reshape(32, db, R + tile)
        lane = lanes((16, tile))
        tiles = []
        for t in range(16):
            even = weights[2 * t, 0:16, R:].astype(f32)
            odd = weights[2 * t + 1, 0:16, R:].astype(f32)
            tiles.append(jnp.where(lane < db, pltpu.roll(even, tile - db, 1), odd))
        table = jnp.concatenate(tiles, axis=1)
        small[...] = table.astype(bf16)
        lane = lanes((1, tile))
        per = tile // rb
        pieces = []
        for t in range(32 // per):
            piece = jnp.zeros((1, tile), f32)
            for i in range(per):
                row = weights[t * per + i, 0:16, R:].astype(f32)[2:3]
                piece = jnp.where(lane // rb == i, pltpu.roll(row, (i * rb + tile - db) % tile, 1), piece)
            pieces.append(piece)
        gain_latent = jnp.concatenate(pieces, axis=1)
        gain_row[...] = gain_latent
        low = (unit * table[0:1]).astype(bf16)
        hidden[...] = low
        late = nn(low, weights[...].reshape(width, R + tile))
        latent_out[...] = late
        plain = late[:, :R]
        inverse = lax.rsqrt(jnp.mean(plain * plain, axis=-1, keepdims=True) + epsilon)
        key = jnp.concatenate(
            [plain * inverse * gain_latent, turn(late[:, R:], cos[...], sin[...])], axis=1
        ).astype(bf16)
        for n in range(8):
            keys[n] = key

    return call(
        kernel,
        [
            ((rows, width), bf16, "v"),
            ((8, rows, R + tile), bf16, "v"),
            ((rows, R + tile), f32, "v"),
            ((16, width), bf16, "v"),
            ((1, R), f32, "v"),
        ],
        [(info, "s"), (tokens, "v"), (cos4, "v"), (sin4, "v")] + [(part, "a") for part in parts],
        [pltpu.VMEM((16, 2, db, R + tile), bf16), pltpu.SemaphoreType.DMA(())],
        macs=rows * width * (R + tile),
    )


def project_query(hidden, cos4, sin4, pack):
    rows, width = hidden.shape
    db = width // 32
    query = HEADS * (NOPE + ROPE)
    tile = ROPE + db
    half = ROPE // 2

    def kernel(hid, cos, sin, packed, q_nope, q_rope, weights, sem):
        start_all(pack_copies(packed, pl.ds(0, query), weights), sem)
        wait_for(weights, sem)
        raw = nn(hid[...], weights[...].reshape(width, query))
        q_nope[...] = raw[:, : HEADS * NOPE].astype(bf16)
        front = raw[:, HEADS * NOPE : HEADS * NOPE + tile]
        back = raw[:, HEADS * NOPE + tile :]
        turned_front = front * cos[...] - back * sin[...]
        turned_back = back * cos[...] + front * sin[...]
        lane = lanes((rows, tile))
        for h in range(HEADS):
            head = jnp.where(
                lane < half,
                pltpu.roll(turned_front, (tile - h * half) % tile, 1),
                jnp.where(lane < ROPE, pltpu.roll(turned_back, (tile - h * half + half) % tile, 1), 0.0),
            )
            q_rope[h * rows : (h + 1) * rows] = head.astype(bf16)

    return call(
        kernel,
        [((rows, HEADS * NOPE), bf16, "v"), ((HEADS * rows, tile), bf16, "v")],
        [(hidden, "v"), (cos4, "v"), (sin4, "v"), (pack, "a")],
        [pltpu.VMEM((32, db, query), bf16), pltpu.SemaphoreType.DMA(())],
        macs=rows * width * query,
    )


def turn(values, cosine, sine_part):
    width = values.shape[1]
    half = ROPE // 2
    lane = lanes(values.shape)
    swapped = jnp.where(lane < half, -pltpu.roll(values, width - half, 1), pltpu.roll(values, half, 1))
    return jnp.where(lane < ROPE, values * cosine + swapped * sine_part, 0.0)


def put_quarters(values, targets, z):
    quarter = values.shape[0] // 4
    for n in range(4):
        for k in range(4):

            @pl.when(z ^ k == n)
            def _(n=n, k=k):
                targets[k][0] = values[n * quarter : (n + 1) * quarter]


def visible(info, shape, row_count):
    place = lax.broadcasted_iota(jnp.int32, shape, 0) + info[1] * row_count
    key = lax.broadcasted_iota(jnp.int32, shape, 1)
    end0 = info[4]
    end1 = info[4] + info[5]
    row_doc = (place >= end0).astype(jnp.int32) + (place >= end1).astype(jnp.int32)
    key_doc = (key >= end0).astype(jnp.int32) + (key >= end1).astype(jnp.int32)
    return (row_doc == key_doc) & (key <= place)


def attend(info, q_nope, q_rope, key_parts, pack, after):
    rows = q_nope.shape[0]
    db = pack.shape[3]
    columns = pl.ds(HEADS * (NOPE + ROPE), HEADS * VD + NOPE + VD)
    width = 32 * db
    tile = q_rope.shape[1]
    out = HEADS * VD
    keys = 16 * rows
    quarter = rows // 4
    rb = R // 32

    def kernel(info, qn, qr, *refs):
        key_ins, refs = refs[:2], refs[2:]
        pack_in, refs = refs[0], refs[1:]
        probs, cat, mixture, head_out, result, key_rows, weights, expand, scores, sem = refs
        start_all(pair_copies(key_ins, info[1] % 2, key_rows), sem.at[0])
        start_all(pack_copies(pack_in, columns, weights), sem.at[1])
        wait_for(weights, sem.at[1])
        for h in range(HEADS):
            expand[h] = weights[:, h * rb : (h + 1) * rb, out:].reshape(R, NOPE + VD)
        for h in range(HEADS):
            own = slice(h * rows, (h + 1) * rows)
            cat[own, :R] = nt(qn[:, h * NOPE : (h + 1) * NOPE], expand[h, :, :NOPE]).astype(bf16)
            cat[own, R:] = qr[own]
        wait_for(key_rows, sem.at[0])
        flat = key_rows[...].reshape(keys, R + tile)
        seen = visible(info, (rows, keys), rows)
        scale = (NOPE + ROPE) ** (-0.5)
        chunk = keys // 4
        for n in range(4):
            part = slice(n * chunk, (n + 1) * chunk)
            scores[:, part] = nt(cat[...], flat[part])
        for h in range(HEADS):
            own = slice(h * rows, (h + 1) * rows)
            score = jnp.where(seen, scale * scores[own], -1e30)
            weight = jnp.exp(score - jnp.max(score, axis=-1, keepdims=True))
            probs[own] = (weight / jnp.sum(weight, axis=-1, keepdims=True)).astype(bf16)
        mixture[...] = nn(probs[...], flat[:, :R]).astype(bf16)
        for h in range(HEADS):
            own = slice(h * rows, (h + 1) * rows)
            head_out[:, h * VD : (h + 1) * VD] = nn(mixture[own], expand[h, :, NOPE:]).astype(bf16)
        summed = nt(head_out[...], weights[:, :, :out].reshape(width, out)).astype(bf16)
        result[...] = summed.reshape(4, quarter, width)

    return call(
        kernel,
        [
            ((HEADS * rows, keys), bf16, "v"),
            ((HEADS * rows, R + tile), bf16, "v"),
            ((HEADS * rows, R), bf16, "v"),
            ((rows, out), bf16, "v"),
        ]
        + [((4, quarter, width), bf16, "v")],
        [(info, "s"), (q_nope, "v"), (q_rope, "v")]
        + [(part, "a") for part in key_parts + [pack]],
        [
            pltpu.VMEM((8, 2, rows, R + tile), bf16),
            pltpu.VMEM((32, db, out + NOPE + VD), bf16),
            pltpu.VMEM((HEADS, R, NOPE + VD), bf16),
            pltpu.VMEM((HEADS * rows, keys), f32),
            pltpu.SemaphoreType.DMA((2,)),
        ],
        macs=HEADS * rows * keys * (2 * R + tile) * 2,
        after=after,
    )


def quarter_norm(info, parts, tokens, small, after):
    _, quarter, width = parts.shape

    def kernel(info, came, tok, table, attention, normed):
        summed = came[0].astype(f32) + came[1].astype(f32) + came[2].astype(f32) + came[3].astype(f32)
        low = summed.astype(bf16)
        attention[0] = low
        middle = tok[info[3]].astype(f32) + low.astype(f32)
        inverse = lax.rsqrt(jnp.mean(middle * middle, axis=-1, keepdims=True) + epsilon)
        rows = (middle * inverse * table[1:2].astype(f32)).astype(bf16)
        for n in range(16):
            normed[n] = rows

    return call(
        kernel,
        [((1, quarter, width), bf16, "v"), ((16, quarter, width), bf16, "v")],
        [(info, "s"), (parts, "v"), (tokens.reshape(4, quarter, width), "v"), (small, "v")],
        [],
        after=after,
    )


def pass_on(from_one, from_three):
    half = from_one.shape[0] // 2
    return [swap(from_three[:half], ky=1), swap(from_one[half:], ky=3)]


def expert_copies(parts, me, targets, which):
    copies = []
    half = parts[3].shape[0]
    for part, ky, first in zip(parts, (0, 1, 3, 2, 2), (0, 0, 0, 0, half), strict=True):
        for i in range(part.shape[0]):
            block = first + i
            for target in targets:
                copies.append((part.at[i, which], target.at[me ^ mask(ky, block // 2, block % 2)]))
    return copies


def expert_rows(info, normed_parts, cots, weights, ff):
    _, quarter, width = normed_parts[0].shape
    extra = cots.shape[-1] - width
    db, wide = weights[0].shape[-2:]
    count = 32 * quarter
    step = count // 4
    lane0 = FF_PAD - extra

    def kernel(info, *refs):
        nref, refs = refs[:2], refs[2:]
        cref, wref, refs = refs[0], refs[1:6], refs[6:]
        act_out, grad_out, first, keep2, send2, x, g, wg, wu, wd, out1, out2, sem = refs
        half = step // quarter
        core_here = info[1] % 2

        def row_copies(i):
            core, at = i // 2, (i % 2) * half
            source = (core_here, 1 - core_here)[core]
            return (
                (nref[core].at[pl.ds(at, half)], x.at[core, pl.ds(at, half)]),
                (cref.at[pl.ds(at // 4, half // 4), source], g.at[core, pl.ds(at // 4, half // 4)]),
            )

        for n, (target, source) in enumerate(zip((wg, wu, wd), range(3), strict=True)):
            start_all(expert_copies(wref, info[0], (target,), source), sem.at[n])
            if n == 0:
                start_all(row_copies(0)[:1], sem.at[8])
            if n == 1:
                start_all(row_copies(0)[1:], sem.at[12])
        for i in range(1, 4):
            start_all(row_copies(i)[:1], sem.at[8 + i])
            start_all(row_copies(i)[1:], sem.at[12 + i])
        tile_lane = lanes((step, extra))
        lane = lanes((step, wide))

        def body(i, carry):
            own = pl.ds(pl.multiple_of(i * step, step), step)
            core, at = i // 2, (i % 2) * half
            here, there = x.at[core, pl.ds(at, half)], g.at[core, pl.ds(at // 4, half // 4)]
            wait_for(here, sem.at[8 + i])

            @pl.when(i == 0)
            def _():
                wait_for(wg, sem.at[0])

            rows = here[...].reshape(step, width)
            gate_pre = nn(rows, wg[...].reshape(width, wide))

            @pl.when(i == 0)
            def _():
                wait_for(wu, sem.at[1])

            up_pre = nn(rows, wu[...].reshape(width, wide))
            wait_for(there, sem.at[12 + i])

            @pl.when(i == 0)
            def _():
                wait_for(wd, sem.at[2])

            cot = there[...].reshape(step, width + extra)
            gate_weight = wg[...].reshape(width, wide)
            up_weight = wu[...].reshape(width, wide)
            down_weight = wd[...].reshape(width, wide)
            back = nn(cot[:, :width], down_weight)
            router = jax.nn.sigmoid(gate_pre[:, lane0:FF_PAD])
            weighted = router * cot[:, width:].astype(f32)
            gates = route_scale * weighted / jnp.sum(weighted, axis=1, keepdims=True)
            gate = jnp.sum(jnp.where(tile_lane == ff - lane0 + info[2], gates, 0.0), axis=1, keepdims=True)
            gate_row = jnp.where(lane < FF_PAD, gate, 1.0)
            sig = jax.nn.sigmoid(gate_pre)
            silu = gate_pre * sig
            act = silu * up_pre
            own_grad = jnp.sum(jnp.where(lane < FF_PAD, act * back, 0.0), axis=1, keepdims=True)
            act_low = (gate_row * act).astype(bf16)
            grad_act = gate_row * back
            grad_gate = (grad_act * up_pre * (sig * (1.0 + gate_pre * (1.0 - sig)))).astype(bf16)
            grad_up = (grad_act * silu).astype(bf16)
            act_out[own] = act_low
            grad_out[own, :wide] = grad_gate
            grad_out[own, wide:] = grad_up
            out1[own] = nt(act_low, down_weight).astype(bf16)
            out2[own, :width] = (nt(grad_gate, gate_weight) + nt(grad_up, up_weight)).astype(bf16)
            high = own_grad.astype(bf16).astype(f32)
            out2[own, width:] = (
                jnp.where(tile_lane == 8 + info[2], high, 0.0)
                + jnp.where(tile_lane == 24 + info[2], own_grad - high, 0.0)
            ).astype(bf16)
            of = jnp.where(core == 0, core_here, 1 - core_here)
            block = step // 2
            for n in range(2):
                part = pl.ds(pl.multiple_of(i * step + n * block, block), block)
                target = first.at[((i % 2) * 2 + n) * 2 + of]
                pltpu.make_async_copy(out1.at[part], target, sem.at[5]).start()

            @pl.when(core == 0)
            def _():
                pltpu.make_async_copy(out2.at[own], keep2.at[own], sem.at[3]).start()

            @pl.when(core == 1)
            def _():
                there = pl.ds(pl.multiple_of((i - 2) * step, step), step)
                pltpu.make_async_copy(out2.at[own], send2.at[there], sem.at[4]).start()

            return carry

        lax.fori_loop(0, 4, body, 0)
        wait_for(keep2, sem.at[3])
        wait_for(send2, sem.at[4])
        wait_for(first, sem.at[5])

    return call(
        kernel,
        [((count, wide), bf16, "v"), ((count, 2 * wide), bf16, "v")]
        + [((8, 4 * quarter, width), bf16, "a")]
        + [((count // 2, width + extra), bf16, "a")] * 2,
        [(info, "s")] + [(part, "a") for part in normed_parts + [cots] + weights],
        [
            pltpu.VMEM((2, 16, quarter, width), bf16),
            pltpu.VMEM((2, 4, 4, quarter, width + extra), bf16),
            pltpu.VMEM((32, db, wide), bf16),
            pltpu.VMEM((32, db, wide), bf16),
            pltpu.VMEM((32, db, wide), bf16),
            pltpu.VMEM((count, width), bf16),
            pltpu.VMEM((count, width + extra), bf16),
            pltpu.SemaphoreType.DMA((16,)),
        ],
        macs=6 * count * width * wide,
    )


def expert_weights(info, normed_parts, cots, act, grad_both, after):
    _, quarter, width = normed_parts[0].shape
    extra = cots.shape[-1] - width
    count, wide = act.shape
    db = width // 32
    step = width // 8
    blocks = step // db

    def kernel(info, *refs):
        nref, refs = refs[:2], refs[2:]
        cref, refs = refs[0], refs[1:]
        a, gb, *results, x, g, grads, sem = refs
        start_all([(cref.at[:, info[1] % 2], g.at[0]), (cref.at[:, 1 - info[1] % 2], g.at[1])], sem.at[0])
        start_all([(nref[0], x.at[0]), (nref[1], x.at[1])], sem.at[1])
        wait_for(g, sem.at[0])
        wait_for(x, sem.at[1])

        def body(i, carry):
            cols = pl.ds(pl.multiple_of(i * step, step), step)
            rows = x[:, :, :, cols].reshape(count, step)
            cot = g[:, :, :, :, cols].reshape(count, step)
            own = pl.ds(i * blocks, blocks)
            both = tn(rows, gb[...]).astype(bf16).reshape(blocks, db, 2 * wide)
            grads[own, 0] = both[:, :, :wide]
            grads[own, 1] = both[:, :, wide:]
            grads[own, 2] = tn(cot, a[...]).astype(bf16).reshape(blocks, db, wide)
            return carry

        lax.fori_loop(0, 8, body, 0)
        for ky in range(4):
            for kx in range(4):
                for kc in (0, 1):
                    pltpu.make_async_copy(
                        grads.at[info[0] ^ mask(ky, kx, kc)], results[2 * ky + kx // 2].at[kx % 2, kc], sem.at[2]
                    ).start()
        for result in results:
            wait_for(result, sem.at[2])

    return call(
        kernel,
        [((2, 2, 3, db, wide), bf16, "a")] * 8,
        [(info, "s")]
        + [(part, "a") for part in normed_parts + [cots]]
        + [(act, "v"), (grad_both, "v")],
        [
            pltpu.VMEM((2, 16, quarter, width), bf16),
            pltpu.VMEM((2, 4, 4, quarter, width + extra), bf16),
            pltpu.VMEM((32, 3, db, wide), bf16),
            pltpu.SemaphoreType.DMA((3,)),
        ],
        macs=3 * count * width * wide,
        after=after,
    )


def quarter_copies(parts, z, target, columns=None):
    if columns is None:
        return [(part.at[0], target.at[z ^ k]) for k, part in enumerate(parts)]
    return [(part.at[0, :, columns], target.at[z ^ k]) for k, part in enumerate(parts)]


def attend_back(
    info, tokens, cotangent, picked, att_parts, grad_parts, small, probs, cat, key_parts, pack2, cos4,
    sin4, after,
):
    rows, width = tokens.shape
    quarter = rows // 4
    db = width // 32
    rb = R // 32
    tile = cat.shape[1] - R
    out = HEADS * VD
    keys = 16 * rows
    query = HEADS * (NOPE + ROPE)
    half = ROPE // 2
    extra = grad_parts[0].shape[-1] - width
    scale = (NOPE + ROPE) ** (-0.5)
    late = out + NOPE + VD

    def kernel(info, tok, cotan, pick, table, pr, ca, cos, sin, *refs):
        att_in, refs = refs[:4], refs[4:]
        grad_in, refs = refs[:4], refs[4:]
        key_in, refs = refs[:2], refs[2:]
        in2, refs = refs[0], refs[1:]
        (
            grad_middle, small_grads, key_keep, key_send, grad_att, grad_heads, grad_abs, grad_q,
            att, arrived, key_rows, w2, expand, grad_mix, grad_scores, key_grads, wide, sem,
        ) = refs
        start_all(quarter_copies(grad_in, info[3], arrived), sem.at[0])
        start_all(quarter_copies(att_in, info[3], att), sem.at[1])
        start_all(pack_copies(in2, pl.ds(query, late), w2), sem.at[2])
        start_all(pair_copies(key_in, info[1] % 2, key_rows), sem.at[3])
        wait_for(arrived, sem.at[0])
        wait_for(att, sem.at[1])
        middle = tok[...].astype(f32) + att[...].reshape(rows, width).astype(f32)
        inverse = lax.rsqrt(jnp.mean(middle * middle, axis=-1, keepdims=True) + epsilon)
        unit = middle * inverse
        gain = table[1:2].astype(f32)
        normed = (unit * gain).astype(bf16)
        came = arrived[...].reshape(rows, width + extra)
        sig = jax.nn.sigmoid(nt(normed, table[...]))
        chosen = pick[...]
        weighted = sig * chosen
        gate_total = jnp.sum(weighted, axis=1, keepdims=True)
        gates = route_scale * weighted / gate_total
        grad_gates = came[:, width : width + 16].astype(f32) + came[:, width + 16 : width + 32].astype(f32)
        grad_weighted = (route_scale * grad_gates - jnp.sum(grad_gates * gates, axis=1, keepdims=True)) / gate_total
        grad_logits = grad_weighted * chosen * sig * (1.0 - sig)
        high, low = high_low(grad_logits)
        grads = tn(high, normed) + tn(low, normed)
        grad_normed = came[:, :width].astype(f32) + nn(high, table[...]) + nn(low, table[...])
        scaled = grad_normed * gain
        grad_mid = cotan[...].astype(f32) + inverse * (
            scaled - unit * jnp.mean(scaled * unit, axis=-1, keepdims=True)
        )
        d_gain = jnp.sum(grad_normed * unit, axis=0, keepdims=True)
        row16 = lax.broadcasted_iota(jnp.int32, (16, width), 0)
        small_grads[...] = jnp.where(row16 >= 8, grads, jnp.where(row16 == 1, d_gain, 0.0))
        grad_middle[...] = grad_mid
        grad_att[...] = grad_mid.astype(bf16)
        wait_for(w2, sem.at[2])
        for h in range(HEADS):
            expand[h] = w2[:, h * rb : (h + 1) * rb, out:].reshape(R, NOPE + VD)
        grad_heads[...] = nn(grad_att[...], w2[:, :, :out].reshape(width, out)).astype(bf16)
        for h in range(HEADS):
            own = slice(h * rows, (h + 1) * rows)
            grad_mix[own] = nt(grad_heads[:, h * VD : (h + 1) * VD], expand[h, :, NOPE:]).astype(bf16)
        wait_for(key_rows, sem.at[3])
        flat = key_rows[...].reshape(keys, R + tile)
        lane = lanes((rows, tile))
        front = jnp.zeros((rows, tile), f32)
        back = jnp.zeros((rows, tile), f32)
        chunk = keys // 4
        for n in range(4):
            part = slice(n * chunk, (n + 1) * chunk)
            wide[:, part] = nt(grad_mix[...], flat[part, :R])
        for h in range(HEADS):
            own = slice(h * rows, (h + 1) * rows)
            grad_prob = wide[own]
            prob = pr[own].astype(f32)
            inner = jnp.sum(prob * grad_prob, axis=-1, keepdims=True)
            grad_scores[own] = (prob * (grad_prob - inner)).astype(bf16)
        grad_cat = scale * nn(grad_scores[...], flat)
        grad_abs[...] = grad_cat[:, :R].astype(bf16)
        for h in range(HEADS):
            own = slice(h * rows, (h + 1) * rows)
            grad_q[:, h * NOPE : (h + 1) * NOPE] = nn(grad_abs[own], expand[h, :, :NOPE]).astype(bf16)
            turned = grad_cat[own, R:]
            inside = (lane >= h * half) & (lane < (h + 1) * half)
            front = jnp.where(inside, pltpu.roll(turned, (h * half) % tile, 1), front)
            back = jnp.where(inside, pltpu.roll(turned, (h * half + tile - half) % tile, 1), back)
        grad_q[:, HEADS * NOPE : HEADS * NOPE + tile] = (front * cos[...] + back * sin[...]).astype(bf16)
        grad_q[:, HEADS * NOPE + tile :] = (back * cos[...] - front * sin[...]).astype(bf16)
        chunk = keys // 4
        for n in range(4):
            cols = slice(n * chunk, (n + 1) * chunk)
            part = scale * tn(grad_scores[:, cols], ca[...])
            latent = part[:, :R] + tn(pr[:, cols], grad_mix[...])
            own = slice(n * 2, (n + 1) * 2)
            key_grads[own, :, :, :R] = latent.astype(bf16).reshape(2, 2, rows, R)
            key_grads[own, :, :, R:] = part[:, R:].astype(bf16).reshape(2, 2, rows, tile)
        core = info[1] % 2
        pltpu.make_async_copy(key_grads.at[:, core], key_keep, sem.at[5]).start()
        pltpu.make_async_copy(key_grads.at[:, 1 - core], key_send, sem.at[6]).start()
        wait_for(key_keep, sem.at[5])
        wait_for(key_send, sem.at[6])

    vmem_ins = [tokens, cotangent, picked, small, probs, cat, cos4, sin4]
    return call(
        kernel,
        [
            ((rows, width), f32, "v"),
            ((16, width), f32, "v"),
            ((8, rows, R + tile), bf16, "a"),
            ((8, rows, R + tile), bf16, "a"),
            ((rows, width), bf16, "v"),
            ((rows, out), bf16, "v"),
            ((HEADS * rows, R), bf16, "v"),
            ((rows, query), bf16, "v"),
        ],
        [(info, "s")]
        + [(array, "v") for array in vmem_ins]
        + [(part, "a") for part in att_parts + grad_parts + key_parts + [pack2]],
        [
            pltpu.VMEM((4, quarter, width), bf16),
            pltpu.VMEM((4, quarter, width + extra), bf16),
            pltpu.VMEM((8, 2, rows, R + tile), bf16),
            pltpu.VMEM((32, db, late), bf16),
            pltpu.VMEM((HEADS, R, NOPE + VD), bf16),
            pltpu.VMEM((HEADS * rows, R), bf16),
            pltpu.VMEM((HEADS * rows, keys), bf16),
            pltpu.VMEM((8, 2, rows, R + tile), bf16),
            pltpu.VMEM((HEADS * rows, keys), f32),
            pltpu.SemaphoreType.DMA((7,)),
        ],
        macs=HEADS * rows * keys * (4 * R + 2 * tile) * 2,
        after=after,
    )


def attention_weights(info, grad_att, grad_heads, grad_abs, grad_q, hidden, head_out, mixture, q_nope, pack, after):
    rows, width = hidden.shape
    quarter = rows // 4
    db = width // 32
    rb = R // 32
    out = HEADS * VD
    late = out + NOPE + VD
    query = HEADS * (NOPE + ROPE)

    def kernel(info, ga, gh, gb, gq, hid, ho, mix, qn, *refs):
        packed, hid0, hid1, hid2, hid3, result, w1, grads, sem = refs
        start_all(pack_copies(packed, pl.ds(0, query), w1), sem.at[0])
        grads[:, :, :, :out] = tn(ga[...], ho[...]).astype(bf16).reshape(16, 2, db, out)
        for h in range(HEADS):
            part = slice(h * rows, (h + 1) * rows)
            here = slice(h * rb, (h + 1) * rb)
            grads[:, :, here, out : out + NOPE] = (
                tn(gb[part], qn[:, h * NOPE : (h + 1) * NOPE]).astype(bf16).reshape(16, 2, rb, NOPE)
            )
            grads[:, :, here, out + NOPE : late] = (
                tn(mix[part], gh[:, h * VD : (h + 1) * VD]).astype(bf16).reshape(16, 2, rb, VD)
            )
        grads[:, :, :, late:] = tn(hid[...], gq[...]).astype(bf16).reshape(16, 2, db, query)
        for n in range(16):
            for core in (0, 1):
                target = result.at[(n % 4) * 2 + core, ((n // 4) % 2) * 2 + n // 8]
                pltpu.make_async_copy(grads.at[n, core], target, sem.at[1]).start()
        wait_for(w1, sem.at[0])
        put_quarters(nt(gq[...], w1[...].reshape(width, query)).astype(bf16), (hid0, hid1, hid2, hid3), info[3])
        wait_for(result, sem.at[1])

    vmem_ins = [grad_att, grad_heads, grad_abs, grad_q, hidden, head_out, mixture, q_nope]
    return call(
        kernel,
        [((1, quarter, width), bf16, "v")] * 4 + [((8, 4, db, late + query), bf16, "a")],
        [(info, "s")] + [(array, "v") for array in vmem_ins] + [(pack, "a")],
        [
            pltpu.VMEM((32, db, query), bf16),
            pltpu.VMEM((16, 2, db, late + query), bf16),
            pltpu.SemaphoreType.DMA((2,)),
        ],
        macs=rows * width * (out + 2 * query) + 2 * HEADS * R * rows * NOPE,
        after=after,
    )


def finish(
    info, tokens, grad_middle, hidden, latent, gain_latent, small, small_grads, key_parts, att_parts, sum_parts,
    parts1, cos4, sin4, after,
):
    rows, width = tokens.shape
    quarter = rows // 4
    db = width // 32
    rb = R // 32
    tile = latent.shape[1] - R
    query = HEADS * (NOPE + ROPE)

    def kernel(info, tok, gm, hid, lat, gl, table, sg, cos, sin, *refs):
        key_in, refs = refs[:4], refs[4:]
        att_in, refs = refs[:4], refs[4:]
        sum_in, refs = refs[:4], refs[4:]
        in1, refs = refs[: len(parts1)], refs[len(parts1) :]
        output, d_tokens, keep, send, own_keys, part, att, sums, w1, grads, sem = refs
        start_all(quarter_copies(key_in, info[3], own_keys), sem.at[6])
        start_all(pair_copies(in1, info[1] % 2, w1), sem.at[0])
        start_all(quarter_copies(sum_in, info[3], part, pl.ds(0, width)), sem.at[1])
        start_all(quarter_copies(att_in, info[3], att), sem.at[2])
        start_all(quarter_copies(sum_in, info[3], sums, pl.ds(width, width)), sem.at[3])
        wait_for(own_keys, sem.at[6])
        own = own_keys[...].reshape(rows, R + tile)
        plain = lat[:, :R]
        inverse = lax.rsqrt(jnp.mean(plain * plain, axis=-1, keepdims=True) + epsilon)
        unit = plain * inverse
        grad_y = own[:, :R]
        scaled = grad_y * gl[...]
        d_gain_latent = jnp.sum(grad_y * unit, axis=0, keepdims=True)
        grad_in = inverse * (scaled - unit * jnp.mean(scaled * unit, axis=-1, keepdims=True))
        grad_latent = jnp.concatenate([grad_in, turn(own[:, R:], cos[...], -sin[...])], axis=1).astype(bf16)
        d_latent = tn(hid[...], grad_latent).astype(bf16)
        grads[...] = d_latent.reshape(16, 2, db, R + tile)
        wait_for(w1, sem.at[0])
        wait_for(part, sem.at[1])
        x = tok[...].astype(f32)
        inverse = lax.rsqrt(jnp.mean(x * x, axis=-1, keepdims=True) + epsilon)
        unit = x * inverse
        grad_hidden = part[...].reshape(rows, width).astype(f32) + nt(
            grad_latent, w1[...].reshape(width, R + tile)
        )
        scaled = grad_hidden * table[0:1].astype(f32)
        d_tokens[...] = gm[...] + inverse * (scaled - unit * jnp.mean(scaled * unit, axis=-1, keepdims=True))
        d_gain = jnp.sum(grad_hidden * unit, axis=0, keepdims=True)
        row16 = lax.broadcasted_iota(jnp.int32, (16, width), 0)
        every = jnp.where(row16 == 0, d_gain, sg[...])
        lane = lanes((16, tile))
        row = lax.broadcasted_iota(jnp.int32, (16, tile), 0)
        per = tile // rb
        for j in range(32):
            t = j // 2
            values = every[:, t * tile : (t + 1) * tile]
            if j % 2 == 0:
                values = pltpu.roll(values, db, 1)
            gains = d_gain_latent[:, (j // per) * tile : (j // per + 1) * tile]
            gains = pltpu.roll(gains, (db + tile - (j % per) * rb) % tile, 1)
            values = jnp.where(row == 2, jnp.where(lane < db + rb, gains, 0.0), values)
            before = grads[j // 2, j % 2, 0:16, R:].astype(f32)
            grads[j // 2, j % 2, 0:16, R:] = jnp.where(lane < db, before, values).astype(bf16)
        core = info[1] % 2
        rows_here = pl.ds(pl.multiple_of(info[3] * (db // 4), db // 4), db // 4)
        pltpu.make_async_copy(grads.at[:, core, rows_here], keep, sem.at[4]).start()
        pltpu.make_async_copy(grads.at[:, 1 - core, rows_here], send, sem.at[5]).start()
        wait_for(att, sem.at[2])
        wait_for(sums, sem.at[3])
        middle = x + att[...].reshape(rows, width).astype(f32)
        output[...] = (middle + sums[...].reshape(rows, width).astype(f32)).astype(bf16)
        wait_for(keep, sem.at[4])
        wait_for(send, sem.at[5])

    vmem_ins = [tokens, grad_middle, hidden, latent, gain_latent, small, small_grads, cos4, sin4]
    return call(
        kernel,
        [
            ((rows, width), bf16, "v"),
            ((rows, width), f32, "v"),
            ((16, db // 4, R + tile), bf16, "a"),
            ((16, db // 4, R + tile), bf16, "a"),
        ],
        [(info, "s")]
        + [(array, "v") for array in vmem_ins]
        + [(part, "a") for part in key_parts + att_parts + sum_parts + parts1],
        [
            pltpu.VMEM((4, quarter, R + tile), f32),
            pltpu.VMEM((4, quarter, width), bf16),
            pltpu.VMEM((4, quarter, width), bf16),
            pltpu.VMEM((4, quarter, width), bf16),
            pltpu.VMEM((16, 2, db, R + tile), bf16),
            pltpu.VMEM((16, 2, db, R + tile), bf16),
            pltpu.SemaphoreType.DMA((7,)),
        ],
        macs=4 * rows * width * (R + tile),
        after=after,
    )


def unpack_experts(info, own, other, ff, sh):
    _, _, db, wide = other.shape

    def kernel(info, a0, a1, a2, a3, b, gate, up, down, sg, su, sd, slots, sem):
        for kx, a in enumerate((a0, a1, a2, a3)):
            pltpu.make_async_copy(a.at[0], slots.at[info[2] ^ (kx * 2)], sem).start()
            pltpu.make_async_copy(b.at[kx], slots.at[info[2] ^ (kx * 2 + 1)], sem).start()
        wait_for(slots, sem)
        for n, (routed, shared) in enumerate(((gate, sg), (up, su), (down, sd))):
            for e in range(8):
                routed[e] = slots[e, n, :, :ff].astype(f32)
            shared[...] = jnp.concatenate(
                [slots[e, n, :, FF_PAD : FF_PAD + sh].astype(f32) for e in range(8)], axis=1
            )

    return call(
        kernel,
        [((8, db, ff), f32, "v")] * 3 + [((db, 8 * sh), f32, "v")] * 3,
        [(info, "s")] + [(part, "a") for part in own] + [(other, "a")],
        [pltpu.VMEM((8, 3, db, wide), bf16), pltpu.SemaphoreType.DMA(())],
    )


def unpack_rest(info, parts):
    _, quarter, columns = parts[0].shape
    db = 4 * quarter
    rb = R // 32

    def kernel(info, a, b, c, d, latent, gain_attn, gain_moe, gain_latent, router_t, block):
        for k, part in enumerate((a, b, c, d)):
            block[info[3] ^ k] = part[0].astype(f32)
        whole = block[...].reshape(db, columns)
        latent[...] = whole[:, : R + ROPE]
        small = whole[0:16, R + ROPE :]
        gain_attn[...] = small[0:1]
        gain_moe[...] = small[1:2]
        gain_latent[...] = small[2:3, :rb]
        router_t[...] = small[8:16]

    return call(
        kernel,
        [
            ((db, R + ROPE), f32, "v"),
            ((1, db), f32, "v"),
            ((1, db), f32, "v"),
            ((1, rb), f32, "v"),
            ((8, db), f32, "v"),
        ],
        [(info, "s")] + [(part, "v") for part in parts],
        [pltpu.VMEM((4, quarter, columns), f32)],
    )


def unpack_attention(grads):
    db, _ = grads.shape
    rb = R // 32
    out = HEADS * VD
    late = out + NOPE + VD
    per_head, half = NOPE + ROPE, ROPE // 2

    def kernel(g, d_out, d_expand, d_query):
        d_out[...] = g[:, :out].astype(f32)
        for h in range(HEADS):
            d_expand[:, h * (NOPE + VD) : (h + 1) * (NOPE + VD)] = g[h * rb : (h + 1) * rb, out:late].astype(f32)
            plain = g[:, late + h * NOPE : late + (h + 1) * NOPE].astype(f32)
            front = late + HEADS * NOPE + h * half
            back = front + HEADS * half
            d_query[:, h * per_head : (h + 1) * per_head] = jnp.concatenate(
                [plain, g[:, front : front + half].astype(f32), g[:, back : back + half].astype(f32)], axis=1
            )

    return call(
        kernel,
        [
            ((db, out), f32, "v"),
            ((rb, HEADS * (NOPE + VD)), f32, "v"),
            ((db, HEADS * per_head), f32, "v"),
        ],
        [(grads, "v")],
        [],
    )


def shards(
    tokens,
    lengths,
    routes,
    cotangent,
    attn_gain,
    w_query,
    w_latent,
    latent_gain,
    w_expand,
    w_out,
    moe_gain,
    w_router,
    w_gate,
    w_up,
    w_down,
    shared_gate,
    shared_up,
    shared_down,
):
    me = lax.axis_index(PLANE)
    place = me % 16
    member = me % 8
    z = lax.axis_index("z")
    rows, width = tokens.shape
    quarter = rows // 4
    db = width // 32
    rb = R // 32
    ff, sh = w_gate.shape[2], shared_gate.shape[1] // 8
    tile = ROPE + db
    query = HEADS * (NOPE + ROPE)
    half = ROPE // 2
    extra = min(128, FF_PAD)
    wide = FF_PAD + SH_PAD
    info = jnp.concatenate([jnp.stack([me, place, member, z]).astype(jnp.int32), lengths[0]])

    one, two = pack_attention(
        w_query, w_latent, attn_gain, moe_gain, latent_gain, w_router.T, w_out.T, w_expand
    )
    pack = lax.all_gather(two, ("yh", "yl", "x", "c"), axis=0).reshape(2, 2, 8, db, -1)
    keep, send = pack_experts(
        info, w_gate, w_up, jnp.swapaxes(w_down, 1, 2), shared_gate, shared_up, shared_down.T, w_router
    )
    came = swap(send, kc=1)
    by_x = [jnp.stack([keep[k], came[k]]) for k in range(4)]
    latent_parts = gather(one, ("yl", "yh", "x"), ())

    position = place * rows + jnp.arange(rows, dtype=jnp.int32)
    ends = jnp.stack([lengths[0, 0], lengths[0, 0] + lengths[0, 1]])
    start = jnp.where(position >= ends[1], ends[1], jnp.where(position >= ends[0], ends[0], 0))
    frequency = rope_base ** (-jnp.arange(half, dtype=f32) / half)
    angles = (position - start).astype(f32)[:, None] * jnp.tile(frequency, 2 * HEADS * half // ROPE)[None, :]
    cos4, sin4 = jnp.cos(angles), jnp.sin(angles)
    picked = jnp.sum(
        (routes[:, :, None] == jnp.arange(16, dtype=jnp.int32)[None, None, :] - 8).astype(f32), axis=1
    )
    lane_pick = jnp.sum(
        (routes[:, :, None] == jnp.arange(extra, dtype=jnp.int32)[None, None, :] - (ff - FF_PAD + extra)), axis=1
    ).astype(bf16)

    hidden, keys, latent, small, gain_latent = project_latent(info, tokens, cos4, sin4, latent_parts)
    mine = jnp.concatenate([by_x[0]] + [swap(by_x[k], kx=k) for k in (1, 2, 3)])
    weights = [mine] + [swap(mine, ky=k) for k in (1, 3)]
    q_nope, q_rope = project_query(hidden, cos4, sin4, pack)
    keys = hold(exchange(hold(keys, mine), ("yh", "x")), q_nope)
    key_parts = [keys, swap(keys, kc=1)]
    cots = hold(jnp.concatenate([cotangent, lane_pick], axis=1), key_parts[0])
    cots = lax.all_gather(cots, ("x", "c"), axis=0).reshape(4, 2, 4, quarter, width + extra)
    probs, cat, mixture, head_out, attention = attend(info, q_nope, q_rope, key_parts, pack, ())
    attention = exchange(attention, "z")
    own_attention, normed = quarter_norm(info, attention, tokens, small, ())
    weights += pass_on(*weights[1:])
    att_parts = [own_attention] + [swap_z(own_attention, k) for k in (1, 2, 3)]
    normed_parts = gather(normed, ("x", "z"), weights[3:] + att_parts[1:])

    act, grad_both, first, keep2, send2 = expert_rows(
        info, normed_parts, cots, weights, ff
    )

    def scattered(values):
        return exchange(values.reshape(16, quarter, -1), ("x", "z"))

    def collect(values):
        return jnp.sum(values.astype(f32), axis=0, keepdims=True).astype(bf16)

    second = total([keep2, swap(send2, kc=1)])
    d_experts = expert_weights(info, normed_parts, cots, act, grad_both, (second,))
    opposite3, opposite1 = swap(d_experts[4], ky=1), swap(d_experts[5], ky=3)
    straight3, straight1 = swap(d_experts[7], ky=3), swap(d_experts[2], ky=1)
    second = collect(hold(scattered(second), d_experts[0]))
    onward3 = total([hold(d_experts[6], second), opposite3])
    onward1 = total([hold(d_experts[3], second), opposite1])
    first = lax.psum_scatter(first, ("x", "c"), scatter_dimension=0).reshape(4, quarter, width)
    first = lax.psum_scatter(first, "z", scatter_dimension=0)[None]
    onward3, onward1 = swap(onward3, ky=3), swap(onward1, ky=1)
    grad_parts = [second] + [swap_z(second, k) for k in (1, 2, 3)]

    grad_middle, small_grads, key_keep, key_send, grad_att, grad_heads, grad_abs, grad_q = attend_back(
        info, tokens, cotangent, picked, att_parts, grad_parts, small, probs, cat, key_parts, pack, cos4, sin4,
        (),
    )
    *hidden_part, most = attention_weights(
        info, grad_att, grad_heads, grad_abs, grad_q, hidden, head_out, mixture, q_nope, pack, (straight3, straight1, onward3, onward1)
    )
    grad_keys = total([key_keep, swap(hold(key_send, straight3, straight1, onward3, onward1), kc=1)]).reshape(32, quarter, R + tile)
    grad_keys = exchange(grad_keys, ("yh", "x", "z"))
    grad_hidden = total([hidden_part[0]] + [swap_z(hidden_part[k], k) for k in (1, 2, 3)])
    sums = jnp.concatenate([grad_hidden, first], axis=2)
    sum_parts = [sums] + [swap_z(sums, k) for k in (1, 2, 3)]
    grad_keys = hold(grad_keys, *sum_parts[1:])


    most = lax.psum_scatter(most, ("x", "c"), scatter_dimension=0)
    grad_keys = jnp.sum(grad_keys.astype(f32), axis=0, keepdims=True)
    grad_key_parts = [grad_keys] + [swap_z(grad_keys, k) for k in (1, 2, 3)]
    d_mine = [
        total([part[k % 2] for part in (d_experts[k // 2], (onward3, straight3)[k // 2], (straight1, onward1)[k // 2])])
        for k in range(4)
    ]

    d_mine = [hold(part, sums) for part in d_mine]
    d_mine[1], d_mine[3] = swap(d_mine[1], kx=1), swap(d_mine[3], kx=3)
    output, d_tokens, keep, send = finish(
        info, tokens, grad_middle, hidden, latent, gain_latent, small, small_grads, grad_key_parts, att_parts,
        sum_parts, latent_parts, cos4, sin4, (d_mine[1], d_mine[3]),
    )
    most = lax.psum_scatter(hold(most, keep), ("yh", "yl"), scatter_dimension=0)
    rest = total([keep, swap(send, kc=1)])
    d_mine[2] = swap(hold(d_mine[2], d_tokens), kx=2)
    rest = exchange(rest, ("yl", "yh", "x"))
    d_mine[2] = hold(d_mine[2], rest)
    d_other = swap(jnp.stack([part[1] for part in d_mine]), kc=1)
    d_routed = unpack_experts(info, d_mine, d_other, ff, sh)
    rest = collect(rest)
    d_out, d_expand, d_query = unpack_attention(most)
    d_latent, d_attn_gain, d_moe_gain, d_latent_gain, d_router_t = unpack_rest(
        info, [rest] + [swap_z(rest, k) for k in (1, 2, 3)]
    )
    return (
        output,
        d_tokens,
        d_attn_gain[0],
        d_query,
        d_latent,
        d_latent_gain[0],
        d_expand,
        d_out.T,
        d_moe_gain[0],
        d_router_t.T,
        d_routed[0],
        d_routed[1],
        jnp.swapaxes(d_routed[2], 1, 2),
        d_routed[3],
        d_routed[4],
        d_routed[5].T,
    )


def solution(mesh):
    rows = P(PLANE, None)
    split = P(PLANE, "z")
    vector = P(PLANE)
    turned = P("z", PLANE)
    expert_rows = P(None, PLANE, "z")
    expert_columns = P(None, "z", PLANE)
    fine = Mesh(mesh.devices.reshape(2, 2, 4, 2, 4), ("yl", "yh", "x", "c", "z"))
    return jax.shard_map(
        shards,
        mesh=fine,
        in_specs=(
            rows,
            P("yl", None),
            rows,
            rows,
            vector,
            split,
            rows,
            vector,
            split,
            turned,
            vector,
            rows,
            expert_rows,
            expert_rows,
            expert_columns,
            split,
            split,
            turned,
        ),
        out_specs=(
            rows,
            rows,
            vector,
            split,
            rows,
            vector,
            split,
            turned,
            vector,
            rows,
            expert_rows,
            expert_rows,
            expert_columns,
            split,
            split,
            turned,
        ),
        check_vma=False,
    )
```

```python
import math

import jax
import jax.numpy as jnp
from jax import lax
from jax.experimental import pallas as pl
from jax.experimental.pallas import tpu as pltpu
from jax.sharding import Mesh
from jax.sharding import PartitionSpec as P

NOPE = 128
ROPE = 64
VD = 128
R = 512
E = 8
FF_PAD = 384
SH_PAD = 128
HEADS = 4

epsilon = 1e-06
rope_base = 50000.0
route_scale = 2.446
bf16 = jnp.bfloat16
f32 = jnp.float32

PLANE = ("yl", "yh", "x", "c")
YS = ("yl", "yh")


def mask(ky=0, kx=0, kc=0):
    return (ky & 1) * 16 + (ky >> 1) * 8 + kx * 2 + kc


def swap(values, ky=0, kx=0, kc=0):
    bits = mask(ky, kx, kc)
    return lax.ppermute(values, PLANE, [(i, i ^ bits) for i in range(32)])


def swap_z(values, k):
    return lax.ppermute(values, "z", [(i, i ^ k) for i in range(4)])


def total(parts, dtype=bf16):
    out = parts[0].astype(f32)
    for part in parts[1:]:
        out = out + part.astype(f32)
    return out.astype(dtype)


def nn(left, right):
    return jnp.dot(left, right, preferred_element_type=f32)


def nt(left, right):
    return lax.dot_general(left, right, (((1,), (1,)), ((), ())), preferred_element_type=f32)


def tn(left, right):
    return lax.dot_general(left, right, (((0,), (0,)), ((), ())), preferred_element_type=f32)


def lanes(shape):
    return lax.broadcasted_iota(jnp.int32, shape, 1)


def high_low(values):
    high = values.astype(bf16)
    return high, (values - high.astype(f32)).astype(bf16)


def start_all(copies, sem):
    for source, destination in copies:
        pltpu.make_async_copy(source, destination, sem).start()


def wait_for(ref, sem):
    pltpu.make_async_copy(ref, ref, sem).wait()


def call(kernel, outs, ins, scratch, macs=0, vmem=63, after=()):
    count, late = len(ins), len(after)
    body = kernel
    if late:

        def body(*refs):
            kernel(*refs[:count], *refs[count + late :])

    moved = sum(array.size * array.dtype.itemsize for array, _ in ins)
    moved += sum(math.prod(shape) * jnp.dtype(dtype).itemsize for shape, dtype, _ in outs)
    spaces = {"s": pltpu.SMEM, "v": pltpu.VMEM, "a": pl.ANY}
    return pl.pallas_call(
        body,
        out_shape=[jax.ShapeDtypeStruct(shape, dtype) for shape, dtype, _ in outs],
        in_specs=[pl.BlockSpec(memory_space=spaces[space]) for _, space in ins]
        + [pl.BlockSpec(memory_space=pl.ANY)] * late,
        out_specs=[pl.BlockSpec(memory_space=spaces[space]) for _, _, space in outs],
        scratch_shapes=scratch,
        compiler_params=pltpu.CompilerParams(vmem_limit_bytes=vmem << 20),
        cost_estimate=pl.CostEstimate(flops=4 * macs, bytes_accessed=moved, transcendentals=0),
    )(*[array for array, _ in ins], *after)


def exchange(blocks, axes):
    return lax.all_to_all(blocks, axes, 0, 0, tiled=True)


def gather(copies, axes, after):
    own = hold(exchange(copies, axes), *after)
    return [own, swap(own, kc=1)]


def pair_copies(parts, core, target, columns=None):
    if columns is not None:
        parts = [part.at[:, :, columns] for part in parts]
    return [(parts[0], target.at[:, core]), (parts[1], target.at[:, 1 - core])]


def pack_copies(pack, columns, target):
    return [
        (pack.at[yh, yl, :, :, columns], target.at[pl.ds(yl * 16 + yh * 8, 8)]) for yh in (0, 1) for yl in (0, 1)
    ]


def hold(values, *after):
    def kernel(*refs):
        pass

    return pl.pallas_call(
        kernel,
        out_shape=jax.ShapeDtypeStruct(values.shape, values.dtype),
        in_specs=[pl.BlockSpec(memory_space=pl.ANY)] * (1 + len(after)),
        out_specs=pl.BlockSpec(memory_space=pl.ANY),
        input_output_aliases={0: 0},
    )(values, *after)


def pack_attention(w_query, w_latent, attn_gain, moe_gain, latent_gain, router_t, out_t, w_expand):
    db = w_query.shape[0]
    query = w_query.shape[1]
    late = w_latent.shape[1]
    out = out_t.shape[1]
    per_head = NOPE + ROPE

    def kernel(q, lat, ag, mg, lg, rt, ot, ex, first, second):
        plain = [q[:, h * per_head : h * per_head + NOPE] for h in range(HEADS)]
        front = [q[:, h * per_head + NOPE : h * per_head + NOPE + ROPE // 2] for h in range(HEADS)]
        back = [q[:, h * per_head + NOPE + ROPE // 2 : (h + 1) * per_head] for h in range(HEADS)]
        rb = lg.shape[1]
        small = jnp.concatenate(
            [
                ag[...].astype(f32),
                mg[...].astype(f32),
                jnp.concatenate([lg[...].astype(f32), jnp.zeros((1, db - rb), f32)], axis=1),
                jnp.zeros((5, db), f32),
                rt[...].astype(f32),
            ]
            + ([jnp.zeros((db - 16, db), f32)] if db > 16 else []),
            axis=0,
        ).astype(bf16)
        one = jnp.concatenate([lat[...], small], axis=1)
        for n in range(16):
            first[n] = one
        width = ex.shape[1] // HEADS
        expand = jnp.concatenate([ex[:, h * width : (h + 1) * width] for h in range(HEADS)], axis=0)
        second[...] = jnp.concatenate(plain + front + back + [ot[...], expand], axis=1)

    two = query + out + w_expand.shape[1] // HEADS
    ins = [w_query, w_latent, attn_gain[None], moe_gain[None], latent_gain[None], router_t, out_t, w_expand]
    return call(
        kernel,
        [((16, db, late + db), bf16, "v"), ((db, two), bf16, "v")],
        [(array, "v") for array in ins],
        [],
    )


def pack_experts(info, gate, up, down_t, shared_gate, shared_up, shared_down_t, router):
    count, db, ff = gate.shape
    sh = shared_gate.shape[1] // count
    wide = FF_PAD + SH_PAD

    def kernel(info, g, u, d, sg, su, sd, rt, keep, send, packed, sem):
        fill = FF_PAD - ff - count
        for n, (routed, shared) in enumerate(((g, sg), (u, su), (d, sd))):
            extra = rt[...] if n == 0 else jnp.zeros((db, count), bf16)
            for e in range(count):
                packed[e, n] = jnp.concatenate(
                    [
                        routed[e],
                        extra,
                        jnp.zeros((db, fill), bf16),
                        shared[:, e * sh : (e + 1) * sh],
                        jnp.zeros((db, SH_PAD - sh), bf16),
                    ],
                    axis=1,
                )
        copies = []
        for kx in range(4):
            copies.append((packed.at[info[2] ^ (kx * 2)], keep.at[kx], sem.at[0]))
            copies.append((packed.at[info[2] ^ (kx * 2 + 1)], send.at[kx], sem.at[1]))
        for source, destination, which in copies:
            pltpu.make_async_copy(source, destination, which).start()
        wait_for(keep, sem.at[0])
        wait_for(send, sem.at[1])

    ins = [gate, up, down_t, shared_gate, shared_up, shared_down_t, router]
    return call(
        kernel,
        [((4, 3, db, wide), bf16, "a")] * 2,
        [(info, "s")] + [(array, "v") for array in ins],
        [pltpu.VMEM((count, 3, db, wide), bf16), pltpu.SemaphoreType.DMA((2,))],
    )


def project_latent(info, tokens, cos4, sin4, parts):
    rows, width = tokens.shape
    db = width // 32
    rb = R // 32
    tile = ROPE + db

    def kernel(info, tok, cos, sin, own, other, hidden, keys, latent_out, small, gain_row, pairs, sem):
        start_all(pair_copies((own, other), info[1] % 2, pairs), sem)
        x = tok[...].astype(f32)
        inverse = lax.rsqrt(jnp.mean(x * x, axis=-1, keepdims=True) + epsilon)
        unit = x * inverse
        wait_for(pairs, sem)
        weights = pairs.reshape(32, db, R + tile)
        lane = lanes((16, tile))
        tiles = []
        for t in range(16):
            even = weights[2 * t, 0:16, R:].astype(f32)
            odd = weights[2 * t + 1, 0:16, R:].astype(f32)
            tiles.append(jnp.where(lane < db, pltpu.roll(even, tile - db, 1), odd))
        table = jnp.concatenate(tiles, axis=1)
        small[...] = table.astype(bf16)
        lane = lanes((1, tile))
        per = tile // rb
        pieces = []
        for t in range(32 // per):
            piece = jnp.zeros((1, tile), f32)
            for i in range(per):
                row = weights[t * per + i, 0:16, R:].astype(f32)[2:3]
                piece = jnp.where(lane // rb == i, pltpu.roll(row, (i * rb + tile - db) % tile, 1), piece)
            pieces.append(piece)
        gain_latent = jnp.concatenate(pieces, axis=1)
        gain_row[...] = gain_latent
        low = (unit * table[0:1]).astype(bf16)
        hidden[...] = low
        late = nn(low, weights[...].reshape(width, R + tile))
        latent_out[...] = late
        plain = late[:, :R]
        inverse = lax.rsqrt(jnp.mean(plain * plain, axis=-1, keepdims=True) + epsilon)
        key = jnp.concatenate(
            [plain * inverse * gain_latent, turn(late[:, R:], cos[...], sin[...])], axis=1
        ).astype(bf16)
        for n in range(8):
            keys[n] = key

    return call(
        kernel,
        [
            ((rows, width), bf16, "v"),
            ((8, rows, R + tile), bf16, "v"),
            ((rows, R + tile), f32, "v"),
            ((16, width), bf16, "v"),
            ((1, R), f32, "v"),
        ],
        [(info, "s"), (tokens, "v"), (cos4, "v"), (sin4, "v")] + [(part, "a") for part in parts],
        [pltpu.VMEM((16, 2, db, R + tile), bf16), pltpu.SemaphoreType.DMA(())],
        macs=rows * width * (R + tile),
    )


def project_query(hidden, cos4, sin4, pack):
    rows, width = hidden.shape
    db = width // 32
    query = HEADS * (NOPE + ROPE)
    tile = ROPE + db
    half = ROPE // 2

    def kernel(hid, cos, sin, packed, q_nope, q_rope, weights, sem):
        start_all(pack_copies(packed, pl.ds(0, query), weights), sem)
        wait_for(weights, sem)
        raw = nn(hid[...], weights[...].reshape(width, query))
        q_nope[...] = raw[:, : HEADS * NOPE].astype(bf16)
        front = raw[:, HEADS * NOPE : HEADS * NOPE + tile]
        back = raw[:, HEADS * NOPE + tile :]
        turned_front = front * cos[...] - back * sin[...]
        turned_back = back * cos[...] + front * sin[...]
        lane = lanes((rows, tile))
        for h in range(HEADS):
            head = jnp.where(
                lane < half,
                pltpu.roll(turned_front, (tile - h * half) % tile, 1),
                jnp.where(lane < ROPE, pltpu.roll(turned_back, (tile - h * half + half) % tile, 1), 0.0),
            )
            q_rope[h * rows : (h + 1) * rows] = head.astype(bf16)

    return call(
        kernel,
        [((rows, HEADS * NOPE), bf16, "v"), ((HEADS * rows, tile), bf16, "v")],
        [(hidden, "v"), (cos4, "v"), (sin4, "v"), (pack, "a")],
        [pltpu.VMEM((32, db, query), bf16), pltpu.SemaphoreType.DMA(())],
        macs=rows * width * query,
    )


def turn(values, cosine, sine_part):
    width = values.shape[1]
    half = ROPE // 2
    lane = lanes(values.shape)
    swapped = jnp.where(lane < half, -pltpu.roll(values, width - half, 1), pltpu.roll(values, half, 1))
    return jnp.where(lane < ROPE, values * cosine + swapped * sine_part, 0.0)


def put_quarters(values, targets, z):
    quarter = values.shape[0] // 4
    for n in range(4):
        for k in range(4):

            @pl.when(z ^ k == n)
            def _(n=n, k=k):
                targets[k][0] = values[n * quarter : (n + 1) * quarter]


def visible(info, shape, row_count):
    place = lax.broadcasted_iota(jnp.int32, shape, 0) + info[1] * row_count
    key = lax.broadcasted_iota(jnp.int32, shape, 1)
    end0 = info[4]
    end1 = info[4] + info[5]
    row_doc = (place >= end0).astype(jnp.int32) + (place >= end1).astype(jnp.int32)
    key_doc = (key >= end0).astype(jnp.int32) + (key >= end1).astype(jnp.int32)
    return (row_doc == key_doc) & (key <= place)


def attend(info, q_nope, q_rope, key_parts, pack, after):
    rows = q_nope.shape[0]
    db = pack.shape[3]
    columns = pl.ds(HEADS * (NOPE + ROPE), HEADS * VD + NOPE + VD)
    width = 32 * db
    tile = q_rope.shape[1]
    out = HEADS * VD
    keys = 16 * rows
    quarter = rows // 4
    rb = R // 32

    def kernel(info, qn, qr, *refs):
        key_ins, refs = refs[:2], refs[2:]
        pack_in, refs = refs[0], refs[1:]
        probs, cat, mixture, head_out, result, key_rows, weights, expand, scores, sem = refs
        start_all(pair_copies(key_ins, info[1] % 2, key_rows), sem.at[0])
        start_all(pack_copies(pack_in, columns, weights), sem.at[1])
        wait_for(weights, sem.at[1])
        for h in range(HEADS):
            expand[h] = weights[:, h * rb : (h + 1) * rb, out:].reshape(R, NOPE + VD)
        for h in range(HEADS):
            own = slice(h * rows, (h + 1) * rows)
            cat[own, :R] = nt(qn[:, h * NOPE : (h + 1) * NOPE], expand[h, :, :NOPE]).astype(bf16)
            cat[own, R:] = qr[own]
        wait_for(key_rows, sem.at[0])
        flat = key_rows[...].reshape(keys, R + tile)
        seen = visible(info, (rows, keys), rows)
        scale = (NOPE + ROPE) ** (-0.5)
        chunk = keys // 4
        for n in range(4):
            part = slice(n * chunk, (n + 1) * chunk)
            scores[:, part] = nt(cat[...], flat[part])
        for h in range(HEADS):
            own = slice(h * rows, (h + 1) * rows)
            score = jnp.where(seen, scale * scores[own], -1e30)
            weight = jnp.exp(score - jnp.max(score, axis=-1, keepdims=True))
            probs[own] = (weight / jnp.sum(weight, axis=-1, keepdims=True)).astype(bf16)
        mixture[...] = nn(probs[...], flat[:, :R]).astype(bf16)
        for h in range(HEADS):
            own = slice(h * rows, (h + 1) * rows)
            head_out[:, h * VD : (h + 1) * VD] = nn(mixture[own], expand[h, :, NOPE:]).astype(bf16)
        summed = nt(head_out[...], weights[:, :, :out].reshape(width, out)).astype(bf16)
        result[...] = summed.reshape(4, quarter, width)

    return call(
        kernel,
        [
            ((HEADS * rows, keys), bf16, "v"),
            ((HEADS * rows, R + tile), bf16, "v"),
            ((HEADS * rows, R), bf16, "v"),
            ((rows, out), bf16, "v"),
        ]
        + [((4, quarter, width), bf16, "v")],
        [(info, "s"), (q_nope, "v"), (q_rope, "v")]
        + [(part, "a") for part in key_parts + [pack]],
        [
            pltpu.VMEM((8, 2, rows, R + tile), bf16),
            pltpu.VMEM((32, db, out + NOPE + VD), bf16),
            pltpu.VMEM((HEADS, R, NOPE + VD), bf16),
            pltpu.VMEM((HEADS * rows, keys), f32),
            pltpu.SemaphoreType.DMA((2,)),
        ],
        macs=HEADS * rows * keys * (2 * R + tile) * 2,
        after=after,
    )


def quarter_norm(info, parts, tokens, small, after):
    _, quarter, width = parts.shape

    def kernel(info, came, tok, table, attention, normed):
        summed = came[0].astype(f32) + came[1].astype(f32) + came[2].astype(f32) + came[3].astype(f32)
        low = summed.astype(bf16)
        attention[0] = low
        middle = tok[info[3]].astype(f32) + low.astype(f32)
        inverse = lax.rsqrt(jnp.mean(middle * middle, axis=-1, keepdims=True) + epsilon)
        rows = (middle * inverse * table[1:2].astype(f32)).astype(bf16)
        for n in range(16):
            normed[n] = rows

    return call(
        kernel,
        [((1, quarter, width), bf16, "v"), ((16, quarter, width), bf16, "v")],
        [(info, "s"), (parts, "v"), (tokens.reshape(4, quarter, width), "v"), (small, "v")],
        [],
        after=after,
    )


def pass_on(from_one, from_three):
    half = from_one.shape[0] // 2
    return [swap(from_three[:half], ky=1), swap(from_one[half:], ky=3)]


def expert_copies(parts, me, targets, which):
    copies = []
    half = parts[3].shape[0]
    for part, ky, first in zip(parts, (0, 1, 3, 2, 2), (0, 0, 0, 0, half), strict=True):
        for i in range(part.shape[0]):
            block = first + i
            for target in targets:
                copies.append((part.at[i, which], target.at[me ^ mask(ky, block // 2, block % 2)]))
    return copies


def expert_rows(info, normed_parts, cots, weights, ff):
    _, quarter, width = normed_parts[0].shape
    extra = cots.shape[-1] - width
    db, wide = weights[0].shape[-2:]
    count = 32 * quarter
    step = count // 4
    lane0 = FF_PAD - extra

    def kernel(info, *refs):
        nref, refs = refs[:2], refs[2:]
        cref, wref, refs = refs[0], refs[1:6], refs[6:]
        act_out, grad_out, first, keep2, send2, x, g, wg, wu, wd, out1, out2, sem = refs
        half = step // quarter
        core_here = info[1] % 2

        def row_copies(i):
            core, at = i // 2, (i % 2) * half
            source = (core_here, 1 - core_here)[core]
            return (
                (nref[core].at[pl.ds(at, half)], x.at[core, pl.ds(at, half)]),
                (cref.at[pl.ds(at // 4, half // 4), source], g.at[core, pl.ds(at // 4, half // 4)]),
            )

        for n, (target, source) in enumerate(zip((wg, wu, wd), range(3), strict=True)):
            start_all(expert_copies(wref, info[0], (target,), source), sem.at[n])
            if n == 0:
                start_all(row_copies(0)[:1], sem.at[8])
            if n == 1:
                start_all(row_copies(0)[1:], sem.at[12])
        for i in range(1, 4):
            start_all(row_copies(i)[:1], sem.at[8 + i])
            start_all(row_copies(i)[1:], sem.at[12 + i])
        tile_lane = lanes((step, extra))
        lane = lanes((step, wide))

        def body(i, carry):
            own = pl.ds(pl.multiple_of(i * step, step), step)
            core, at = i // 2, (i % 2) * half
            here, there = x.at[core, pl.ds(at, half)], g.at[core, pl.ds(at // 4, half // 4)]
            wait_for(here, sem.at[8 + i])

            @pl.when(i == 0)
            def _():
                wait_for(wg, sem.at[0])

            rows = here[...].reshape(step, width)
            gate_pre = nn(rows, wg[...].reshape(width, wide))

            @pl.when(i == 0)
            def _():
                wait_for(wu, sem.at[1])

            up_pre = nn(rows, wu[...].reshape(width, wide))
            wait_for(there, sem.at[12 + i])

            @pl.when(i == 0)
            def _():
                wait_for(wd, sem.at[2])

            cot = there[...].reshape(step, width + extra)
            gate_weight = wg[...].reshape(width, wide)
            up_weight = wu[...].reshape(width, wide)
            down_weight = wd[...].reshape(width, wide)
            back = nn(cot[:, :width], down_weight)
            router = jax.nn.sigmoid(gate_pre[:, lane0:FF_PAD])
            weighted = router * cot[:, width:].astype(f32)
            gates = route_scale * weighted / jnp.sum(weighted, axis=1, keepdims=True)
            gate = jnp.sum(jnp.where(tile_lane == ff - lane0 + info[2], gates, 0.0), axis=1, keepdims=True)
            gate_row = jnp.where(lane < FF_PAD, gate, 1.0)
            sig = jax.nn.sigmoid(gate_pre)
            silu = gate_pre * sig
            act = silu * up_pre
            own_grad = jnp.sum(jnp.where(lane < FF_PAD, act * back, 0.0), axis=1, keepdims=True)
            act_low = (gate_row * act).astype(bf16)
            grad_act = gate_row * back
            grad_gate = (grad_act * up_pre * (sig * (1.0 + gate_pre * (1.0 - sig)))).astype(bf16)
            grad_up = (grad_act * silu).astype(bf16)
            act_out[own] = act_low
            grad_out[own, :wide] = grad_gate
            grad_out[own, wide:] = grad_up
            out1[own] = nt(act_low, down_weight).astype(bf16)
            out2[own, :width] = (nt(grad_gate, gate_weight) + nt(grad_up, up_weight)).astype(bf16)
            high = own_grad.astype(bf16).astype(f32)
            out2[own, width:] = (
                jnp.where(tile_lane == 8 + info[2], high, 0.0)
                + jnp.where(tile_lane == 24 + info[2], own_grad - high, 0.0)
            ).astype(bf16)
            of = jnp.where(core == 0, core_here, 1 - core_here)
            block = step // 2
            for n in range(2):
                part = pl.ds(pl.multiple_of(i * step + n * block, block), block)
                target = first.at[((i % 2) * 2 + n) * 2 + of]
                pltpu.make_async_copy(out1.at[part], target, sem.at[5]).start()

            @pl.when(core == 0)
            def _():
                pltpu.make_async_copy(out2.at[own], keep2.at[own], sem.at[3]).start()

            @pl.when(core == 1)
            def _():
                there = pl.ds(pl.multiple_of((i - 2) * step, step), step)
                pltpu.make_async_copy(out2.at[own], send2.at[there], sem.at[4]).start()

            return carry

        lax.fori_loop(0, 4, body, 0)
        wait_for(keep2, sem.at[3])
        wait_for(send2, sem.at[4])
        wait_for(first, sem.at[5])

    return call(
        kernel,
        [((count, wide), bf16, "v"), ((count, 2 * wide), bf16, "v")]
        + [((8, 4 * quarter, width), bf16, "a")]
        + [((count // 2, width + extra), bf16, "a")] * 2,
        [(info, "s")] + [(part, "a") for part in normed_parts + [cots] + weights],
        [
            pltpu.VMEM((2, 16, quarter, width), bf16),
            pltpu.VMEM((2, 4, 4, quarter, width + extra), bf16),
            pltpu.VMEM((32, db, wide), bf16),
            pltpu.VMEM((32, db, wide), bf16),
            pltpu.VMEM((32, db, wide), bf16),
            pltpu.VMEM((count, width), bf16),
            pltpu.VMEM((count, width + extra), bf16),
            pltpu.SemaphoreType.DMA((16,)),
        ],
        macs=6 * count * width * wide,
    )


def expert_weights(info, normed_parts, cots, act, grad_both, after):
    _, quarter, width = normed_parts[0].shape
    extra = cots.shape[-1] - width
    count, wide = act.shape
    db = width // 32
    step = width // 8
    blocks = step // db

    def kernel(info, *refs):
        nref, refs = refs[:2], refs[2:]
        cref, refs = refs[0], refs[1:]
        a, gb, *results, x, g, grads, sem = refs
        start_all([(cref.at[:, info[1] % 2], g.at[0]), (cref.at[:, 1 - info[1] % 2], g.at[1])], sem.at[0])
        start_all([(nref[0], x.at[0]), (nref[1], x.at[1])], sem.at[1])
        wait_for(g, sem.at[0])
        wait_for(x, sem.at[1])

        def body(i, carry):
            cols = pl.ds(pl.multiple_of(i * step, step), step)
            rows = x[:, :, :, cols].reshape(count, step)
            cot = g[:, :, :, :, cols].reshape(count, step)
            own = pl.ds(i * blocks, blocks)
            both = tn(rows, gb[...]).astype(bf16).reshape(blocks, db, 2 * wide)
            grads[own, 0] = both[:, :, :wide]
            grads[own, 1] = both[:, :, wide:]
            grads[own, 2] = tn(cot, a[...]).astype(bf16).reshape(blocks, db, wide)
            return carry

        lax.fori_loop(0, 8, body, 0)
        for ky in range(4):
            for kx in range(4):
                for kc in (0, 1):
                    pltpu.make_async_copy(
                        grads.at[info[0] ^ mask(ky, kx, kc)], results[2 * ky + kx // 2].at[kx % 2, kc], sem.at[2]
                    ).start()
        for result in results:
            wait_for(result, sem.at[2])

    return call(
        kernel,
        [((2, 2, 3, db, wide), bf16, "a")] * 8,
        [(info, "s")]
        + [(part, "a") for part in normed_parts + [cots]]
        + [(act, "v"), (grad_both, "v")],
        [
            pltpu.VMEM((2, 16, quarter, width), bf16),
            pltpu.VMEM((2, 4, 4, quarter, width + extra), bf16),
            pltpu.VMEM((32, 3, db, wide), bf16),
            pltpu.SemaphoreType.DMA((3,)),
        ],
        macs=3 * count * width * wide,
        after=after,
    )


def quarter_copies(parts, z, target, columns=None):
    if columns is None:
        return [(part.at[0], target.at[z ^ k]) for k, part in enumerate(parts)]
    return [(part.at[0, :, columns], target.at[z ^ k]) for k, part in enumerate(parts)]


def attend_back(
    info, tokens, cotangent, picked, att_parts, grad_parts, small, probs, cat, key_parts, pack2, cos4,
    sin4, after,
):
    rows, width = tokens.shape
    quarter = rows // 4
    db = width // 32
    rb = R // 32
    tile = cat.shape[1] - R
    out = HEADS * VD
    keys = 16 * rows
    query = HEADS * (NOPE + ROPE)
    half = ROPE // 2
    extra = grad_parts[0].shape[-1] - width
    scale = (NOPE + ROPE) ** (-0.5)
    late = out + NOPE + VD

    def kernel(info, tok, cotan, pick, table, pr, ca, cos, sin, *refs):
        att_in, refs = refs[:4], refs[4:]
        grad_in, refs = refs[:4], refs[4:]
        key_in, refs = refs[:2], refs[2:]
        in2, refs = refs[0], refs[1:]
        (
            grad_middle, small_grads, key_keep, key_send, grad_att, grad_heads, grad_abs, grad_q,
            att, arrived, key_rows, w2, expand, grad_mix, grad_scores, key_grads, wide, sem,
        ) = refs
        start_all(quarter_copies(grad_in, info[3], arrived), sem.at[0])
        start_all(quarter_copies(att_in, info[3], att), sem.at[1])
        start_all(pack_copies(in2, pl.ds(query, late), w2), sem.at[2])
        start_all(pair_copies(key_in, info[1] % 2, key_rows), sem.at[3])
        wait_for(arrived, sem.at[0])
        wait_for(att, sem.at[1])
        middle = tok[...].astype(f32) + att[...].reshape(rows, width).astype(f32)
        inverse = lax.rsqrt(jnp.mean(middle * middle, axis=-1, keepdims=True) + epsilon)
        unit = middle * inverse
        gain = table[1:2].astype(f32)
        normed = (unit * gain).astype(bf16)
        came = arrived[...].reshape(rows, width + extra)
        sig = jax.nn.sigmoid(nt(normed, table[...]))
        chosen = pick[...]
        weighted = sig * chosen
        gate_total = jnp.sum(weighted, axis=1, keepdims=True)
        gates = route_scale * weighted / gate_total
        grad_gates = came[:, width : width + 16].astype(f32) + came[:, width + 16 : width + 32].astype(f32)
        grad_weighted = (route_scale * grad_gates - jnp.sum(grad_gates * gates, axis=1, keepdims=True)) / gate_total
        grad_logits = grad_weighted * chosen * sig * (1.0 - sig)
        high, low = high_low(grad_logits)
        grads = tn(high, normed) + tn(low, normed)
        grad_normed = came[:, :width].astype(f32) + nn(high, table[...]) + nn(low, table[...])
        scaled = grad_normed * gain
        grad_mid = cotan[...].astype(f32) + inverse * (
            scaled - unit * jnp.mean(scaled * unit, axis=-1, keepdims=True)
        )
        d_gain = jnp.sum(grad_normed * unit, axis=0, keepdims=True)
        row16 = lax.broadcasted_iota(jnp.int32, (16, width), 0)
        small_grads[...] = jnp.where(row16 >= 8, grads, jnp.where(row16 == 1, d_gain, 0.0))
        grad_middle[...] = grad_mid
        grad_att[...] = grad_mid.astype(bf16)
        wait_for(w2, sem.at[2])
        for h in range(HEADS):
            expand[h] = w2[:, h * rb : (h + 1) * rb, out:].reshape(R, NOPE + VD)
        grad_heads[...] = nn(grad_att[...], w2[:, :, :out].reshape(width, out)).astype(bf16)
        for h in range(HEADS):
            own = slice(h * rows, (h + 1) * rows)
            grad_mix[own] = nt(grad_heads[:, h * VD : (h + 1) * VD], expand[h, :, NOPE:]).astype(bf16)
        wait_for(key_rows, sem.at[3])
        flat = key_rows[...].reshape(keys, R + tile)
        lane = lanes((rows, tile))
        front = jnp.zeros((rows, tile), f32)
        back = jnp.zeros((rows, tile), f32)
        chunk = keys // 4
        for n in range(4):
            part = slice(n * chunk, (n + 1) * chunk)
            wide[:, part] = nt(grad_mix[...], flat[part, :R])
        for h in range(HEADS):
            own = slice(h * rows, (h + 1) * rows)
            grad_prob = wide[own]
            prob = pr[own].astype(f32)
            inner = jnp.sum(prob * grad_prob, axis=-1, keepdims=True)
            grad_scores[own] = (prob * (grad_prob - inner)).astype(bf16)
        grad_cat = scale * nn(grad_scores[...], flat)
        grad_abs[...] = grad_cat[:, :R].astype(bf16)
        for h in range(HEADS):
            own = slice(h * rows, (h + 1) * rows)
            grad_q[:, h * NOPE : (h + 1) * NOPE] = nn(grad_abs[own], expand[h, :, :NOPE]).astype(bf16)
            turned = grad_cat[own, R:]
            inside = (lane >= h * half) & (lane < (h + 1) * half)
            front = jnp.where(inside, pltpu.roll(turned, (h * half) % tile, 1), front)
            back = jnp.where(inside, pltpu.roll(turned, (h * half + tile - half) % tile, 1), back)
        grad_q[:, HEADS * NOPE : HEADS * NOPE + tile] = (front * cos[...] + back * sin[...]).astype(bf16)
        grad_q[:, HEADS * NOPE + tile :] = (back * cos[...] - front * sin[...]).astype(bf16)
        chunk = keys // 4
        for n in range(4):
            cols = slice(n * chunk, (n + 1) * chunk)
            part = scale * tn(grad_scores[:, cols], ca[...])
            latent = part[:, :R] + tn(pr[:, cols], grad_mix[...])
            own = slice(n * 2, (n + 1) * 2)
            key_grads[own, :, :, :R] = latent.astype(bf16).reshape(2, 2, rows, R)
            key_grads[own, :, :, R:] = part[:, R:].astype(bf16).reshape(2, 2, rows, tile)
        core = info[1] % 2
        pltpu.make_async_copy(key_grads.at[:, core], key_keep, sem.at[5]).start()
        pltpu.make_async_copy(key_grads.at[:, 1 - core], key_send, sem.at[6]).start()
        wait_for(key_keep, sem.at[5])
        wait_for(key_send, sem.at[6])

    vmem_ins = [tokens, cotangent, picked, small, probs, cat, cos4, sin4]
    return call(
        kernel,
        [
            ((rows, width), f32, "v"),
            ((16, width), f32, "v"),
            ((8, rows, R + tile), bf16, "a"),
            ((8, rows, R + tile), bf16, "a"),
            ((rows, width), bf16, "v"),
            ((rows, out), bf16, "v"),
            ((HEADS * rows, R), bf16, "v"),
            ((rows, query), bf16, "v"),
        ],
        [(info, "s")]
        + [(array, "v") for array in vmem_ins]
        + [(part, "a") for part in att_parts + grad_parts + key_parts + [pack2]],
        [
            pltpu.VMEM((4, quarter, width), bf16),
            pltpu.VMEM((4, quarter, width + extra), bf16),
            pltpu.VMEM((8, 2, rows, R + tile), bf16),
            pltpu.VMEM((32, db, late), bf16),
            pltpu.VMEM((HEADS, R, NOPE + VD), bf16),
            pltpu.VMEM((HEADS * rows, R), bf16),
            pltpu.VMEM((HEADS * rows, keys), bf16),
            pltpu.VMEM((8, 2, rows, R + tile), bf16),
            pltpu.VMEM((HEADS * rows, keys), f32),
            pltpu.SemaphoreType.DMA((7,)),
        ],
        macs=HEADS * rows * keys * (4 * R + 2 * tile) * 2,
        after=after,
    )


def attention_weights(info, grad_att, grad_heads, grad_abs, grad_q, hidden, head_out, mixture, q_nope, pack, after):
    rows, width = hidden.shape
    quarter = rows // 4
    db = width // 32
    rb = R // 32
    out = HEADS * VD
    late = out + NOPE + VD
    query = HEADS * (NOPE + ROPE)

    def kernel(info, ga, gh, gb, gq, hid, ho, mix, qn, *refs):
        packed, hid0, hid1, hid2, hid3, result, w1, grads, sem = refs
        start_all(pack_copies(packed, pl.ds(0, query), w1), sem.at[0])
        grads[:, :, :, :out] = tn(ga[...], ho[...]).astype(bf16).reshape(16, 2, db, out)
        for h in range(HEADS):
            part = slice(h * rows, (h + 1) * rows)
            here = slice(h * rb, (h + 1) * rb)
            grads[:, :, here, out : out + NOPE] = (
                tn(gb[part], qn[:, h * NOPE : (h + 1) * NOPE]).astype(bf16).reshape(16, 2, rb, NOPE)
            )
            grads[:, :, here, out + NOPE : late] = (
                tn(mix[part], gh[:, h * VD : (h + 1) * VD]).astype(bf16).reshape(16, 2, rb, VD)
            )
        grads[:, :, :, late:] = tn(hid[...], gq[...]).astype(bf16).reshape(16, 2, db, query)
        for n in range(16):
            for core in (0, 1):
                target = result.at[(n % 4) * 2 + core, ((n // 4) % 2) * 2 + n // 8]
                pltpu.make_async_copy(grads.at[n, core], target, sem.at[1]).start()
        wait_for(w1, sem.at[0])
        put_quarters(nt(gq[...], w1[...].reshape(width, query)).astype(bf16), (hid0, hid1, hid2, hid3), info[3])
        wait_for(result, sem.at[1])

    vmem_ins = [grad_att, grad_heads, grad_abs, grad_q, hidden, head_out, mixture, q_nope]
    return call(
        kernel,
        [((1, quarter, width), bf16, "v")] * 4 + [((8, 4, db, late + query), bf16, "a")],
        [(info, "s")] + [(array, "v") for array in vmem_ins] + [(pack, "a")],
        [
            pltpu.VMEM((32, db, query), bf16),
            pltpu.VMEM((16, 2, db, late + query), bf16),
            pltpu.SemaphoreType.DMA((2,)),
        ],
        macs=rows * width * (out + 2 * query) + 2 * HEADS * R * rows * NOPE,
        after=after,
    )


def finish(
    info, tokens, grad_middle, hidden, latent, gain_latent, small, small_grads, key_parts, att_parts, sum_parts,
    parts1, cos4, sin4, after,
):
    rows, width = tokens.shape
    quarter = rows // 4
    db = width // 32
    rb = R // 32
    tile = latent.shape[1] - R
    query = HEADS * (NOPE + ROPE)

    def kernel(info, tok, gm, hid, lat, gl, table, sg, cos, sin, *refs):
        key_in, refs = refs[:4], refs[4:]
        att_in, refs = refs[:4], refs[4:]
        sum_in, refs = refs[:4], refs[4:]
        in1, refs = refs[: len(parts1)], refs[len(parts1) :]
        output, d_tokens, keep, send, own_keys, part, att, sums, w1, grads, sem = refs
        start_all(quarter_copies(key_in, info[3], own_keys), sem.at[6])
        start_all(pair_copies(in1, info[1] % 2, w1), sem.at[0])
        start_all(quarter_copies(sum_in, info[3], part, pl.ds(0, width)), sem.at[1])
        start_all(quarter_copies(att_in, info[3], att), sem.at[2])
        start_all(quarter_copies(sum_in, info[3], sums, pl.ds(width, width)), sem.at[3])
        wait_for(own_keys, sem.at[6])
        own = own_keys[...].reshape(rows, R + tile)
        plain = lat[:, :R]
        inverse = lax.rsqrt(jnp.mean(plain * plain, axis=-1, keepdims=True) + epsilon)
        unit = plain * inverse
        grad_y = own[:, :R]
        scaled = grad_y * gl[...]
        d_gain_latent = jnp.sum(grad_y * unit, axis=0, keepdims=True)
        grad_in = inverse * (scaled - unit * jnp.mean(scaled * unit, axis=-1, keepdims=True))
        grad_latent = jnp.concatenate([grad_in, turn(own[:, R:], cos[...], -sin[...])], axis=1).astype(bf16)
        d_latent = tn(hid[...], grad_latent).astype(bf16)
        grads[...] = d_latent.reshape(16, 2, db, R + tile)
        wait_for(w1, sem.at[0])
        wait_for(part, sem.at[1])
        x = tok[...].astype(f32)
        inverse = lax.rsqrt(jnp.mean(x * x, axis=-1, keepdims=True) + epsilon)
        unit = x * inverse
        grad_hidden = part[...].reshape(rows, width).astype(f32) + nt(
            grad_latent, w1[...].reshape(width, R + tile)
        )
        scaled = grad_hidden * table[0:1].astype(f32)
        d_tokens[...] = gm[...] + inverse * (scaled - unit * jnp.mean(scaled * unit, axis=-1, keepdims=True))
        d_gain = jnp.sum(grad_hidden * unit, axis=0, keepdims=True)
        row16 = lax.broadcasted_iota(jnp.int32, (16, width), 0)
        every = jnp.where(row16 == 0, d_gain, sg[...])
        lane = lanes((16, tile))
        row = lax.broadcasted_iota(jnp.int32, (16, tile), 0)
        per = tile // rb
        for j in range(32):
            t = j // 2
            values = every[:, t * tile : (t + 1) * tile]
            if j % 2 == 0:
                values = pltpu.roll(values, db, 1)
            gains = d_gain_latent[:, (j // per) * tile : (j // per + 1) * tile]
            gains = pltpu.roll(gains, (db + tile - (j % per) * rb) % tile, 1)
            values = jnp.where(row == 2, jnp.where(lane < db + rb, gains, 0.0), values)
            before = grads[j // 2, j % 2, 0:16, R:].astype(f32)
            grads[j // 2, j % 2, 0:16, R:] = jnp.where(lane < db, before, values).astype(bf16)
        core = info[1] % 2
        rows_here = pl.ds(pl.multiple_of(info[3] * (db // 4), db // 4), db // 4)
        pltpu.make_async_copy(grads.at[:, core, rows_here], keep, sem.at[4]).start()
        pltpu.make_async_copy(grads.at[:, 1 - core, rows_here], send, sem.at[5]).start()
        wait_for(att, sem.at[2])
        wait_for(sums, sem.at[3])
        middle = x + att[...].reshape(rows, width).astype(f32)
        output[...] = (middle + sums[...].reshape(rows, width).astype(f32)).astype(bf16)
        wait_for(keep, sem.at[4])
        wait_for(send, sem.at[5])

    vmem_ins = [tokens, grad_middle, hidden, latent, gain_latent, small, small_grads, cos4, sin4]
    return call(
        kernel,
        [
            ((rows, width), bf16, "v"),
            ((rows, width), f32, "v"),
            ((16, db // 4, R + tile), bf16, "a"),
            ((16, db // 4, R + tile), bf16, "a"),
        ],
        [(info, "s")]
        + [(array, "v") for array in vmem_ins]
        + [(part, "a") for part in key_parts + att_parts + sum_parts + parts1],
        [
            pltpu.VMEM((4, quarter, R + tile), f32),
            pltpu.VMEM((4, quarter, width), bf16),
            pltpu.VMEM((4, quarter, width), bf16),
            pltpu.VMEM((4, quarter, width), bf16),
            pltpu.VMEM((16, 2, db, R + tile), bf16),
            pltpu.VMEM((16, 2, db, R + tile), bf16),
            pltpu.SemaphoreType.DMA((7,)),
        ],
        macs=4 * rows * width * (R + tile),
        after=after,
    )


def unpack_experts(info, own, other, ff, sh):
    _, _, db, wide = other.shape

    def kernel(info, a0, a1, a2, a3, b, gate, up, down, sg, su, sd, slots, sem):
        for kx, a in enumerate((a0, a1, a2, a3)):
            pltpu.make_async_copy(a.at[0], slots.at[info[2] ^ (kx * 2)], sem).start()
            pltpu.make_async_copy(b.at[kx], slots.at[info[2] ^ (kx * 2 + 1)], sem).start()
        wait_for(slots, sem)
        for n, (routed, shared) in enumerate(((gate, sg), (up, su), (down, sd))):
            for e in range(8):
                routed[e] = slots[e, n, :, :ff].astype(f32)
            shared[...] = jnp.concatenate(
                [slots[e, n, :, FF_PAD : FF_PAD + sh].astype(f32) for e in range(8)], axis=1
            )

    return call(
        kernel,
        [((8, db, ff), f32, "v")] * 3 + [((db, 8 * sh), f32, "v")] * 3,
        [(info, "s")] + [(part, "a") for part in own] + [(other, "a")],
        [pltpu.VMEM((8, 3, db, wide), bf16), pltpu.SemaphoreType.DMA(())],
    )


def unpack_rest(info, parts):
    _, quarter, columns = parts[0].shape
    db = 4 * quarter
    rb = R // 32

    def kernel(info, a, b, c, d, latent, gain_attn, gain_moe, gain_latent, router_t, block):
        for k, part in enumerate((a, b, c, d)):
            block[info[3] ^ k] = part[0].astype(f32)
        whole = block[...].reshape(db, columns)
        latent[...] = whole[:, : R + ROPE]
        small = whole[0:16, R + ROPE :]
        gain_attn[...] = small[0:1]
        gain_moe[...] = small[1:2]
        gain_latent[...] = small[2:3, :rb]
        router_t[...] = small[8:16]

    return call(
        kernel,
        [
            ((db, R + ROPE), f32, "v"),
            ((1, db), f32, "v"),
            ((1, db), f32, "v"),
            ((1, rb), f32, "v"),
            ((8, db), f32, "v"),
        ],
        [(info, "s")] + [(part, "v") for part in parts],
        [pltpu.VMEM((4, quarter, columns), f32)],
    )


def unpack_attention(grads):
    db, _ = grads.shape
    rb = R // 32
    out = HEADS * VD
    late = out + NOPE + VD
    per_head, half = NOPE + ROPE, ROPE // 2

    def kernel(g, d_out, d_expand, d_query):
        d_out[...] = g[:, :out].astype(f32)
        for h in range(HEADS):
            d_expand[:, h * (NOPE + VD) : (h + 1) * (NOPE + VD)] = g[h * rb : (h + 1) * rb, out:late].astype(f32)
            plain = g[:, late + h * NOPE : late + (h + 1) * NOPE].astype(f32)
            front = late + HEADS * NOPE + h * half
            back = front + HEADS * half
            d_query[:, h * per_head : (h + 1) * per_head] = jnp.concatenate(
                [plain, g[:, front : front + half].astype(f32), g[:, back : back + half].astype(f32)], axis=1
            )

    return call(
        kernel,
        [
            ((db, out), f32, "v"),
            ((rb, HEADS * (NOPE + VD)), f32, "v"),
            ((db, HEADS * per_head), f32, "v"),
        ],
        [(grads, "v")],
        [],
    )


def shards(
    tokens,
    lengths,
    routes,
    cotangent,
    attn_gain,
    w_query,
    w_latent,
    latent_gain,
    w_expand,
    w_out,
    moe_gain,
    w_router,
    w_gate,
    w_up,
    w_down,
    shared_gate,
    shared_up,
    shared_down,
):
    me = lax.axis_index(PLANE)
    place = me % 16
    member = me % 8
    z = lax.axis_index("z")
    rows, width = tokens.shape
    quarter = rows // 4
    db = width // 32
    rb = R // 32
    ff, sh = w_gate.shape[2], shared_gate.shape[1] // 8
    tile = ROPE + db
    query = HEADS * (NOPE + ROPE)
    half = ROPE // 2
    extra = min(128, FF_PAD)
    wide = FF_PAD + SH_PAD
    info = jnp.concatenate([jnp.stack([me, place, member, z]).astype(jnp.int32), lengths[0]])

    one, two = pack_attention(
        w_query, w_latent, attn_gain, moe_gain, latent_gain, w_router.T, w_out.T, w_expand
    )
    pack = lax.all_gather(two, ("yh", "yl", "x", "c"), axis=0).reshape(2, 2, 8, db, -1)
    keep, send = pack_experts(
        info, w_gate, w_up, jnp.swapaxes(w_down, 1, 2), shared_gate, shared_up, shared_down.T, w_router
    )
    came = swap(send, kc=1)
    by_x = [jnp.stack([keep[k], came[k]]) for k in range(4)]
    latent_parts = gather(one, ("yl", "yh", "x"), ())

    position = place * rows + jnp.arange(rows, dtype=jnp.int32)
    ends = jnp.stack([lengths[0, 0], lengths[0, 0] + lengths[0, 1]])
    start = jnp.where(position >= ends[1], ends[1], jnp.where(position >= ends[0], ends[0], 0))
    frequency = rope_base ** (-jnp.arange(half, dtype=f32) / half)
    angles = (position - start).astype(f32)[:, None] * jnp.tile(frequency, 2 * HEADS * half // ROPE)[None, :]
    cos4, sin4 = jnp.cos(angles), jnp.sin(angles)
    picked = jnp.sum(
        (routes[:, :, None] == jnp.arange(16, dtype=jnp.int32)[None, None, :] - 8).astype(f32), axis=1
    )
    lane_pick = jnp.sum(
        (routes[:, :, None] == jnp.arange(extra, dtype=jnp.int32)[None, None, :] - (ff - FF_PAD + extra)), axis=1
    ).astype(bf16)

    hidden, keys, latent, small, gain_latent = project_latent(info, tokens, cos4, sin4, latent_parts)
    mine = jnp.concatenate([by_x[0]] + [swap(by_x[k], kx=k) for k in (1, 2, 3)])
    weights = [mine] + [swap(mine, ky=k) for k in (1, 3)]
    q_nope, q_rope = project_query(hidden, cos4, sin4, pack)
    keys = hold(exchange(hold(keys, mine), ("yh", "x")), q_nope)
    key_parts = [keys, swap(keys, kc=1)]
    cots = hold(jnp.concatenate([cotangent, lane_pick], axis=1), key_parts[0])
    cots = lax.all_gather(cots, ("x", "c"), axis=0).reshape(4, 2, 4, quarter, width + extra)
    probs, cat, mixture, head_out, attention = attend(info, q_nope, q_rope, key_parts, pack, ())
    attention = exchange(attention, "z")
    own_attention, normed = quarter_norm(info, attention, tokens, small, ())
    weights += pass_on(*weights[1:])
    att_parts = [own_attention] + [swap_z(own_attention, k) for k in (1, 2, 3)]
    normed_parts = gather(normed, ("x", "z"), weights[3:] + att_parts[1:])

    act, grad_both, first, keep2, send2 = expert_rows(
        info, normed_parts, cots, weights, ff
    )

    def scattered(values):
        return exchange(values.reshape(16, quarter, -1), ("x", "z"))

    def collect(values):
        return jnp.sum(values.astype(f32), axis=0, keepdims=True).astype(bf16)

    second = total([keep2, swap(send2, kc=1)])
    d_experts = expert_weights(info, normed_parts, cots, act, grad_both, (second,))
    opposite3, opposite1 = swap(d_experts[4], ky=1), swap(d_experts[5], ky=3)
    straight3, straight1 = swap(d_experts[7], ky=3), swap(d_experts[2], ky=1)
    second = collect(hold(scattered(second), d_experts[0]))
    onward3 = total([hold(d_experts[6], second), opposite3])
    onward1 = total([hold(d_experts[3], second), opposite1])
    first = lax.psum_scatter(first, ("x", "c"), scatter_dimension=0).reshape(4, quarter, width)
    first = lax.psum_scatter(first, "z", scatter_dimension=0)[None]
    onward3, onward1 = swap(onward3, ky=3), swap(onward1, ky=1)
    grad_parts = [second] + [swap_z(second, k) for k in (1, 2, 3)]

    grad_middle, small_grads, key_keep, key_send, grad_att, grad_heads, grad_abs, grad_q = attend_back(
        info, tokens, cotangent, picked, att_parts, grad_parts, small, probs, cat, key_parts, pack, cos4, sin4,
        (),
    )
    *hidden_part, most = attention_weights(
        info, grad_att, grad_heads, grad_abs, grad_q, hidden, head_out, mixture, q_nope, pack, (straight3, straight1, onward3, onward1)
    )
    grad_keys = total([key_keep, swap(hold(key_send, straight3, straight1, onward3, onward1), kc=1)]).reshape(32, quarter, R + tile)
    key_sum = grad_keys
    grad_keys = exchange(grad_keys, ("yh", "x", "z"))
    grad_hidden = total([hidden_part[0]] + [swap_z(hidden_part[k], k) for k in (1, 2, 3)])
    sums = jnp.concatenate([grad_hidden, first], axis=2)
    sum_parts = [sums] + [swap_z(sums, k) for k in (1, 2, 3)]
    grad_keys = hold(grad_keys, *sum_parts[1:])


    most = lax.psum_scatter(most, ("x", "c"), scatter_dimension=0)
    grad_keys = jnp.sum(grad_keys.astype(f32), axis=0, keepdims=True)
    grad_key_parts = [grad_keys] + [swap_z(grad_keys, k) for k in (1, 2, 3)]
    d_mine = [
        total(
            [part[k % 2] for part in (hold(d_experts[k // 2], key_sum), (onward3, straight3)[k // 2], (straight1, onward1)[k // 2])]
        )
        for k in range(4)
    ]

    d_mine = [hold(part, sums) for part in d_mine]
    d_mine[1], d_mine[3] = swap(d_mine[1], kx=1), swap(d_mine[3], kx=3)
    output, d_tokens, keep, send = finish(
        info, tokens, grad_middle, hidden, latent, gain_latent, small, small_grads, grad_key_parts, att_parts,
        sum_parts, latent_parts, cos4, sin4, (d_mine[1], d_mine[3]),
    )
    most = lax.psum_scatter(hold(most, keep), ("yh", "yl"), scatter_dimension=0)
    rest = total([keep, swap(send, kc=1)])
    d_mine[2] = swap(hold(d_mine[2], d_tokens), kx=2)
    rest = exchange(rest, ("yl", "yh", "x"))
    d_mine[2] = hold(d_mine[2], rest)
    d_other = swap(jnp.stack([part[1] for part in d_mine]), kc=1)
    d_routed = unpack_experts(info, d_mine, d_other, ff, sh)
    rest = collect(rest)
    d_out, d_expand, d_query = unpack_attention(most)
    d_latent, d_attn_gain, d_moe_gain, d_latent_gain, d_router_t = unpack_rest(
        info, [rest] + [swap_z(rest, k) for k in (1, 2, 3)]
    )
    return (
        output,
        d_tokens,
        d_attn_gain[0],
        d_query,
        d_latent,
        d_latent_gain[0],
        d_expand,
        d_out.T,
        d_moe_gain[0],
        d_router_t.T,
        d_routed[0],
        d_routed[1],
        jnp.swapaxes(d_routed[2], 1, 2),
        d_routed[3],
        d_routed[4],
        d_routed[5].T,
    )


def solution(mesh):
    rows = P(PLANE, None)
    split = P(PLANE, "z")
    vector = P(PLANE)
    turned = P("z", PLANE)
    expert_rows = P(None, PLANE, "z")
    expert_columns = P(None, "z", PLANE)
    fine = Mesh(mesh.devices.reshape(2, 2, 4, 2, 4), ("yl", "yh", "x", "c", "z"))
    return jax.shard_map(
        shards,
        mesh=fine,
        in_specs=(
            rows,
            P("yl", None),
            rows,
            rows,
            vector,
            split,
            rows,
            vector,
            split,
            turned,
            vector,
            rows,
            expert_rows,
            expert_rows,
            expert_columns,
            split,
            split,
            turned,
        ),
        out_specs=(
            rows,
            rows,
            vector,
            split,
            rows,
            vector,
            split,
            turned,
            vector,
            rows,
            expert_rows,
            expert_rows,
            expert_columns,
            split,
            split,
            turned,
        ),
        check_vma=False,
    )
```
